32 devices in a mesh: dp: 16 (over z, y, x), mp: 2 (over core).
Axes of the slice: x: 2, y: 2, z: 4, core: 2. Of those that a mesh axis runs over, the one named last changes fastest.
Arguments:
- tokens: bfloat16 [9216, 768], P('dp'), may hold values from -6 to 6
- cotangent: bfloat16 [9216, 768], P('dp'), may hold values from -8 to 8
- task_mask: int32 [32, 16], P('dp'), may hold values 0 or 1
- group_ids: int32 [32, 288], P('dp'), may hold values from 0 to 4, as said below
- matrices: float32 [768, 9216], P('dp', 'mp'), may hold values from -3 to 3
- matrix_first: float32 [768, 9216], P('dp', 'mp'), may hold values from -9216 to 9216
- matrix_second: float32 [768, 9216], P('dp', 'mp'), may hold values from 0 to 9216
- matrix_average: float32 [768, 9216], P('dp', 'mp'), may hold values from -3 to 3
- norm_bias: float32 [6, 768], replicated, may hold values from -1 to 2
- norm_first: float32 [6, 768], replicated, may hold values from -9216 to 9216
- norm_second: float32 [6, 768], replicated, may hold values from 0 to 9216
- norm_average: float32 [6, 768], replicated, may hold values from -1 to 2
- column_bias: float32 [4608], P('mp'), may hold values from -3 to 3
- column_first: float32 [4608], P('mp'), may hold values from -9216 to 9216
- column_second: float32 [4608], P('mp'), may hold values from 0 to 9216
- column_average: float32 [4608], P('mp'), may hold values from -1 to 1
Outputs:
- output: bfloat16 [9216, 768], P('dp')
- input_grad: float32 [9216, 768], P('dp')
- matrix_grad: float32 [768, 9216], P('dp', 'mp')
- matrix_updated: float32 [768, 9216], P('dp', 'mp')
- matrix_moment: float32 [768, 9216], P('dp', 'mp')
- matrix_squares: float32 [768, 9216], P('dp', 'mp')
- matrix_smoothed: float32 [768, 9216], P('dp', 'mp')
- norm_grad: float32 [6, 768], replicated
- norm_updated: float32 [6, 768], replicated
- norm_moment: float32 [6, 768], replicated
- norm_squares: float32 [6, 768], replicated
- norm_smoothed: float32 [6, 768], replicated
- column_grad: float32 [4608], P('mp')
- column_updated: float32 [4608], P('mp')
- column_moment: float32 [4608], P('mp')
- column_squares: float32 [4608], P('mp')
- column_smoothed: float32 [4608], P('mp')
The draws below stay inside these ranges and needn't reach their ends.
Inputs may be any that keep to these rules, and one draw needn't show every extreme that they name: `group_ids`: within each item the first 16 ids are 0 and the ids never fall; the rest are 2 t + 1 for the observations of timestep t followed by 2 t + 2 for its readouts, t from 0 to 1, every id present.
All inputs are finite; a program needn't handle non-finite values. No bound on the sum of `task_mask` on one device may be relied on, other than what follows from the above.
Results may differ from the reference program's by a relative error of at most 0.015.
Values may be sent and summed in bfloat16 or wider, within the bound.
A program may use at most 128 MiB of HBM per device.

```python
import jax
import jax.numpy as jnp
from jax import lax

D = 768
HEADS = 12
HD = 64
FF = 3072
LEN = 288
TASK = 16
WINDOW = 2
STEP = 10
ITEMS_DEV = 2
ITEMS = 32
TOKENS = 9216
HEAD_COLS = 384
UNIT_COLS = 1536
GROUP_COLS = 4608
MAT_COLS = 9216
BIAS_COLS = 2304
BIAS_ALL = 4608
N_DP = 16
N_MP = 2


def layout_scales(query_level, key_level, value_level, out_level, up_level, down_level):
    widths = [HEAD_COLS, HEAD_COLS, HEAD_COLS, HEAD_COLS, UNIT_COLS, UNIT_COLS]
    levels = [query_level, key_level, value_level, out_level, up_level, down_level]
    pieces = [jnp.full((block_width,), block_level, jnp.float32) for block_width, block_level in zip(widths, levels)]
    return jnp.tile(jnp.concatenate(pieces), MAT_COLS // GROUP_COLS)


def weight_levels():
    return layout_scales(1.2 * D ** (-0.5), 1.2 * D ** (-0.5), D ** (-0.5), 6.0 * D ** (-0.5), D ** (-0.5), FF ** (-0.5))


def grad_levels():
    return layout_scales(0.6, 0.6, 0.6, 0.25, 0.45, 0.8) * TOKENS ** 0.5


def draw_cotangent(key, part):
    key = jax.random.fold_in(key, 11)
    rows = jnp.arange(TOKENS, dtype=jnp.float32)[:, None] / TOKENS
    noise = jnp.clip(jax.random.normal(key, (TOKENS, D), jnp.float32), -4.0, 4.0)
    return (noise * (0.6 + 1.2 * rows)).astype(jnp.bfloat16)


def draw_group_ids(key, part):
    key = jax.random.fold_in(key, 12)
    jitter_key, readout_key = jax.random.split(key)
    free_span = LEN - TASK
    even_span = free_span // WINDOW
    jitter = jax.random.randint(jitter_key, (ITEMS, WINDOW), -(even_span // 3), even_span // 3 + 1)
    step_index = jnp.arange(WINDOW)[None, :]
    lengths_now = jnp.where(step_index < WINDOW - 1, even_span + jitter, 0)
    lengths_now = jnp.where(step_index == WINDOW - 1, free_span - jnp.sum(lengths_now, axis=1, keepdims=True), lengths_now)
    step_ends = jnp.cumsum(lengths_now, axis=1)
    readouts = jax.random.randint(readout_key, (ITEMS, WINDOW), 1, 5)
    places = jnp.arange(free_span)[None, :]
    step_of = jnp.sum(places[:, :, None] >= step_ends[:, None, :], axis=2)
    one_hot = step_of[:, :, None] == step_index[:, None, :]
    end_here = jnp.sum(jnp.where(one_hot, step_ends[:, None, :], 0), axis=2)
    read_here = jnp.sum(jnp.where(one_hot, readouts[:, None, :], 0), axis=2)
    labels = jnp.where(places < end_here - read_here, 2 * step_of + 1, 2 * step_of + 2)
    return jnp.concatenate([jnp.zeros((ITEMS, TASK), jnp.int32), labels.astype(jnp.int32)], axis=1)


def draw_matrices(key, part):
    key = jax.random.fold_in(key, 13)
    noise = jnp.clip(jax.random.normal(key, (D, MAT_COLS), jnp.float32), -4.0, 4.0)
    return noise * weight_levels()


def draw_matrix_first(key, part):
    key = jax.random.fold_in(key, 14)
    noise = jnp.clip(jax.random.normal(key, (D, MAT_COLS), jnp.float32), -4.0, 4.0)
    return noise * grad_levels() * 0.11


def draw_matrix_second(key, part):
    key = jax.random.fold_in(key, 15)
    factor = jnp.exp(jax.random.uniform(key, (D, MAT_COLS), jnp.float32, 0.0, 1.3862944))
    levels = grad_levels()
    return 0.001 * levels * levels * factor


def draw_matrix_average(key, part):
    key = jax.random.fold_in(key, 16)
    noise = jnp.clip(jax.random.normal(key, (D, MAT_COLS), jnp.float32), -4.0, 4.0)
    return noise * weight_levels()


def norm_rows(noise):
    gain_rows = jnp.array([1.0, 0.0, 1.0, 0.0, 0.0, 0.0], jnp.float32)[:, None]
    return gain_rows * (1.0 + 0.1 * noise) + (1.0 - gain_rows) * 0.2 * noise


def draw_norm_bias(key, part):
    key = jax.random.fold_in(key, 17)
    noise = jnp.clip(jax.random.normal(key, (6, D), jnp.float32), -4.0, 4.0)
    return norm_rows(noise)


def draw_norm_first(key, part):
    key = jax.random.fold_in(key, 18)
    noise = jnp.clip(jax.random.normal(key, (6, D), jnp.float32), -4.0, 4.0)
    return noise * 1.3 * 0.11 * TOKENS ** 0.5


def draw_norm_second(key, part):
    key = jax.random.fold_in(key, 19)
    factor = jnp.exp(jax.random.uniform(key, (6, D), jnp.float32, 0.0, 1.3862944))
    return 0.001 * 1.69 * TOKENS * factor


def draw_norm_average(key, part):
    key = jax.random.fold_in(key, 20)
    noise = jnp.clip(jax.random.normal(key, (6, D), jnp.float32), -4.0, 4.0)
    return norm_rows(noise)


def draw_column_first(key, part):
    key = jax.random.fold_in(key, 21)
    noise = jnp.clip(jax.random.normal(key, (BIAS_ALL,), jnp.float32), -4.0, 4.0)
    return noise * 0.6 * 0.11 * TOKENS ** 0.5


def draw_column_second(key, part):
    key = jax.random.fold_in(key, 22)
    factor = jnp.exp(jax.random.uniform(key, (BIAS_ALL,), jnp.float32, 0.0, 1.3862944))
    return 0.001 * 0.36 * TOKENS * factor


def draw_column_average(key, part):
    key = jax.random.fold_in(key, 23)
    noise = jnp.clip(jax.random.normal(key, (BIAS_ALL,), jnp.float32), -4.0, 4.0)
    return noise * 0.2


def plant(drawn, rng, smallest, top_value):
    place = [jax.random.randint(jax.random.fold_in(rng, axis), (), 0, length) for axis, length in enumerate(drawn.shape)]
    main_axis = drawn.shape.index(max(drawn.shape))
    neighbour = place[:main_axis] + [(place[main_axis] + 1) % drawn.shape[main_axis]] + place[main_axis + 1:]
    return drawn.at[tuple(place)].set(smallest).at[tuple(neighbour)].set(top_value)


def block_levels(rng, extent, cuts, low, top_value):
    level, own = 1.0, jax.random.fold_in(rng, 6)
    for position, shards_of in cuts:
        draws = jnp.exp(jax.random.uniform(jax.random.fold_in(own, position), (shards_of,), jnp.float32, low / len(cuts), top_value / len(cuts)))
        level = level * jnp.repeat(draws, extent[position] // shards_of).reshape([-1 if axis == position else 1 for axis in range(len(extent))])
    return level


def centred(rng, dims, scale, limit, shards=(), held_as=jnp.bfloat16):
    entries = jax.random.normal(rng, dims, jnp.float32) * scale
    if len(shards) > 0:
        entries = block_levels(rng, dims, shards, -0.22, 0.18) * entries
    return jnp.clip(entries, min=-limit, max=limit).astype(held_as)


def setup_inputs(seed: int = 0) -> dict:
    seeds = jax.random.split(jax.random.key(seed), 17)
    return {
        "tokens": centred(seeds[0], (TOKENS, D), 1.0, 6.0, ((0, 16),)),
        "cotangent": draw_cotangent(jax.random.fold_in(seeds[16], 71), 0),
        "task_mask": plant((jax.random.randint(seeds[2], (ITEMS, TASK), 0, 4) < 3).astype(jnp.int32), jax.random.fold_in(seeds[2], 1), 0, 1),
        "group_ids": draw_group_ids(jax.random.fold_in(seeds[16], 71), 0),
        "matrices": draw_matrices(jax.random.fold_in(seeds[16], 71), 0),
        "matrix_first": draw_matrix_first(jax.random.fold_in(seeds[16], 71), 0),
        "matrix_second": draw_matrix_second(jax.random.fold_in(seeds[16], 71), 0),
        "matrix_average": draw_matrix_average(jax.random.fold_in(seeds[16], 71), 0),
        "norm_bias": draw_norm_bias(jax.random.fold_in(seeds[16], 71), 0),
        "norm_first": draw_norm_first(jax.random.fold_in(seeds[16], 71), 0),
        "norm_second": draw_norm_second(jax.random.fold_in(seeds[16], 71), 0),
        "norm_average": draw_norm_average(jax.random.fold_in(seeds[16], 71), 0),
        "column_bias": centred(seeds[12], (BIAS_ALL,), 0.2, 3.0, ((0, 2),), jnp.float32),
        "column_first": draw_column_first(jax.random.fold_in(seeds[16], 71), 0),
        "column_second": draw_column_second(jax.random.fold_in(seeds[16], 71), 0),
        "column_average": draw_column_average(jax.random.fold_in(seeds[16], 71), 0),
    }


NORM_EPSILON = 1e-06
NEGATIVE = -1e+30
GELU_SCALE = 0.7978845608028654
GELU_CUBIC = 0.044715
BETA_FIRST = 0.9
BETA_SECOND = 0.999
EPS_ADAM = 1e-08
RATE_MATRIX = 0.1
RATE_VECTOR = 0.3
DECAY_MATRIX = 0.1
AVERAGE_KEEP = 0.7

@jax.custom_vjp
def low(v):
    return lax.optimization_barrier(v.astype(jnp.bfloat16)).astype(jnp.float32)

@jax.custom_vjp
def low_back(v):
    return v

def low_keep(v):
    return (low(v), None)

def low_pass(kept, grad):
    return (grad,)

def back_keep(v):
    return (v, None)

def back_low(kept, grad):
    return (low(grad),)
low.defvjp(low_keep, low_pass)
low_back.defvjp(back_keep, back_low)

def product(left, right):
    return jnp.dot(left, right, precision=lax.Precision.HIGHEST)

def layer_norm(values, gain_row, bias_row):
    center = values - lax.optimization_barrier(jnp.mean(values, -1, keepdims=True))
    spread = lax.optimization_barrier(jnp.mean(center * center, -1, keepdims=True))
    return center * lax.rsqrt(spread + NORM_EPSILON) * gain_row + bias_row

def gelu_tanh(values):
    inner_arg = GELU_SCALE * (values + GELU_CUBIC * values * values * values)
    return 0.5 * values * (1.0 + jnp.tanh(inner_arg))

def allowed_pairs(group_block, live_block):
    item_count = group_block.shape[0]
    seq_length = group_block.shape[1]
    task_slots = live_block.shape[1]
    key_live = jnp.concatenate([live_block == 1, jnp.ones((item_count, seq_length - task_slots), dtype=bool)], axis=1)
    query_ids = group_block[:, :, None]
    key_ids = group_block[:, None, :]
    earlier = ((key_ids == 0) | (key_ids % 2 == 1)) & (key_ids <= query_ids)
    visible = (earlier | (key_ids == query_ids)) & key_live[:, None, :]
    return visible | jnp.eye(seq_length, dtype=bool)[None]

def attention_core(queries, key_vals, value_vals, groups, lives):
    item_count = groups.shape[0]
    query_four = queries.reshape(item_count, LEN, HEADS, HD)
    key_four = key_vals.reshape(item_count, LEN, HEADS, HD)
    value_four = value_vals.reshape(item_count, LEN, HEADS, HD)
    scores = jnp.einsum('nqhe,nkhe->nhqk', query_four, key_four, precision=lax.Precision.HIGHEST) * HD ** (-0.5)
    scores = low_back(scores)
    allowed = allowed_pairs(groups, lives)[:, None]
    scores = jnp.where(allowed, scores, NEGATIVE)
    row_peak = lax.optimization_barrier(jnp.max(scores, -1, keepdims=True))
    weights = jnp.exp(scores - row_peak)
    probs_full = weights / lax.optimization_barrier(jnp.sum(weights, -1, keepdims=True))
    attended = jnp.einsum('nhqk,nkhe->nqhe', low(probs_full), value_four, precision=lax.Precision.HIGHEST)
    return attended.reshape(item_count * LEN, D)

def layer_forward(mats, norms, columns_in, values, groups, lives):
    grouped = low(mats).reshape(D, N_MP, GROUP_COLS)

    def columns(start_col, stop_col):
        return grouped[:, :, start_col:stop_col].reshape(D, -1)
    w_query = columns(0, HEAD_COLS)
    w_key = columns(HEAD_COLS, 2 * HEAD_COLS)
    w_value = columns(2 * HEAD_COLS, 3 * HEAD_COLS)
    w_out = columns(3 * HEAD_COLS, 4 * HEAD_COLS)
    w_up = columns(4 * HEAD_COLS, 4 * HEAD_COLS + UNIT_COLS)
    w_down = columns(4 * HEAD_COLS + UNIT_COLS, GROUP_COLS)
    bias_grouped = columns_in.reshape(N_MP, BIAS_COLS)
    bias_query = bias_grouped[:, :HEAD_COLS].reshape(-1)
    bias_value = bias_grouped[:, HEAD_COLS:2 * HEAD_COLS].reshape(-1)
    bias_unit = bias_grouped[:, 2 * HEAD_COLS:].reshape(-1)
    act_one = low(layer_norm(values, norms[0], norms[1]))
    query_low = low(low_back(product(act_one, w_query) + bias_query))
    key_low = low(low_back(product(act_one, w_key)))
    value_low = low(low_back(product(act_one, w_value) + bias_value))
    attended = jax.checkpoint(attention_core)(query_low, key_low, value_low, groups, lives)
    heads_out = low(low_back(attended))
    residual = values + low_back(product(heads_out, w_out.T)) + norms[4]
    act_two = low(layer_norm(residual, norms[2], norms[3]))
    pre_unit = low_back(product(act_two, w_up) + bias_unit)
    hidden = low(gelu_tanh(pre_unit))
    return residual + low_back(product(hidden, w_down.T)) + norms[5]

def adam_update(weight_now, gradient, first_now, second_now, step_rate, weight_decay):
    first_new = BETA_FIRST * first_now + (1.0 - BETA_FIRST) * gradient
    second_new = BETA_SECOND * second_now + (1.0 - BETA_SECOND) * gradient * gradient
    first_fixed = first_new / (1.0 - BETA_FIRST ** STEP)
    second_fixed = second_new / (1.0 - BETA_SECOND ** STEP)
    weight_new = weight_now - step_rate * (first_fixed / (jnp.sqrt(second_fixed) + EPS_ADAM) + weight_decay * weight_now)
    return (weight_new, first_new, second_new)

def reference(tokens, cotangent, task_mask, group_ids, matrices, matrix_first, matrix_second, matrix_average, norm_bias, norm_first, norm_second, norm_average, column_bias, column_first, column_second, column_average):
    block_rows = ITEMS_DEV * LEN
    inputs = tokens.astype(jnp.float32).reshape(N_DP, block_rows, D)
    cotangents = cotangent.astype(jnp.float32).reshape(N_DP, block_rows, D)
    groups = group_ids.reshape(N_DP, ITEMS_DEV, LEN)
    lives = task_mask.reshape(N_DP, ITEMS_DEV, TASK)

    def one_block(totals, packed):
        block_in, block_cot, block_groups, block_lives = packed

        def forward_fn(mats, norms, columns_in, values):
            return layer_forward(mats, norms, columns_in, values, block_groups, block_lives)
        result, pullback = jax.vjp(forward_fn, matrices, norm_bias, column_bias, block_in)
        grads = pullback(block_cot)
        totals = (totals[0] + grads[0], totals[1] + grads[1], totals[2] + grads[2])
        return (totals, (result.astype(jnp.bfloat16), grads[3]))
    start = (jnp.zeros_like(matrices), jnp.zeros_like(norm_bias), jnp.zeros_like(column_bias))
    totals, (blocks_out, blocks_grad) = lax.scan(one_block, start, (inputs, cotangents, groups, lives))
    output = blocks_out.reshape(TOKENS, D)
    input_grad = blocks_grad.reshape(TOKENS, D)
    matrix_grad, norm_grad, column_grad = totals
    matrix_updated, matrix_moment, matrix_squares = adam_update(matrices, matrix_grad, matrix_first, matrix_second, RATE_MATRIX, DECAY_MATRIX)
    norm_updated, norm_moment, norm_squares = adam_update(norm_bias, norm_grad, norm_first, norm_second, RATE_VECTOR, 0.0)
    column_updated, column_moment, column_squares = adam_update(column_bias, column_grad, column_first, column_second, RATE_VECTOR, 0.0)
    matrix_smoothed = AVERAGE_KEEP * matrix_average + (1.0 - AVERAGE_KEEP) * matrix_updated
    norm_smoothed = AVERAGE_KEEP * norm_average + (1.0 - AVERAGE_KEEP) * norm_updated
    column_smoothed = AVERAGE_KEEP * column_average + (1.0 - AVERAGE_KEEP) * column_updated
    return (output, input_grad, matrix_grad, matrix_updated, matrix_moment, matrix_squares, matrix_smoothed, norm_grad, norm_updated, norm_moment, norm_squares, norm_smoothed, column_grad, column_updated, column_moment, column_squares, column_smoothed)
```

```python
import functools

import jax
import jax.numpy as jnp
from jax import lax
from jax.experimental import pallas as pl
from jax.experimental.pallas import tpu as pltpu
from jax.sharding import PartitionSpec as P

MESH = pl.DeviceIdType.MESH

D = 768
HEADS = 12
HD = 64
FF = 3072
STEP = 10


NORM_EPSILON = 1e-06
NEGATIVE = -1e30
GELU_SCALE = 0.7978845608028654
GELU_CUBIC = 0.044715
BETA_FIRST = 0.9
BETA_SECOND = 0.999
EPS_ADAM = 1e-08
RATE_MATRIX = 0.1
RATE_VECTOR = 0.3
DECAY_MATRIX = 0.1
AVERAGE_KEEP = 0.7


NZ, NY, NX = 4, 2, 2
OUTER = NZ * NY * NX
UNIT = 128


class Place:
    def __init__(self, inner):
        index = lax.axis_index("dp")
        outer = index // inner
        self.inner = inner
        self.rest = index % inner
        self.core = lax.axis_index("mp")
        self.x = outer % NX
        self.y = (outer // NX) % NY
        self.z = outer // (NX * NY)

    def device(self, z, y, x):
        return (((z * NY + y) * NX + x) * self.inner + self.rest, self.core)

    def along_z(self, step):
        return self.device((self.z + step) % NZ, self.y, self.x)

    def across_y(self):
        return self.device(self.z, 1 - self.y, self.x)

    def across_x(self):
        return self.device(self.z, self.y, 1 - self.x)

    def sibling(self):
        return (self.device(self.z, self.y, self.x)[0], 1 - self.core)

    def greet(self, with_sibling):
        barrier = pltpu.get_barrier_semaphore()
        peers = [self.along_z(step) for step in range(1, NZ)] + [self.across_y(), self.across_x()]
        if with_sibling:
            peers.append(self.sibling())
        for peer in peers:
            pl.semaphore_signal(barrier, inc=1, device_id=peer, device_id_type=MESH)
        pl.semaphore_wait(barrier, len(peers))


def remote(src, dst, send_sem, recv_sem, peer):
    return pltpu.make_async_remote_copy(
        src_ref=src, dst_ref=dst, send_sem=send_sem, recv_sem=recv_sem, device_id=peer, device_id_type=MESH
    )


class Gather:
    def __init__(self, place, full, z_send, z_recv, hop_send, hop_recv):
        self.place, self.full = place, full
        self.z_send, self.z_recv, self.hop_send, self.hop_recv = z_send, z_recv, hop_send, hop_recv

    def z_copy(self, unit, step, owner_z):
        p = self.place
        block = self.full.at[owner_z, p.y, p.x, :, pl.ds(unit * UNIT, UNIT)]
        return remote(block, block, self.z_send.at[unit, step - 1], self.z_recv.at[unit, step - 1], p.along_z(step))

    def hop_copy(self, unit, hop, mine):
        p = self.place
        cols = pl.ds(unit * UNIT, UNIT)
        x_first = unit % 2 == 0
        over_x = x_first == (hop == 0)
        y = p.y if (mine or over_x) else 1 - p.y
        x = p.x if (mine or not over_x) else 1 - p.x
        if hop == 0:
            block = self.full.at[:, y, x, :, cols]
        elif x_first:
            block = self.full.at[:, y, :, :, cols]
        else:
            block = self.full.at[:, :, x, :, cols]
        peer = p.across_x() if over_x else p.across_y()
        return remote(block, block, self.hop_send.at[unit, hop], self.hop_recv.at[unit, hop], peer)

    def start_z(self, unit):
        for step in range(1, NZ):
            self.z_copy(unit, step, self.place.z).start()

    def start_hop(self, unit, hop):
        if hop == 0:
            for step in range(1, NZ):
                self.z_copy(unit, step, (self.place.z - step) % NZ).wait_recv()
        else:
            self.hop_copy(unit, 0, False).wait_recv()
        self.hop_copy(unit, hop, True).start()

    def finish(self, unit):
        self.hop_copy(unit, 1, False).wait_recv()

    def drain(self, unit):
        for step in range(1, NZ):
            self.z_copy(unit, step, self.place.z).wait_send()
        for hop in range(2):
            self.hop_copy(unit, hop, True).wait_send()


class Scatter:
    def __init__(self, place, full, got_a, got_b, got_z, result, hop_send, hop_recv, z_send, z_recv):
        self.place, self.full, self.got_a, self.got_b, self.got_z, self.result = place, full, got_a, got_b, got_z, result
        self.hop_send, self.hop_recv, self.z_send, self.z_recv = hop_send, hop_recv, z_send, z_recv

    def part(self, unit, hop, mine):
        p = self.place
        cols = pl.ds(unit * UNIT, UNIT)
        y = p.y if mine else 1 - p.y
        x = p.x if mine else 1 - p.x
        if unit % 2 == 0:
            return (slice(None), y, slice(None), slice(None), cols) if hop == 0 else (slice(None), p.y, x, slice(None), cols)
        return (slice(None), slice(None), x, slice(None), cols) if hop == 0 else (slice(None), y, p.x, slice(None), cols)

    def hop_copy(self, unit, hop):
        p = self.place
        over_y = (unit % 2 == 0) == (hop == 0)
        got = (self.got_a if hop == 0 else self.got_b).at[unit]
        return remote(
            self.full.at[self.part(unit, hop, False)],
            got,
            self.hop_send.at[unit, hop],
            self.hop_recv.at[unit, hop],
            p.across_y() if over_y else p.across_x(),
        )

    def z_copy(self, unit, step):
        p = self.place
        block = self.full.at[(p.z + step) % NZ, p.y, p.x, :, pl.ds(unit * UNIT, UNIT)]
        return remote(
            block, self.got_z.at[unit, step - 1], self.z_send.at[unit, step - 1], self.z_recv.at[unit, step - 1], p.along_z(step)
        )

    def start(self, unit):
        self.hop_copy(unit, 0).start()

    def add(self, unit, hop):
        self.hop_copy(unit, hop).wait_recv()
        part = self.part(unit, hop, True)
        got = (self.got_a if hop == 0 else self.got_b)[unit]
        self.full[part] = (self.full[part].astype(jnp.float32) + got.astype(jnp.float32)).astype(jnp.bfloat16)

    def middle(self, unit):
        self.add(unit, 0)
        self.hop_copy(unit, 1).start()

    def last(self, unit):
        self.add(unit, 1)
        for step in range(1, NZ):
            self.z_copy(unit, step).start()

    def finish(self, unit):
        p = self.place
        cols = pl.ds(unit * UNIT, UNIT)
        total = self.full[p.z, p.y, p.x, :, cols].astype(jnp.float32)
        for step in range(1, NZ):
            self.z_copy(unit, step).wait_recv()
            total = total + self.got_z[unit, step - 1].astype(jnp.float32)
        self.result[:, cols] = total

    def drain(self, unit):
        for hop in range(2):
            self.hop_copy(unit, hop).wait_send()
        for step in range(1, NZ):
            self.z_copy(unit, step).wait_send()


def gather_kernel(inner, units, mats, out, full, *sems):
    place = Place(inner)
    place.greet(False)
    gather = Gather(place, full, *sems)
    full[place.z, place.y, place.x] = mats[...].astype(jnp.bfloat16)
    pairs = units // 2
    for pair in range(min(3, pairs)):
        gather.start_z(2 * pair)
        gather.start_z(2 * pair + 1)
    for t in range(pairs + LAG):
        if t < pairs:
            gather.start_hop(2 * t, 0)
            gather.start_hop(2 * t + 1, 0)
            if t + 3 < pairs:
                gather.start_z(2 * t + 6)
                gather.start_z(2 * t + 7)
        if t >= LAG:
            gather.start_hop(2 * (t - LAG), 1)
            gather.start_hop(2 * (t - LAG) + 1, 1)
    for unit in range(units):
        gather.finish(unit)
        gather.drain(unit)
    out[...] = full[...].reshape(out.shape)


def scatter_kernel(inner, units, grads, out, full, *rest):
    place = Place(inner)
    place.greet(False)
    full[...] = grads[...].reshape(full.shape)
    got_a, got_b, got_z, hop_send, hop_recv, z_send, z_recv = rest
    scatter = Scatter(place, full, got_a, got_b, got_z, out, hop_send, hop_recv, z_send, z_recv)
    pairs = units // 2
    for t in range(pairs + 3 * LAG):
        for part in range(2):
            if t < pairs:
                scatter.start(2 * t + part)
            if 0 <= t - LAG < pairs:
                scatter.middle(2 * (t - LAG) + part)
            if 0 <= t - 2 * LAG < pairs:
                scatter.last(2 * (t - 2 * LAG) + part)
            if 0 <= t - 3 * LAG < pairs:
                scatter.finish(2 * (t - 3 * LAG) + part)
    for unit in range(units):
        scatter.drain(unit)


LAG = 2


def gather_rows(mats, inner):
    rows, cols = mats.shape
    units = cols // UNIT
    dma = pltpu.SemaphoreType.DMA
    return pl.pallas_call(
        functools.partial(gather_kernel, inner, units),
        out_shape=jax.ShapeDtypeStruct((OUTER * rows, cols), jnp.bfloat16),
        in_specs=[pl.BlockSpec(memory_space=pltpu.VMEM)],
        out_specs=pl.BlockSpec(memory_space=pltpu.VMEM),
        scratch_shapes=[
            pltpu.VMEM((NZ, NY, NX, rows, cols), jnp.bfloat16),
            dma((units, NZ - 1)),
            dma((units, NZ - 1)),
            dma((units, 2)),
            dma((units, 2)),
        ],
        compiler_params=pltpu.CompilerParams(collective_id=0, has_side_effects=True, vmem_limit_bytes=56 << 20),
    )(mats)


def scatter_rows(grads, inner):
    rows, cols = grads.shape[0] // OUTER, grads.shape[1]
    units = cols // UNIT
    dma = pltpu.SemaphoreType.DMA
    return pl.pallas_call(
        functools.partial(scatter_kernel, inner, units),
        out_shape=jax.ShapeDtypeStruct((rows, cols), jnp.float32),
        in_specs=[pl.BlockSpec(memory_space=pltpu.VMEM)],
        out_specs=pl.BlockSpec(memory_space=pltpu.VMEM),
        scratch_shapes=[
            pltpu.VMEM((NZ, NY, NX, rows, cols), jnp.bfloat16),
            pltpu.VMEM((units, NZ, 2, rows, UNIT), jnp.bfloat16),
            pltpu.VMEM((units, NZ, rows, UNIT), jnp.bfloat16),
            pltpu.VMEM((units, NZ - 1, rows, UNIT), jnp.bfloat16),
            dma((units, 2)),
            dma((units, 2)),
            dma((units, NZ - 1)),
            dma((units, NZ - 1)),
        ],
        compiler_params=pltpu.CompilerParams(collective_id=1, has_side_effects=True, vmem_limit_bytes=56 << 20),
    )(grads)


def layer_norm(values, gain_row, bias_row):
    center = values - jnp.mean(values, -1, keepdims=True)
    spread = jnp.mean(center * center, -1, keepdims=True)
    return center * lax.rsqrt(spread + NORM_EPSILON) * gain_row + bias_row


def gelu_tanh(values):
    inner_arg = GELU_SCALE * (values + GELU_CUBIC * values * values * values)
    return 0.5 * values * (1.0 + jnp.tanh(inner_arg))


def allowed_pairs(group_block, live_block):
    item_count = group_block.shape[0]
    seq_length = group_block.shape[1]
    task_slots = live_block.shape[1]
    key_live = jnp.concatenate(
        [live_block == 1, jnp.ones((item_count, seq_length - task_slots), dtype=bool)], axis=1
    )
    query_ids = group_block[:, :, None]
    key_ids = group_block[:, None, :]
    earlier = ((key_ids == 0) | (key_ids % 2 == 1)) & (key_ids <= query_ids)
    visible = (earlier | (key_ids == query_ids)) & key_live[:, None, :]
    return visible | jnp.eye(seq_length, dtype=bool)[None]


def block_scores(query_blk, key_blk, group_blk, live_blk):
    head_scale = key_blk.shape[-1] ** (-0.5)
    scores = (
        jnp.einsum("nqhe,nkhe->nhqk", query_blk, key_blk, preferred_element_type=jnp.float32)
        * head_scale
    )
    allowed = allowed_pairs(group_blk, live_blk)[:, None]
    return jnp.where(allowed, scores, NEGATIVE)


def attend_block(query_blk, key_blk, value_blk, group_blk, live_blk):
    scores = block_scores(query_blk, key_blk, group_blk, live_blk)
    row_peak = jnp.max(scores, -1, keepdims=True)
    row_total = jnp.sum(jnp.exp(scores - row_peak), -1, keepdims=True)
    log_total = row_peak + jnp.log(row_total)
    probs_low = jnp.exp(scores - log_total).astype(jnp.bfloat16)
    attended = jnp.einsum(
        "nhqk,nkhe->nqhe", probs_low, value_blk, preferred_element_type=jnp.float32
    )
    return (attended, log_total[..., 0])


def attend_back(query_blk, key_blk, value_blk, grad_blk, log_total, group_blk, live_blk):
    head_scale = key_blk.shape[-1] ** (-0.5)
    scores = block_scores(query_blk, key_blk, group_blk, live_blk)
    probs_full = jnp.exp(scores - log_total[..., None])
    probs_low = probs_full.astype(jnp.bfloat16)
    grad_value = jnp.einsum(
        "nhqk,nqhe->nkhe", probs_low, grad_blk, preferred_element_type=jnp.float32
    )
    grad_probs = jnp.einsum(
        "nqhe,nkhe->nhqk", grad_blk, value_blk, preferred_element_type=jnp.float32
    )
    grad_scores = probs_full * (grad_probs - jnp.sum(probs_full * grad_probs, -1, keepdims=True))
    scores_low = grad_scores.astype(jnp.bfloat16)
    grad_query = (
        jnp.einsum("nhqk,nkhe->nqhe", scores_low, key_blk, preferred_element_type=jnp.float32)
        * head_scale
    )
    grad_key = (
        jnp.einsum("nhqk,nqhe->nkhe", scores_low, query_blk, preferred_element_type=jnp.float32)
        * head_scale
    )
    return (
        grad_query.astype(jnp.bfloat16),
        grad_key.astype(jnp.bfloat16),
        grad_value.astype(jnp.bfloat16),
    )


def adam_update(weight_now, gradient, first_now, second_now, step_rate, weight_decay):
    first_new = BETA_FIRST * first_now + (1.0 - BETA_FIRST) * gradient
    second_new = BETA_SECOND * second_now + (1.0 - BETA_SECOND) * gradient * gradient
    first_fixed = first_new / (1.0 - BETA_FIRST**STEP)
    second_fixed = second_new / (1.0 - BETA_SECOND**STEP)
    weight_new = weight_now - step_rate * (
        first_fixed / (jnp.sqrt(second_fixed) + EPS_ADAM) + weight_decay * weight_now
    )
    return (weight_new, first_new, second_new)


def local(
    tokens,
    cotangent,
    task_mask,
    group_ids,
    matrices,
    matrix_first,
    matrix_second,
    matrix_average,
    norm_bias,
    norm_first,
    norm_second,
    norm_average,
    column_bias,
    column_first,
    column_second,
    column_average,
):
    tensor_size = lax.axis_size("mp")
    head_cols = D // tensor_size
    unit_cols = FF // tensor_size
    head_local = HEADS // tensor_size
    item_count = group_ids.shape[0]
    seq_length = group_ids.shape[1]
    block_count = item_count // 2
    dp_size = lax.axis_size("dp")
    inner = dp_size // OUTER
    if inner > 1:
        groups = [[o * inner + i for i in range(inner)] for o in range(OUTER)]
        slab = lax.all_gather(matrices.astype(jnp.bfloat16), "dp", axis=0, tiled=True, axis_index_groups=groups)
    else:
        slab = matrices
    weights = gather_rows(slab, inner)
    w_qkv = weights[:, : 3 * head_cols]
    w_out = weights[:, 3 * head_cols : 4 * head_cols]
    w_up = weights[:, 4 * head_cols : 4 * head_cols + unit_cols]
    w_down = weights[:, 4 * head_cols + unit_cols :]
    bias_query = column_bias[:head_cols]
    bias_value = column_bias[head_cols : 2 * head_cols]
    bias_unit = column_bias[2 * head_cols :]
    inputs = tokens.astype(jnp.float32)
    act_one = layer_norm(inputs, norm_bias[0], norm_bias[1]).astype(jnp.bfloat16)
    projected = jnp.dot(act_one, w_qkv, preferred_element_type=jnp.float32)
    query_low = (projected[:, :head_cols] + bias_query).astype(jnp.bfloat16)
    key_low = projected[:, head_cols : 2 * head_cols].astype(jnp.bfloat16)
    value_low = (projected[:, 2 * head_cols :] + bias_value).astype(jnp.bfloat16)

    def blocks(array):
        return array.reshape(block_count, 2, seq_length, head_local, HD)

    group_blocks = group_ids.reshape(block_count, 2, seq_length)
    live_blocks = task_mask.reshape(block_count, 2, task_mask.shape[1])
    attended, log_total = lax.map(
        lambda packed: attend_block(*packed),
        (blocks(query_low), blocks(key_low), blocks(value_low), group_blocks, live_blocks),
    )
    heads_out = attended.reshape(-1, head_cols).astype(jnp.bfloat16)
    head_part = jnp.einsum("rc,dc->rd", heads_out, w_out, preferred_element_type=jnp.float32)
    residual = (
        inputs + lax.psum(head_part.astype(jnp.bfloat16), "mp").astype(jnp.float32) + norm_bias[4]
    )
    act_two = layer_norm(residual, norm_bias[2], norm_bias[3]).astype(jnp.bfloat16)
    pre_unit = jnp.dot(act_two, w_up, preferred_element_type=jnp.float32) + bias_unit
    hidden = gelu_tanh(pre_unit).astype(jnp.bfloat16)
    unit_part = jnp.einsum("rf,df->rd", hidden, w_down, preferred_element_type=jnp.float32)
    final_sum = (
        residual + lax.psum(unit_part.astype(jnp.bfloat16), "mp").astype(jnp.float32) + norm_bias[5]
    )
    output = final_sum.astype(jnp.bfloat16)
    grad_final = cotangent.astype(jnp.float32)
    grad_down = jnp.einsum("rd,rf->df", cotangent, hidden, preferred_element_type=jnp.float32)
    grad_hidden = jnp.dot(cotangent, w_down, preferred_element_type=jnp.float32)
    unused_gelu, gelu_back = jax.vjp(gelu_tanh, pre_unit)
    grad_pre = gelu_back(grad_hidden)[0].astype(jnp.bfloat16)
    grad_up = jnp.einsum("rd,rf->df", act_two, grad_pre, preferred_element_type=jnp.float32)
    unit_input = lax.psum(
        jnp.einsum("rf,df->rd", grad_pre, w_up, preferred_element_type=jnp.float32).astype(
            jnp.bfloat16
        ),
        "mp",
    ).astype(jnp.float32)
    unused_two, norm_back_two = jax.vjp(layer_norm, residual, norm_bias[2], norm_bias[3])
    grad_res_norm, grad_gain_two, grad_shift_two = norm_back_two(unit_input)
    grad_residual = grad_final + grad_res_norm
    grad_res_low = grad_residual.astype(jnp.bfloat16)
    grad_out = jnp.einsum("rd,rc->dc", grad_res_low, heads_out, preferred_element_type=jnp.float32)
    grad_heads = jnp.dot(grad_res_low, w_out, preferred_element_type=jnp.float32).astype(
        jnp.bfloat16
    )
    grad_query, grad_key, grad_value = lax.map(
        lambda packed: attend_back(*packed),
        (
            blocks(query_low),
            blocks(key_low),
            blocks(value_low),
            blocks(grad_heads),
            log_total,
            group_blocks,
            live_blocks,
        ),
    )
    grad_query = grad_query.reshape(-1, head_cols)
    grad_key = grad_key.reshape(-1, head_cols)
    grad_value = grad_value.reshape(-1, head_cols)
    grad_proj = jnp.concatenate([grad_query, grad_key, grad_value], axis=1)
    grad_qkv = jnp.einsum("rd,rc->dc", act_one, grad_proj, preferred_element_type=jnp.float32)
    head_input = lax.psum(
        jnp.einsum("rc,dc->rd", grad_proj, w_qkv, preferred_element_type=jnp.float32).astype(
            jnp.bfloat16
        ),
        "mp",
    ).astype(jnp.float32)
    unused_one, norm_back_one = jax.vjp(layer_norm, inputs, norm_bias[0], norm_bias[1])
    grad_in_norm, grad_gain_one, grad_shift_one = norm_back_one(head_input)
    input_grad = grad_residual + grad_in_norm
    norm_local = jnp.stack(
        [
            grad_gain_one,
            grad_shift_one,
            grad_gain_two,
            grad_shift_two,
            jnp.sum(grad_residual, 0),
            jnp.sum(grad_final, 0),
        ]
    )
    column_local = jnp.concatenate(
        [
            jnp.sum(grad_query.astype(jnp.float32), 0),
            jnp.sum(grad_value.astype(jnp.float32), 0),
            jnp.sum(grad_pre.astype(jnp.float32), 0),
        ]
    )
    norm_grad, column_grad = lax.psum((norm_local, column_local), "dp")
    matrix_grad = scatter_rows(
        jnp.concatenate([grad_qkv, grad_out, grad_up, grad_down], axis=1).astype(jnp.bfloat16), inner
    )
    if inner > 1:
        matrix_grad = lax.psum_scatter(
            matrix_grad, "dp", scatter_dimension=0, tiled=True, axis_index_groups=groups
        )
    matrix_updated, matrix_moment, matrix_squares = adam_update(
        matrices, matrix_grad, matrix_first, matrix_second, RATE_MATRIX, DECAY_MATRIX
    )
    norm_updated, norm_moment, norm_squares = adam_update(
        norm_bias, norm_grad, norm_first, norm_second, RATE_VECTOR, 0.0
    )
    column_updated, column_moment, column_squares = adam_update(
        column_bias, column_grad, column_first, column_second, RATE_VECTOR, 0.0
    )
    matrix_smoothed = AVERAGE_KEEP * matrix_average + (1.0 - AVERAGE_KEEP) * matrix_updated
    norm_smoothed = AVERAGE_KEEP * norm_average + (1.0 - AVERAGE_KEEP) * norm_updated
    column_smoothed = AVERAGE_KEEP * column_average + (1.0 - AVERAGE_KEEP) * column_updated
    return (
        output,
        input_grad,
        matrix_grad,
        matrix_updated,
        matrix_moment,
        matrix_squares,
        matrix_smoothed,
        norm_grad,
        norm_updated,
        norm_moment,
        norm_squares,
        norm_smoothed,
        column_grad,
        column_updated,
        column_moment,
        column_squares,
        column_smoothed,
    )


def solution(mesh):
    placed = (
        P("dp", None),
        P("dp", None),
        P("dp", None),
        P("dp", None),
        P("dp", "mp"),
        P("dp", "mp"),
        P("dp", "mp"),
        P("dp", "mp"),
        P(),
        P(),
        P(),
        P(),
        P("mp"),
        P("mp"),
        P("mp"),
        P("mp"),
    )
    return jax.shard_map(
        local,
        mesh=mesh,
        in_specs=placed,
        out_specs=(
            P("dp", None),
            P("dp", None),
            P("dp", "mp"),
            P("dp", "mp"),
            P("dp", "mp"),
            P("dp", "mp"),
            P("dp", "mp"),
            P(),
            P(),
            P(),
            P(),
            P(),
            P("mp"),
            P("mp"),
            P("mp"),
            P("mp"),
            P("mp"),
        ),
        check_vma=False,
    )
```

```python
import functools

import jax
import jax.numpy as jnp
from jax import lax
from jax.experimental import pallas as pl
from jax.experimental.pallas import tpu as pltpu
from jax.sharding import PartitionSpec as P

MESH = pl.DeviceIdType.MESH

D = 768
HEADS = 12
HD = 64
FF = 3072
STEP = 10


NORM_EPSILON = 1e-06
NEGATIVE = -1e30
GELU_SCALE = 0.7978845608028654
GELU_CUBIC = 0.044715
BETA_FIRST = 0.9
BETA_SECOND = 0.999
EPS_ADAM = 1e-08
RATE_MATRIX = 0.1
RATE_VECTOR = 0.3
DECAY_MATRIX = 0.1
AVERAGE_KEEP = 0.7


NZ, NY, NX = 4, 2, 2
OUTER = NZ * NY * NX
ROW_TILE = 32
COL_TILE = 256
F32, BF16 = jnp.float32, jnp.bfloat16


class Place:
    def __init__(self, inner):
        index = lax.axis_index("dp")
        outer = index // inner
        self.inner = inner
        self.rest = index % inner
        self.core = lax.axis_index("mp")
        self.x = outer % NX
        self.y = (outer // NX) % NY
        self.z = outer // (NX * NY)

    def device(self, z, y, x):
        return (((z * NY + y) * NX + x) * self.inner + self.rest, self.core)

    def along_z(self, step):
        return self.device((self.z + step) % NZ, self.y, self.x)

    def across_y(self):
        return self.device(self.z, 1 - self.y, self.x)

    def across_x(self):
        return self.device(self.z, self.y, 1 - self.x)

    def sibling(self):
        return (self.device(self.z, self.y, self.x)[0], 1 - self.core)

    def greet(self):
        barrier = pltpu.get_barrier_semaphore()
        peers = [self.along_z(step) for step in range(1, NZ)]
        peers += [self.across_y(), self.across_x(), self.sibling()]
        for peer in peers:
            pl.semaphore_signal(barrier, inc=1, device_id=peer, device_id_type=MESH)
        pl.semaphore_wait(barrier, len(peers))


def remote(src, dst, send_sem, recv_sem, peer):
    return pltpu.make_async_remote_copy(
        src_ref=src,
        dst_ref=dst,
        send_sem=send_sem,
        recv_sem=recv_sem,
        device_id=peer,
        device_id_type=MESH,
    )


class Gather:
    def __init__(self, place, units, full, z_send, z_recv, hop_send, hop_recv):
        self.place, self.units, self.full = place, units, full
        self.z_send, self.z_recv, self.hop_send, self.hop_recv = z_send, z_recv, hop_send, hop_recv

    def z_copy(self, unit, step, owner_z):
        p = self.place
        block = self.full.at[owner_z, p.y, p.x, :, pl.ds(*self.units[unit])]
        return remote(
            block,
            block,
            self.z_send.at[unit, step - 1],
            self.z_recv.at[unit, step - 1],
            p.along_z(step),
        )

    def hop_copy(self, unit, hop, mine):
        p = self.place
        cols = pl.ds(*self.units[unit])
        x_first = unit % 2 == 0
        over_x = x_first == (hop == 0)
        y = p.y if (mine or over_x) else 1 - p.y
        x = p.x if (mine or not over_x) else 1 - p.x
        if hop == 0:
            block = self.full.at[:, y, x, :, cols]
        elif x_first:
            block = self.full.at[:, y, :, :, cols]
        else:
            block = self.full.at[:, :, x, :, cols]
        peer = p.across_x() if over_x else p.across_y()
        return remote(
            block, block, self.hop_send.at[unit, hop], self.hop_recv.at[unit, hop], peer
        )

    def start_z(self, unit):
        for step in range(1, NZ):
            self.z_copy(unit, step, self.place.z).start()

    def start_hop(self, unit, hop):
        if hop == 0:
            for step in range(1, NZ):
                self.z_copy(unit, step, (self.place.z - step) % NZ).wait_recv()
        else:
            self.hop_copy(unit, 0, False).wait_recv()
        self.hop_copy(unit, hop, True).start()

    def finish(self, unit):
        self.hop_copy(unit, 1, False).wait_recv()

    def drain(self, unit):
        for step in range(1, NZ):
            self.z_copy(unit, step, self.place.z).wait_send()
        for hop in range(2):
            self.hop_copy(unit, hop, True).wait_send()


class Scatter:
    def __init__(
        self, place, units, full, got_a, got_b, got_z, result, hop_send, hop_recv, z_send, z_recv
    ):
        self.place, self.units, self.full, self.result = place, units, full, result
        self.got_a, self.got_b, self.got_z = got_a, got_b, got_z
        self.hop_send, self.hop_recv, self.z_send, self.z_recv = hop_send, hop_recv, z_send, z_recv
        self.begun = 0
        self.passed = [0, 0, 0]

    def part(self, unit, hop, mine):
        p = self.place
        cols = pl.ds(*self.units[unit])
        every = slice(None)
        y = p.y if mine else 1 - p.y
        x = p.x if mine else 1 - p.x
        if unit % 2 == 0:
            return (every, y, every, every, cols) if hop == 0 else (every, p.y, x, every, cols)
        return (every, every, x, every, cols) if hop == 0 else (every, y, p.x, every, cols)

    def landing(self, unit, hop):
        cols = pl.ds(*self.units[unit])
        if hop == 0:
            return self.got_a.at[:, :, :, cols]
        return self.got_b.at[:, :, cols]

    def hop_copy(self, unit, hop):
        p = self.place
        over_y = (unit % 2 == 0) == (hop == 0)
        return remote(
            self.full.at[self.part(unit, hop, False)],
            self.landing(unit, hop),
            self.hop_send.at[unit, hop],
            self.hop_recv.at[unit, hop],
            p.across_y() if over_y else p.across_x(),
        )

    def z_copy(self, unit, step):
        p = self.place
        cols = pl.ds(*self.units[unit])
        return remote(
            self.full.at[(p.z + step) % NZ, p.y, p.x, :, cols],
            self.got_z.at[step - 1, :, cols],
            self.z_send.at[unit, step - 1],
            self.z_recv.at[unit, step - 1],
            p.along_z(step),
        )

    def add(self, unit, hop):
        self.hop_copy(unit, hop).wait_recv()
        part = self.part(unit, hop, True)
        got = self.landing(unit, hop)[...]
        self.full[part] = (self.full[part].astype(F32) + got.astype(F32)).astype(BF16)

    def start(self, unit):
        self.hop_copy(unit, 0).start()

    def middle(self, unit):
        self.add(unit, 0)
        self.hop_copy(unit, 1).start()

    def last(self, unit):
        self.add(unit, 1)
        for step in range(1, NZ):
            self.z_copy(unit, step).start()

    def finish(self, unit):
        p = self.place
        cols = pl.ds(*self.units[unit])
        total = self.full[p.z, p.y, p.x, :, cols].astype(F32)
        for step in range(1, NZ):
            self.z_copy(unit, step).wait_recv()
            total = total + self.got_z[step - 1, :, cols].astype(F32)
        self.result[:, cols] = total

    def drain(self, unit):
        for hop in range(2):
            self.hop_copy(unit, hop).wait_send()
        for step in range(1, NZ):
            self.z_copy(unit, step).wait_send()

    def begin(self, pairs):
        for pair in range(self.begun, self.begun + pairs):
            self.start(2 * pair)
            self.start(2 * pair + 1)
        self.begun += pairs

    def advance(self):
        limits = [self.begun, self.passed[0], self.passed[1]]
        for depth, stage in enumerate((self.middle, self.last, self.finish)):
            pair = self.passed[depth]
            if pair < limits[depth]:
                stage(2 * pair)
                stage(2 * pair + 1)
                self.passed[depth] += 1

    def complete(self):
        while self.passed[2] < self.begun:
            self.advance()


def rows_dot(left, right):
    return jnp.dot(left, right, preferred_element_type=F32)


def dot_rt(left, right):
    return lax.dot_general(left, right, (((1,), (1,)), ((), ())), preferred_element_type=F32)


def dot_lt(left, right):
    return lax.dot_general(left, right, (((0,), (0,)), ((), ())), preferred_element_type=F32)


def normalized(values):
    center = values - jnp.mean(values, -1, keepdims=True)
    spread = jnp.mean(center * center, -1, keepdims=True)
    scale = lax.rsqrt(spread + NORM_EPSILON)
    return center * scale, scale


def total_rows(values):
    return jnp.sum(values, 0, keepdims=True)


GATHER_UNITS = (
    [(0, 128), (128, 128), (256, 256), (512, 256), (768, 384), (1152, 384)]
    + [(1536 + 256 * i, 256) for i in range(6)]
    + [(3072 + 256 * i, 256) for i in range(6)]
)
SCATTER_UNITS = (
    [(3072 + 256 * i, 256) for i in range(6)]
    + [(1536 + 256 * i, 256) for i in range(6)]
    + [(1152, 128), (1280, 256)]
    + [(0, 256), (256, 128), (384, 256), (640, 128), (768, 128), (896, 256)]
)
HEAD_COLS, UNIT_COLS = 384, 1536
Q0, K0, V0, O0, U0, W0 = 0, 384, 768, 1152, 1536, 3072


def block_kernel(inner, items, length, tokens, cotangent, task_mask, group_ids, matrices, norm, column, *rest):
    (out, input_grad, matrix_grad, vectors) = rest[:4]
    (full, grads, got_a, got_b, got_z) = rest[4:9]
    (act_one, act_one_t, act_two, act_two_t, cot_t, proj, grad_proj, heads, grad_heads) = rest[9:18]
    (caps, probs, residual, slope, hidden, grad_pre, grad_res, grad_low, ex_send, ex_recv) = rest[18:28]
    (vec_got, vec_z) = rest[28:30]
    (gz_send, gz_recv, gh_send, gh_recv, sh_send, sh_recv, sz_send, sz_recv) = rest[30:38]
    (es, er, vs, vr) = rest[38:42]
    rows = items * length
    place = Place(inner)
    gather = Gather(place, GATHER_UNITS, full, gz_send, gz_recv, gh_send, gh_recv)
    scatter = Scatter(
        place, SCATTER_UNITS, grads, got_a, got_b, got_z, matrix_grad, sh_send, sh_recv, sz_send, sz_recv
    )
    place.greet()

    def weight(start, width):
        return full[:, :, :, :, pl.ds(start, width)].reshape(D, width)

    def put_grad(start, width, value):
        grads[:, :, :, :, pl.ds(start, width)] = value.astype(BF16).reshape(grads.shape[:4] + (width,))

    def tiles(body, carry=None):
        def step(index, value):
            return body(pl.ds(pl.multiple_of(index * ROW_TILE, ROW_TILE), ROW_TILE), value)

        return lax.fori_loop(0, rows // ROW_TILE, step, carry)

    def exchange(turn, item):
        part = pl.ds(item * length, length)
        slot = turn % 2
        return remote(
            ex_send.at[slot, part],
            ex_recv.at[slot, part],
            es.at[turn, item],
            er.at[turn, item],
            place.sibling(),
        )

    def send_part(turn, item, value):
        if turn >= 2:
            exchange(turn - 2, item).wait_send()
        ex_send[turn % 2, pl.ds(item * length, length)] = value.astype(BF16)
        exchange(turn, item).start()

    def wait_part(turn):
        for item in range(items):
            exchange(turn, item).wait_recv()

    def both(turn, tile):
        return ex_send[turn % 2, tile].astype(F32) + ex_recv[turn % 2, tile].astype(F32)

    pairs = len(GATHER_UNITS) // 2
    ahead = 2

    def cast_pair(pair):
        for unit in (2 * pair, 2 * pair + 1):
            cols = pl.ds(*GATHER_UNITS[unit])
            full[place.z, place.y, place.x, :, cols] = matrices[:, cols].astype(BF16)
            gather.start_z(unit)

    def gather_step(t):
        for unit in (2 * t, 2 * t + 1):
            if t < pairs:
                gather.start_hop(unit, 0)
        if t + ahead < pairs:
            cast_pair(t + ahead)
        if t >= 1:
            for unit in (2 * t - 2, 2 * t - 1):
                gather.start_hop(unit, 1)

    def gather_finish(first, last):
        for unit in range(2 * first, 2 * last):
            gather.finish(unit)

    for pair in range(ahead):
        cast_pair(pair)

    def norm_one(tile, carry):
        unit_x, _ = normalized(tokens[tile].astype(F32))
        act_one[tile] = (unit_x * norm[0:1] + norm[1:2]).astype(BF16)
        return carry + total_rows(cotangent[tile].astype(F32))

    r5 = tiles(norm_one, jnp.zeros((1, D), F32))
    gather_step(0)

    key_index = lax.broadcasted_iota(jnp.int32, (length, length), 0)
    query_index = lax.broadcasted_iota(jnp.int32, (length, length), 1)
    same = key_index == query_index
    slots = task_mask.shape[1]
    slot_same = lax.broadcasted_iota(jnp.int32, (slots, slots), 0) == lax.broadcasted_iota(
        jnp.int32, (slots, slots), 1
    )
    for item in range(items):
        query_ids = group_ids[item : item + 1, :]
        key_ids = jnp.sum(jnp.where(same, query_ids, 0), axis=1, keepdims=True)
        filled = jnp.sum(jnp.where(slot_same, task_mask[item : item + 1, :], 0), axis=1, keepdims=True)
        live = jnp.concatenate([filled, jnp.ones((length - slots, 1), jnp.int32)], axis=0)
        odd_key = jnp.where((key_ids == 0) | (key_ids % 2 == 1), 1, 0)
        earlier = (odd_key == 1) & (key_ids <= query_ids)
        visible = (earlier | (key_ids == query_ids)) & (live == 1)
        caps[item] = jnp.where(visible | same, 3.0e38, NEGATIVE)
    gather_step(1)
    act_one_t[...] = act_one[...].T
    cot_t[...] = cotangent[...].T
    gather_step(2)
    gather_step(3)
    gather_finish(0, 3)

    for item in range(items):
        part = pl.ds(item * length, length)
        for start, scale, bias in ((Q0, HD**-0.5, 0), (K0, 1.0, None), (V0, 1.0, HEAD_COLS)):
            value = rows_dot(act_one[part], weight(start, HEAD_COLS))
            if bias is not None:
                value = value + column[:, bias : bias + HEAD_COLS]
            value = value.astype(BF16)
            if scale != 1.0:
                value = value * jnp.asarray(scale, BF16)
            proj[part, start : start + HEAD_COLS] = value

    head_pairs = HEAD_COLS // 128
    lane = lax.broadcasted_iota(jnp.int32, (length, 128), 1)
    first_half = lane < HD

    def lanes(start, pair):
        return pl.ds(pl.multiple_of(start + pair * 128, 128), 128)

    def attend(item):
        part = pl.ds(item * length, length)

        def one_pair(pair, carry):
            query, key, value = (proj[part, lanes(start, pair)] for start in (Q0, K0, V0))
            sides = []
            for side in range(2):
                own = first_half if side == 0 else ~first_half
                scores = dot_rt(jnp.where(own, key, jnp.zeros_like(key)), query)
                scores = jnp.minimum(scores, caps[item])
                weights = jnp.exp(scores - jnp.max(scores, 0, keepdims=True))
                prob = weights * (1.0 / jnp.sum(weights, 0, keepdims=True))
                probs[item, pair * 2 + side] = prob
                sides.append(dot_lt(prob.astype(BF16), value))
            heads[part, lanes(0, pair)] = jnp.where(first_half, sides[0], sides[1]).astype(BF16)
            return carry

        lax.fori_loop(0, head_pairs, one_pair, 0)

    for item in range(items):
        part = pl.ds(item * length, length)
        attend(item)
        send_part(0, item, dot_rt(heads[part], weight(O0, HEAD_COLS)))
        gather_step(4 + item)
    wait_part(0)

    def norm_two(tile, carry):
        value = tokens[tile].astype(F32) + both(0, tile) + norm[4:5]
        residual[tile] = value
        unit_x, _ = normalized(value)
        act_two[tile] = (unit_x * norm[2:3] + norm[3:4]).astype(BF16)
        return carry

    tiles(norm_two, 0)
    gather_step(6)
    act_two_t[...] = act_two[...].T
    gather_finish(3, 6)

    def up(index, carry):
        start = pl.multiple_of(index * COL_TILE, COL_TILE)
        cols = pl.ds(start, COL_TILE)
        unit = rows_dot(act_two[...], weight(pl.multiple_of(U0 + start, COL_TILE), COL_TILE))
        unit = unit + column[:, pl.ds(pl.multiple_of(2 * HEAD_COLS + start, COL_TILE), COL_TILE)]
        square = unit * unit
        bent = jnp.tanh(unit * (GELU_SCALE + (GELU_SCALE * GELU_CUBIC) * square))
        half = 0.5 * (1.0 + bent)
        hidden[:, cols] = (unit * half).astype(BF16)
        slope[:, cols] = half + 0.5 * unit * (1.0 - bent * bent) * (
            GELU_SCALE + (3.0 * GELU_SCALE * GELU_CUBIC) * square
        )
        return carry

    lax.fori_loop(0, 3, up, 0)
    gather_step(7)
    lax.fori_loop(3, 6, up, 0)
    gather_step(8)

    def down_grad(index, carry):
        start = pl.multiple_of(index * COL_TILE, COL_TILE)
        put_grad(
            pl.multiple_of(W0 + start, COL_TILE), COL_TILE, rows_dot(cot_t[...], hidden[:, pl.ds(start, COL_TILE)])
        )
        return carry

    lax.fori_loop(0, 2, down_grad, 0)
    scatter.begin(1)
    gather_step(9)
    lax.fori_loop(2, 4, down_grad, 0)
    scatter.begin(1)
    lax.fori_loop(4, 6, down_grad, 0)
    scatter.begin(1)
    gather_finish(6, 9)

    def pre_grad(index):
        start = index * COL_TILE
        cols = pl.ds(start, COL_TILE)
        value = rows_dot(cotangent[...], weight(W0 + start, COL_TILE))
        low = (value * slope[:, cols]).astype(BF16)
        grad_pre[:, cols] = low
        row, first = divmod(2 * HEAD_COLS + start, D)
        vectors[6 + row : 7 + row, first : first + COL_TILE] = total_rows(low.astype(F32))
        put_grad(U0 + start, COL_TILE, rows_dot(act_two_t[...], low))

    for index in range(UNIT_COLS // COL_TILE):
        pre_grad(index)
        if index % 2 == 1:
            scatter.begin(1)
        if index in (1, 3, 5):
            scatter.advance()
    for item in range(items):
        part = pl.ds(item * length, length)
        send_part(1, item, dot_rt(grad_pre[part], weight(U0, UNIT_COLS)))
    scatter.advance()
    wait_part(1)

    def norm_two_back(tile, carry):
        gain_sum, shift_sum, res_sum = carry
        incoming = both(1, tile)
        unit_x, scale = normalized(residual[tile])
        pulled = incoming * norm[2:3]
        inner_mean = jnp.mean(pulled, -1, keepdims=True)
        cross_mean = jnp.mean(pulled * unit_x, -1, keepdims=True)
        value = cotangent[tile].astype(F32) + scale * (pulled - inner_mean - unit_x * cross_mean)
        grad_res[tile] = value
        grad_low[tile] = value.astype(BF16)
        return (
            gain_sum + total_rows(incoming * unit_x),
            shift_sum + total_rows(incoming),
            res_sum + total_rows(value),
        )

    zero_row = jnp.zeros((1, D), F32)
    r2g, r2b, r4 = tiles(norm_two_back, (zero_row, zero_row, zero_row))
    scatter.advance()
    put_grad(O0, HEAD_COLS, dot_lt(grad_low[...], heads[...]))
    scatter.begin(1)
    for item in range(items):
        part = pl.ds(item * length, length)
        grad_heads[part] = rows_dot(grad_low[part], weight(O0, HEAD_COLS)).astype(BF16)
    scatter.advance()

    def attend_back(item):
        part = pl.ds(item * length, length)

        def one_pair(pair, carry):
            query, key, value = (proj[part, lanes(start, pair)] for start in (Q0, K0, V0))
            grad = grad_heads[part, lanes(0, pair)]
            sides = []
            for side in range(2):
                own = first_half if side == 0 else ~first_half
                prob = probs[item, pair * 2 + side]
                grad_prob = dot_rt(jnp.where(own, value, jnp.zeros_like(value)), grad)
                inner_sum = jnp.sum(prob * grad_prob, 0, keepdims=True)
                low = (prob * (grad_prob - inner_sum)).astype(BF16)
                sides.append(
                    (dot_lt(low, key) * (HD**-0.5), rows_dot(low, query), rows_dot(prob.astype(BF16), grad))
                )
            for start, left, right in zip((Q0, K0, V0), sides[0], sides[1]):
                grad_proj[part, lanes(start, pair)] = jnp.where(first_half, left, right).astype(BF16)
            return carry

        lax.fori_loop(0, head_pairs, one_pair, 0)

    for item in range(items):
        attend_back(item)
        scatter.advance()

    for item in range(items):
        part = pl.ds(item * length, length)
        send_part(2, item, dot_rt(hidden[part], weight(W0, UNIT_COLS)))
    put_grad(Q0, HEAD_COLS, rows_dot(act_one_t[...], grad_proj[:, Q0 : Q0 + HEAD_COLS]))
    scatter.begin(1)
    put_grad(K0, HEAD_COLS, rows_dot(act_one_t[...], grad_proj[:, K0 : K0 + HEAD_COLS]))
    scatter.begin(1)
    scatter.advance()
    put_grad(V0, HEAD_COLS, rows_dot(act_one_t[...], grad_proj[:, V0 : V0 + HEAD_COLS]))
    scatter.begin(1)
    scatter.advance()
    wait_part(2)
    for item in range(items):
        part = pl.ds(item * length, length)
        send_part(3, item, dot_rt(grad_proj[part], weight(Q0, 3 * HEAD_COLS)))
    r_q = total_rows(grad_proj[:, Q0 : Q0 + HEAD_COLS].astype(F32))
    r_v = total_rows(grad_proj[:, V0 : V0 + HEAD_COLS].astype(F32))

    def finish_out(tile, carry):
        out[tile] = (residual[tile] + both(2, tile) + norm[5:6]).astype(BF16)
        return carry

    tiles(finish_out, 0)
    scatter.advance()
    wait_part(3)

    def norm_one_back(tile, carry):
        gain_sum, shift_sum = carry
        incoming = both(3, tile)
        unit_x, scale = normalized(tokens[tile].astype(F32))
        pulled = incoming * norm[0:1]
        inner_mean = jnp.mean(pulled, -1, keepdims=True)
        cross_mean = jnp.mean(pulled * unit_x, -1, keepdims=True)
        input_grad[tile] = grad_res[tile] + scale * (pulled - inner_mean - unit_x * cross_mean)
        return gain_sum + total_rows(incoming * unit_x), shift_sum + total_rows(incoming)

    r1g, r1b = tiles(norm_one_back, (zero_row, zero_row))
    scatter.advance()

    for row, value in enumerate((r1g, r1b, r2g, r2b, r4, r5)):
        vectors[row : row + 1, :] = value
    vectors[6:7, :HEAD_COLS] = r_q
    vectors[6:7, HEAD_COLS:] = r_v
    for row in range(9, vectors.shape[0]):
        vectors[row : row + 1, :] = zero_row
    for hop, peer in enumerate((place.across_x(), place.across_y())):
        move = remote(vectors, vec_got.at[hop], vs.at[hop], vr.at[hop], peer)
        move.start()
        move.wait()
        vectors[...] = vectors[...] + vec_got[hop]
        scatter.advance()
    vec_z[place.z] = vectors[...]

    def vec_copy(step, owner_z):
        block = vec_z.at[owner_z]
        return remote(block, block, vs.at[1 + step], vr.at[1 + step], place.along_z(step))

    for step in range(1, NZ):
        vec_copy(step, place.z).start()
    scatter.complete()
    for step in range(1, NZ):
        vec_copy(step, (place.z - step) % NZ).wait_recv()
        vec_copy(step, place.z).wait_send()
    vectors[...] = (vec_z[0] + vec_z[1]) + (vec_z[2] + vec_z[3])
    for unit in range(len(GATHER_UNITS)):
        gather.drain(unit)
    for unit in range(len(SCATTER_UNITS)):
        scatter.drain(unit)
    for turn in (2, 3):
        for item in range(items):
            exchange(turn, item).wait_send()


def run_block(inner, tokens, cotangent, task_mask, group_ids, slab, norm_bias, column_bias):
    rows = tokens.shape[0]
    items, length = group_ids.shape
    slab_rows, cols = slab.shape
    heads = HEAD_COLS // HD
    gather_units, scatter_units = len(GATHER_UNITS), len(SCATTER_UNITS)
    dma = pltpu.SemaphoreType.DMA
    vmem = pltpu.VMEM
    in_vmem = pl.BlockSpec(memory_space=pltpu.VMEM)
    return pl.pallas_call(
        functools.partial(block_kernel, inner, items, length),
        out_shape=(
            jax.ShapeDtypeStruct((rows, D), BF16),
            jax.ShapeDtypeStruct((rows, D), F32),
            jax.ShapeDtypeStruct((slab_rows, cols), F32),
            jax.ShapeDtypeStruct((16, D), F32),
        ),
        in_specs=[in_vmem] * 7,
        out_specs=(in_vmem,) * 4,
        scratch_shapes=[
            vmem((NZ, NY, NX, slab_rows, cols), BF16),
            vmem((NZ, NY, NX, slab_rows, cols), BF16),
            vmem((NZ, 2, slab_rows, cols), BF16),
            vmem((NZ, slab_rows, cols), BF16),
            vmem((NZ - 1, slab_rows, cols), BF16),
            vmem((rows, D), BF16),
            vmem((D, rows), BF16),
            vmem((rows, D), BF16),
            vmem((D, rows), BF16),
            vmem((D, rows), BF16),
            vmem((rows, 3 * HEAD_COLS), BF16),
            vmem((rows, 3 * HEAD_COLS), BF16),
            vmem((rows, HEAD_COLS), BF16),
            vmem((rows, HEAD_COLS), BF16),
            vmem((items, length, length), F32),
            vmem((items, heads, length, length), F32),
            vmem((rows, D), F32),
            vmem((rows, UNIT_COLS), F32),
            vmem((rows, UNIT_COLS), BF16),
            vmem((rows, UNIT_COLS), BF16),
            vmem((rows, D), F32),
            vmem((rows, D), BF16),
            vmem((2, rows, D), BF16),
            vmem((2, rows, D), BF16),
            vmem((2, 16, D), F32),
            vmem((NZ, 16, D), F32),
            dma((gather_units, NZ - 1)),
            dma((gather_units, NZ - 1)),
            dma((gather_units, 2)),
            dma((gather_units, 2)),
            dma((scatter_units, 2)),
            dma((scatter_units, 2)),
            dma((scatter_units, NZ - 1)),
            dma((scatter_units, NZ - 1)),
            dma((4, items)),
            dma((4, items)),
            dma((2 + NZ - 1,)),
            dma((2 + NZ - 1,)),
        ],
        compiler_params=pltpu.CompilerParams(
            collective_id=0, has_side_effects=True, vmem_limit_bytes=60 << 20
        ),
    )(tokens, cotangent, task_mask, group_ids, slab, norm_bias, column_bias)


def adam_update(weight_now, gradient, first_now, second_now, step_rate, weight_decay):
    first_new = BETA_FIRST * first_now + (1.0 - BETA_FIRST) * gradient
    second_new = BETA_SECOND * second_now + (1.0 - BETA_SECOND) * gradient * gradient
    first_fixed = first_new / (1.0 - BETA_FIRST**STEP)
    second_fixed = second_new / (1.0 - BETA_SECOND**STEP)
    weight_new = weight_now - step_rate * (
        first_fixed / (jnp.sqrt(second_fixed) + EPS_ADAM) + weight_decay * weight_now
    )
    return (weight_new, first_new, second_new)


def local(
    tokens,
    cotangent,
    task_mask,
    group_ids,
    matrices,
    matrix_first,
    matrix_second,
    matrix_average,
    norm_bias,
    norm_first,
    norm_second,
    norm_average,
    column_bias,
    column_first,
    column_second,
    column_average,
):
    inner = lax.axis_size("dp") // OUTER
    groups = [[outer * inner + i for i in range(inner)] for outer in range(OUTER)]
    slab = matrices
    if inner > 1:
        slab = lax.all_gather(
            matrices.astype(BF16), "dp", axis=0, tiled=True, axis_index_groups=groups
        ).astype(F32)
    output, input_grad, matrix_grad, vectors = run_block(
        inner, tokens, cotangent, task_mask, group_ids, slab, norm_bias, column_bias.reshape(1, -1)
    )
    if inner > 1:
        matrix_grad = lax.psum_scatter(
            matrix_grad, "dp", scatter_dimension=0, tiled=True, axis_index_groups=groups
        )
        vectors = jnp.sum(lax.all_gather(vectors, "dp", axis=0, axis_index_groups=groups), 0)
    norm_grad = vectors[:6]
    column_grad = vectors[6:9].reshape(-1)
    matrix_updated, matrix_moment, matrix_squares = adam_update(
        matrices, matrix_grad, matrix_first, matrix_second, RATE_MATRIX, DECAY_MATRIX
    )
    norm_updated, norm_moment, norm_squares = adam_update(
        norm_bias, norm_grad, norm_first, norm_second, RATE_VECTOR, 0.0
    )
    column_updated, column_moment, column_squares = adam_update(
        column_bias, column_grad, column_first, column_second, RATE_VECTOR, 0.0
    )
    matrix_smoothed = AVERAGE_KEEP * matrix_average + (1.0 - AVERAGE_KEEP) * matrix_updated
    norm_smoothed = AVERAGE_KEEP * norm_average + (1.0 - AVERAGE_KEEP) * norm_updated
    column_smoothed = AVERAGE_KEEP * column_average + (1.0 - AVERAGE_KEEP) * column_updated
    return (
        output,
        input_grad,
        matrix_grad,
        matrix_updated,
        matrix_moment,
        matrix_squares,
        matrix_smoothed,
        norm_grad,
        norm_updated,
        norm_moment,
        norm_squares,
        norm_smoothed,
        column_grad,
        column_updated,
        column_moment,
        column_squares,
        column_smoothed,
    )


def solution(mesh):
    placed = (
        P("dp", None),
        P("dp", None),
        P("dp", None),
        P("dp", None),
        P("dp", "mp"),
        P("dp", "mp"),
        P("dp", "mp"),
        P("dp", "mp"),
        P(),
        P(),
        P(),
        P(),
        P("mp"),
        P("mp"),
        P("mp"),
        P("mp"),
    )
    return jax.shard_map(
        local,
        mesh=mesh,
        in_specs=placed,
        out_specs=(
            P("dp", None),
            P("dp", None),
            P("dp", "mp"),
            P("dp", "mp"),
            P("dp", "mp"),
            P("dp", "mp"),
            P("dp", "mp"),
            P(),
            P(),
            P(),
            P(),
            P(),
            P("mp"),
            P("mp"),
            P("mp"),
            P("mp"),
            P("mp"),
        ),
        check_vma=False,
    )
```

```python
import functools

import jax
import jax.numpy as jnp
from jax import lax
from jax.experimental import pallas as pl
from jax.experimental.pallas import tpu as pltpu
from jax.sharding import PartitionSpec as P

MESH = pl.DeviceIdType.MESH

D = 768
HEADS = 12
HD = 64
FF = 3072
STEP = 10


NORM_EPSILON = 1e-06
NEGATIVE = -1e30
GELU_SCALE = 0.7978845608028654
GELU_CUBIC = 0.044715
BETA_FIRST = 0.9
BETA_SECOND = 0.999
EPS_ADAM = 1e-08
RATE_MATRIX = 0.1
RATE_VECTOR = 0.3
DECAY_MATRIX = 0.1
AVERAGE_KEEP = 0.7


NZ, NY, NX = 4, 2, 2
OUTER = NZ * NY * NX
COL_TILE = 256
F32, BF16 = jnp.float32, jnp.bfloat16


class Place:
    def __init__(self, inner):
        index = lax.axis_index("dp")
        outer = index // inner
        self.inner = inner
        self.rest = index % inner
        self.core = lax.axis_index("mp")
        self.x = outer % NX
        self.y = (outer // NX) % NY
        self.z = outer // (NX * NY)

    def device(self, z, y, x):
        return (((z * NY + y) * NX + x) * self.inner + self.rest, self.core)

    def along_z(self, step):
        return self.device((self.z + step) % NZ, self.y, self.x)

    def across_y(self):
        return self.device(self.z, 1 - self.y, self.x)

    def across_x(self):
        return self.device(self.z, self.y, 1 - self.x)

    def sibling(self):
        return (self.device(self.z, self.y, self.x)[0], 1 - self.core)

    def greet(self):
        barrier = pltpu.get_barrier_semaphore()
        peers = [self.along_z(step) for step in range(1, NZ)]
        peers += [self.across_y(), self.across_x(), self.sibling()]
        for peer in peers:
            pl.semaphore_signal(barrier, inc=1, device_id=peer, device_id_type=MESH)
        pl.semaphore_wait(barrier, len(peers))


def remote(src, dst, send_sem, recv_sem, peer):
    return pltpu.make_async_remote_copy(
        src_ref=src,
        dst_ref=dst,
        send_sem=send_sem,
        recv_sem=recv_sem,
        device_id=peer,
        device_id_type=MESH,
    )


AXIS = {"z": 0, "y": 1, "x": 2}


class Mover:
    def __init__(self, place, units, full, send_sem, recv_sem):
        self.place, self.units, self.full = place, units, full
        self.send_sem, self.recv_sem = send_sem, recv_sem

    def peers(self, axis):
        p = self.place
        if axis == "z":
            return [p.along_z(step) for step in range(1, NZ)]
        return [p.across_y() if axis == "y" else p.across_x()]

    def block(self, unit, whole, axis=None, step=None):
        p = self.place
        start, width, _ = self.units[unit]
        index = []
        for name, here in (("z", p.z), ("y", p.y), ("x", p.x)):
            if name in whole:
                index.append(slice(None))
            elif name == axis:
                index.append((p.z + step) % NZ if name == "z" else 1 - here)
            else:
                index.append(here)
        return tuple(index) + (slice(None), pl.ds(start, width))

    def copy(self, unit, stage, step, src, dst, peer):
        return remote(
            src,
            dst,
            self.send_sem.at[unit, stage, step - 1],
            self.recv_sem.at[unit, stage, step - 1],
            peer,
        )

    def sends(self, unit, stage):
        raise NotImplementedError

    def arrivals(self, unit, stage):
        raise NotImplementedError

    def begin(self, unit, stage):
        for move in self.sends(unit, stage):
            move.start()

    def settle(self, unit, stage):
        for move in self.arrivals(unit, stage):
            move.wait_recv()

    def drain(self):
        for unit in range(len(self.units)):
            for stage in range(3):
                for move in self.sends(unit, stage):
                    move.wait_send()


class Gather(Mover):
    def sends(self, unit, stage):
        route = self.units[unit][2]
        mine = self.full.at[self.block(unit, route[:stage])]
        return [
            self.copy(unit, stage, step, mine, mine, peer)
            for step, peer in enumerate(self.peers(route[stage]), 1)
        ]

    def arrivals(self, unit, stage):
        route = self.units[unit][2]
        moves = []
        for step, peer in enumerate(self.peers(route[stage]), 1):
            theirs = self.full.at[self.block(unit, route[:stage], route[stage], -step)]
            moves.append(self.copy(unit, stage, step, theirs, theirs, peer))
        return moves


class Scatter(Mover):
    def __init__(self, place, units, full, landings, result, send_sem, recv_sem):
        super().__init__(place, units, full, send_sem, recv_sem)
        self.landings, self.result = landings, result

    def landing(self, unit, stage, step):
        start, width, route = self.units[unit]
        late = route[0] != "z"
        cols = pl.ds(start, width) if late else pl.ds(Z_FIRST[unit], width)
        got = self.landings[0 if late else 1][stage]
        if route[stage] == "z":
            got = got.at[step - 1]
        lead = (slice(None),) * (3 - stage - 1)
        return got.at[lead + (slice(None), cols)]

    def sends(self, unit, stage):
        route = self.units[unit][2]
        return [
            self.copy(
                unit,
                stage,
                step,
                self.full.at[self.block(unit, route[stage + 1 :], route[stage], step)],
                self.landing(unit, stage, step),
                peer,
            )
            for step, peer in enumerate(self.peers(route[stage]), 1)
        ]

    def arrivals(self, unit, stage):
        return self.sends(unit, stage)

    def add(self, unit, stage):
        route = self.units[unit][2]
        self.settle(unit, stage)
        part = self.block(unit, route[stage + 1 :])
        total = self.full[part].astype(F32)
        for step in range(1, len(self.peers(route[stage])) + 1):
            total = total + self.landing(unit, stage, step)[...].astype(F32)
        if stage == 2:
            start, width, _ = self.units[unit]
            self.result[:, pl.ds(start, width)] = total
        else:
            self.full[part] = total.astype(BF16)


def rows_dot(left, right):
    return jnp.dot(left, right, preferred_element_type=F32)


def dot_rt(left, right):
    return lax.dot_general(left, right, (((1,), (1,)), ((), ())), preferred_element_type=F32)


def dot_lt(left, right):
    return lax.dot_general(left, right, (((0,), (0,)), ((), ())), preferred_element_type=F32)


def normalized(values):
    center = values - jnp.mean(values, -1, keepdims=True)
    spread = jnp.mean(center * center, -1, keepdims=True)
    scale = lax.rsqrt(spread + NORM_EPSILON)
    return center * scale, scale


def total_rows(values):
    return jnp.sum(values, 0, keepdims=True)


GATHER_UNITS = (
    (0, 128, "zxy"),
    (128, 128, "zyx"),
    (256, 128, "zxy"),
    (384, 128, "zyx"),
    (512, 128, "zxy"),
    (640, 128, "zyx"),
    (768, 128, "zxy"),
    (896, 128, "zyx"),
    (1024, 128, "zxy"),
    (1152, 128, "zyx"),
    (1280, 128, "zxy"),
    (1408, 128, "zyx"),
    (1536, 256, "zxy"),
    (1792, 256, "zyx"),
    (2048, 256, "zxy"),
    (2304, 256, "zyx"),
    (2560, 256, "zxy"),
    (2816, 256, "zyx"),
    (3072, 256, "zxy"),
    (3328, 256, "zyx"),
    (3584, 256, "zxy"),
    (3840, 256, "zyx"),
    (4096, 256, "zxy"),
    (4352, 256, "zyx"),
)
SCATTER_UNITS = (
    (3072, 128, "zxy"),
    (3200, 128, "zyx"),
    (3328, 256, "yxz"),
    (3584, 256, "xyz"),
    (3840, 256, "yxz"),
    (4096, 256, "xyz"),
    (4352, 256, "yxz"),
    (1536, 256, "xyz"),
    (1792, 256, "yxz"),
    (2048, 256, "xyz"),
    (2304, 256, "yxz"),
    (2560, 256, "xyz"),
    (2816, 128, "zxy"),
    (2944, 128, "zyx"),
    (1152, 128, "yxz"),
    (1280, 256, "xyz"),
    (0, 256, "yxz"),
    (256, 128, "xyz"),
    (384, 256, "xyz"),
    (640, 128, "yxz"),
    (768, 256, "yxz"),
    (1024, 128, "xyz"),
)
Z_FIRST = {0: 0, 1: 128, 12: 256, 13: 384}
Z_FIRST_COLS = 512
PLAN = (
    ("g", 0, 0), ("g", 1, 0), ("g", 2, 0), ("g", 3, 0), ("g", 4, 0), ("ln1", 0), ("ln1", 1), ("caps", 0),
    ("tr", 0), ("g", 5, 0), ("tr", 1), ("g", 0, 1), ("g", 6, 0), ("g", 1, 1), ("g", 7, 0), ("g", 2, 1),
    ("g", 0, 2), ("g", 8, 0), ("g", 1, 2), ("g", 3, 1), ("g", 9, 0), ("g", 2, 2), ("g", 4, 1), ("g", 10, 0),
    ("g", 5, 1), ("g", 11, 0), ("g", 6, 1), ("g", 3, 2), ("g", 12, 0), ("g", 4, 2), ("g", 7, 1), ("g", 6, 2),
    ("g", 8, 1), ("g", 13, 0), ("g", 9, 1), ("g", 5, 2), ("g", 10, 1), ("g", 14, 0), ("g", 8, 2), ("g", 11, 1),
    ("g", 7, 2), ("g", 15, 0), ("g", 12, 1), ("g", 10, 2), ("g", 16, 0), ("g", 13, 1), ("g", 9, 2),
    ("g", 17, 0), ("g", 14, 1), ("gf", 0), ("gf", 1), ("gf", 2), ("gf", 3), ("gf", 4), ("gf", 5), ("gf", 6),
    ("gf", 7), ("gf", 8), ("qkv", 0), ("qkv", 1), ("g", 12, 2), ("att", 0, 0), ("g", 11, 2), ("g", 15, 1),
    ("g", 18, 0), ("att", 0, 1), ("att", 0, 2), ("g", 16, 1), ("g", 19, 0), ("g", 14, 2), ("g", 13, 2),
    ("g", 20, 0), ("g", 17, 1), ("gf", 9), ("gf", 10), ("gf", 11), ("op0", 0), ("g", 21, 0), ("att", 1, 0),
    ("g", 18, 1), ("att", 1, 1), ("g", 16, 2), ("g", 22, 0), ("att", 1, 2), ("g", 19, 1), ("ln2", 0),
    ("g", 15, 2), ("op0", 1), ("g", 23, 0), ("g", 20, 1), ("ln2", 1), ("g", 21, 1), ("tr", 2), ("gf", 12),
    ("up", 0), ("g", 18, 2), ("gf", 13), ("up", 1), ("gf", 14), ("up", 2), ("g", 22, 1), ("g", 17, 2),
    ("g", 23, 1), ("gf", 15), ("up", 3), ("g", 20, 2), ("gf", 16), ("up", 4), ("g", 22, 2), ("g", 19, 2),
    ("g", 21, 2), ("gf", 17), ("up", 5), ("gd", 0), ("gd", 1), ("gd", 2), ("gd", 3), ("gd", 4), ("gd", 5),
    ("gf", 18), ("pre", 0), ("g", 23, 2), ("s", 0, 0), ("gf", 19), ("pre", 1), ("s", 1, 0), ("gf", 20),
    ("pre", 2), ("gf", 21), ("pre", 3), ("s", 0, 1), ("s", 2, 0), ("s", 3, 0), ("gf", 22), ("pre", 4),
    ("s", 0, 2), ("gf", 23), ("pre", 5), ("s", 1, 1), ("s", 12, 0), ("s", 5, 0), ("da2", 0), ("s", 4, 0),
    ("da2", 1), ("s", 13, 0), ("s", 2, 1), ("s", 0, 3), ("s", 3, 1), ("ln2b", 0), ("s", 1, 2), ("ln2b", 1),
    ("s", 12, 1), ("gout", 0), ("do", 0), ("s", 6, 0), ("do", 1), ("s", 5, 1), ("s", 7, 0), ("attb", 0, 0),
    ("s", 4, 1), ("attb", 0, 1), ("s", 1, 3), ("s", 2, 2), ("s", 3, 2), ("s", 12, 2), ("s", 13, 1),
    ("attb", 0, 2), ("attb", 1, 0), ("attb", 1, 1), ("s", 2, 3), ("s", 6, 1), ("s", 7, 1), ("attb", 1, 2),
    ("s", 3, 3), ("s", 12, 3), ("s", 4, 2), ("s", 5, 2), ("s", 13, 2), ("s", 8, 0), ("s", 9, 0), ("gp", 0),
    ("gp", 1), ("s", 6, 2), ("s", 13, 3), ("s", 7, 2), ("gp", 2), ("s", 4, 3), ("s", 11, 0), ("da1", 0),
    ("s", 10, 0), ("da1", 1), ("op2", 0), ("op2", 1), ("s", 5, 3), ("ln1b", 0), ("s", 6, 3), ("s", 8, 1),
    ("s", 9, 1), ("ln1b", 1), ("op2s", 0), ("vec", 0), ("s", 7, 3), ("s", 14, 0), ("s", 15, 0), ("s", 11, 1),
    ("s", 10, 1), ("vec", 1), ("s", 8, 2), ("s", 9, 2), ("s", 16, 0), ("s", 14, 1), ("vec", 2), ("s", 8, 3),
    ("s", 15, 1), ("s", 11, 2), ("s", 17, 0), ("s", 9, 3), ("vec", 3), ("fout", 0), ("s", 10, 2), ("s", 18, 0),
    ("fout", 1), ("s", 14, 2), ("s", 19, 0), ("s", 11, 3), ("s", 16, 1), ("s", 17, 1), ("s", 10, 3),
    ("s", 15, 2), ("s", 20, 0), ("s", 14, 3), ("s", 19, 1), ("s", 18, 1), ("s", 15, 3), ("s", 17, 2),
    ("s", 21, 0), ("s", 16, 2), ("s", 17, 3), ("s", 19, 2), ("s", 20, 1), ("s", 21, 1), ("s", 16, 3),
    ("s", 18, 2), ("s", 19, 3), ("s", 21, 2), ("s", 20, 2), ("s", 18, 3), ("s", 21, 3), ("s", 20, 3),
)

HEAD_COLS, UNIT_COLS = 384, 1536
Q0, K0, V0, O0, U0, W0 = 0, 384, 768, 1152, 1536, 3072


def block_kernel(inner, items, length, tokens, cotangent, task_mask, group_ids, matrices, norm, column, *rest):
    (out, input_grad, matrix_grad, vectors) = rest[:4]
    (full, grads) = rest[4:6]
    landings = (rest[6:9], rest[9:12])
    (act_one, act_one_t, act_two, act_two_t, cot_t, proj, grad_proj, heads, grad_heads) = rest[12:21]
    (caps, probs, residual, slope, hidden, grad_pre, grad_res, grad_low, ex_send, ex_recv) = rest[21:31]
    (vec_got, vec_z, g_send, g_recv, s_send, s_recv, es, er, vs, vr) = rest[31:]
    place = Place(inner)
    gather = Gather(place, GATHER_UNITS, full, g_send, g_recv)
    scatter = Scatter(place, SCATTER_UNITS, grads, landings, matrix_grad, s_send, s_recv)

    def weight(start, width):
        return full[:, :, :, :, pl.ds(start, width)].reshape(D, width)

    def put_grad(start, width, value):
        grads[:, :, :, :, pl.ds(start, width)] = value.astype(BF16).reshape(grads.shape[:4] + (width,))

    def rows_of(item):
        return pl.ds(item * length, length)

    def add_vector(row, first, value):
        cols = pl.ds(first, value.shape[1])
        vectors[row : row + 1, cols] = vectors[row : row + 1, cols] + value

    def exchange(turn, item):
        part = rows_of(item)
        return remote(
            ex_send.at[turn % 2, part],
            ex_recv.at[turn % 2, part],
            es.at[turn, item],
            er.at[turn, item],
            place.sibling(),
        )

    def fill_part(turn, item, value):
        if turn >= 2:
            exchange(turn - 2, item).wait_send()
        ex_send[turn % 2, rows_of(item)] = value.astype(BF16)

    def both(turn, item):
        exchange(turn, item).wait_recv()
        part = rows_of(item)
        return ex_send[turn % 2, part].astype(F32) + ex_recv[turn % 2, part].astype(F32)

    def norm_one(item):
        part = rows_of(item)
        unit_x, _ = normalized(tokens[part].astype(F32))
        act_one[part] = (unit_x * norm[0:1] + norm[1:2]).astype(BF16)
        add_vector(5, 0, total_rows(cotangent[part].astype(F32)))

    def masks(_):
        key_index = lax.broadcasted_iota(jnp.int32, (length, length), 0)
        query_index = lax.broadcasted_iota(jnp.int32, (length, length), 1)
        same = key_index == query_index
        slots = task_mask.shape[1]
        slot_same = lax.broadcasted_iota(jnp.int32, (slots, slots), 0) == lax.broadcasted_iota(
            jnp.int32, (slots, slots), 1
        )
        for item in range(items):
            query_ids = group_ids[item : item + 1, :]
            key_ids = jnp.sum(jnp.where(same, query_ids, 0), axis=1, keepdims=True)
            filled = jnp.sum(jnp.where(slot_same, task_mask[item : item + 1, :], 0), axis=1, keepdims=True)
            live = jnp.concatenate([filled, jnp.ones((length - slots, 1), jnp.int32)], axis=0)
            odd_key = jnp.where((key_ids == 0) | (key_ids % 2 == 1), 1, 0)
            earlier = (odd_key == 1) & (key_ids <= query_ids)
            visible = (earlier | (key_ids == query_ids)) & (live == 1)
            caps[item] = jnp.where(visible | same, 3.0e38, NEGATIVE)

    def turned(which):
        source, target = ((act_one, act_one_t), (cotangent, cot_t), (act_two, act_two_t))[which]
        target[...] = source[...].T

    def project(item):
        part = rows_of(item)
        for start, scale, bias in ((Q0, HD**-0.5, 0), (K0, 1.0, None), (V0, 1.0, HEAD_COLS)):
            value = rows_dot(act_one[part], weight(start, HEAD_COLS))
            if bias is not None:
                value = value + column[:, bias : bias + HEAD_COLS]
            value = value.astype(BF16)
            if scale != 1.0:
                value = value * jnp.asarray(scale, BF16)
            proj[part, start : start + HEAD_COLS] = value

    lane = lax.broadcasted_iota(jnp.int32, (length, 128), 1)
    first_half = lane < HD

    def lanes(start, pair):
        return pl.ds(start + pair * 128, 128)

    def attend(item, pair):
        part = rows_of(item)
        query, key, value = (proj[part, lanes(start, pair)] for start in (Q0, K0, V0))
        sides = []
        for side in range(2):
            own = first_half if side == 0 else ~first_half
            scores = dot_rt(jnp.where(own, key, jnp.zeros_like(key)), query)
            scores = jnp.minimum(scores, caps[item])
            weights = jnp.exp(scores - jnp.max(scores, 0, keepdims=True))
            prob = weights * (1.0 / jnp.sum(weights, 0, keepdims=True))
            probs[item, pair * 2 + side] = prob
            sides.append(dot_lt(prob.astype(BF16), value))
        heads[part, lanes(0, pair)] = jnp.where(first_half, sides[0], sides[1]).astype(BF16)

    def heads_out(item):
        fill_part(0, item, dot_rt(heads[rows_of(item)], weight(O0, HEAD_COLS)))
        exchange(0, item).start()

    def norm_two(item):
        part = rows_of(item)
        value = tokens[part].astype(F32) + both(0, item) + norm[4:5]
        residual[part] = value
        unit_x, _ = normalized(value)
        act_two[part] = (unit_x * norm[2:3] + norm[3:4]).astype(BF16)

    def up(index):
        start = index * COL_TILE
        cols = pl.ds(start, COL_TILE)
        unit = rows_dot(act_two[...], weight(U0 + start, COL_TILE))
        unit = unit + column[:, pl.ds(2 * HEAD_COLS + start, COL_TILE)]
        square = unit * unit
        bent = jnp.tanh(unit * (GELU_SCALE + (GELU_SCALE * GELU_CUBIC) * square))
        half = 0.5 * (1.0 + bent)
        hidden[:, cols] = (unit * half).astype(BF16)
        slope[:, cols] = half + 0.5 * unit * (1.0 - bent * bent) * (
            GELU_SCALE + (3.0 * GELU_SCALE * GELU_CUBIC) * square
        )

    def down_grad(index):
        start = index * COL_TILE
        put_grad(W0 + start, COL_TILE, rows_dot(cot_t[...], hidden[:, pl.ds(start, COL_TILE)]))

    def pre_grad(index):
        start = index * COL_TILE
        cols = pl.ds(start, COL_TILE)
        value = rows_dot(cotangent[...], weight(W0 + start, COL_TILE))
        low = (value * slope[:, cols]).astype(BF16)
        grad_pre[:, cols] = low
        row, first = divmod(2 * HEAD_COLS + start, D)
        add_vector(6 + row, first, total_rows(low.astype(F32)))
        put_grad(U0 + start, COL_TILE, rows_dot(act_two_t[...], low))

    def units_back(item):
        fill_part(1, item, dot_rt(grad_pre[rows_of(item)], weight(U0, UNIT_COLS)))
        exchange(1, item).start()

    def norm_back(incoming, values, gain):
        unit_x, scale = normalized(values)
        pulled = incoming * gain
        inner_mean = jnp.mean(pulled, -1, keepdims=True)
        cross_mean = jnp.mean(pulled * unit_x, -1, keepdims=True)
        return scale * (pulled - inner_mean - unit_x * cross_mean), total_rows(incoming * unit_x), total_rows(incoming)

    def norm_two_back(item):
        part = rows_of(item)
        value, gain_sum, shift_sum = norm_back(both(1, item), residual[part], norm[2:3])
        value = cotangent[part].astype(F32) + value
        grad_res[part] = value
        grad_low[part] = value.astype(BF16)
        add_vector(2, 0, gain_sum)
        add_vector(3, 0, shift_sum)
        add_vector(4, 0, total_rows(value))

    def out_grad(_):
        put_grad(O0, HEAD_COLS, dot_lt(grad_low[...], heads[...]))

    def heads_back(item):
        part = rows_of(item)
        grad_heads[part] = rows_dot(grad_low[part], weight(O0, HEAD_COLS)).astype(BF16)

    def attend_back(item, pair):
        part = rows_of(item)
        query, key, value = (proj[part, lanes(start, pair)] for start in (Q0, K0, V0))
        grad = grad_heads[part, lanes(0, pair)]
        sides = []
        for side in range(2):
            own = first_half if side == 0 else ~first_half
            prob = probs[item, pair * 2 + side]
            grad_prob = dot_rt(jnp.where(own, value, jnp.zeros_like(value)), grad)
            inner_sum = jnp.sum(prob * grad_prob, 0, keepdims=True)
            low = (prob * (grad_prob - inner_sum)).astype(BF16)
            sides.append(
                (dot_lt(low, key) * (HD**-0.5), rows_dot(low, query), rows_dot(prob.astype(BF16), grad))
            )
        for start, left, right in zip((Q0, K0, V0), sides[0], sides[1]):
            low = jnp.where(first_half, left, right).astype(BF16)
            grad_proj[part, lanes(start, pair)] = low
            if start != K0:
                add_vector(6, (0 if start == Q0 else HEAD_COLS) + pair * 128, total_rows(low.astype(F32)))

    def proj_grad(index):
        cols = pl.ds(index * HEAD_COLS, HEAD_COLS)
        put_grad(index * HEAD_COLS, HEAD_COLS, rows_dot(act_one_t[...], grad_proj[:, cols]))

    def heads_in(item):
        fill_part(2, item, dot_rt(grad_proj[rows_of(item)], weight(Q0, 3 * HEAD_COLS)))
        exchange(2, item).start()

    def units_out(item):
        fill_part(3, item, dot_rt(hidden[rows_of(item)], weight(W0, UNIT_COLS)))

    def send_units(_):
        for item in range(items):
            exchange(3, item).start()

    def norm_one_back(item):
        part = rows_of(item)
        value, gain_sum, shift_sum = norm_back(both(2, item), tokens[part].astype(F32), norm[0:1])
        input_grad[part] = grad_res[part] + value
        add_vector(0, 0, gain_sum)
        add_vector(1, 0, shift_sum)

    def finish_out(item):
        part = rows_of(item)
        out[part] = (residual[part] + both(3, item) + norm[5:6]).astype(BF16)

    def vec_copy(stage, owner_z=None, step=0):
        if stage < 2:
            peer = (place.across_x(), place.across_y())[stage]
            return remote(vectors, vec_got.at[stage], vs.at[stage], vr.at[stage], peer)
        block = vec_z.at[owner_z]
        return remote(block, block, vs.at[1 + step], vr.at[1 + step], place.along_z(step))

    def small_sums(stage):
        if stage in (1, 2):
            vec_copy(stage - 1).wait()
            vectors[...] = vectors[...] + vec_got[stage - 1]
        if stage < 2:
            vec_copy(stage).start()
        elif stage == 2:
            vec_z[place.z] = vectors[...]
            for step in range(1, NZ):
                vec_copy(2, place.z, step).start()
        else:
            for step in range(1, NZ):
                vec_copy(2, (place.z - step) % NZ, step).wait_recv()
                vec_copy(2, place.z, step).wait_send()
            vectors[...] = (vec_z[0] + vec_z[1]) + (vec_z[2] + vec_z[3])

    pieces = {
        "ln1": norm_one,
        "caps": masks,
        "tr": turned,
        "qkv": project,
        "att": attend,
        "op0": heads_out,
        "ln2": norm_two,
        "up": up,
        "gd": down_grad,
        "pre": pre_grad,
        "da2": units_back,
        "ln2b": norm_two_back,
        "gout": out_grad,
        "do": heads_back,
        "attb": attend_back,
        "gp": proj_grad,
        "da1": heads_in,
        "op2": units_out,
        "op2s": send_units,
        "ln1b": norm_one_back,
        "fout": finish_out,
        "vec": small_sums,
    }

    vectors[...] = jnp.zeros_like(vectors)
    place.greet()
    for kind, *what in PLAN:
        if kind == "g":
            unit, stage = what
            if stage == 0:
                cols = pl.ds(*GATHER_UNITS[unit][:2])
                full[place.z, place.y, place.x, :, cols] = matrices[:, cols].astype(BF16)
            else:
                gather.settle(unit, stage - 1)
            gather.begin(unit, stage)
        elif kind == "gf":
            gather.settle(what[0], 2)
        elif kind == "s":
            unit, stage = what
            if stage > 0:
                scatter.add(unit, stage - 1)
            if stage < 3:
                scatter.begin(unit, stage)
        else:
            pieces[kind](*what)
    gather.drain()
    scatter.drain()
    for turn in (2, 3):
        for item in range(items):
            exchange(turn, item).wait_send()


def run_block(inner, tokens, cotangent, task_mask, group_ids, slab, norm_bias, column_bias):
    rows = tokens.shape[0]
    items, length = group_ids.shape
    slab_rows, cols = slab.shape
    heads = HEAD_COLS // HD
    gather_units, scatter_units = len(GATHER_UNITS), len(SCATTER_UNITS)
    dma = pltpu.SemaphoreType.DMA
    vmem = pltpu.VMEM
    in_vmem = pl.BlockSpec(memory_space=pltpu.VMEM)
    return pl.pallas_call(
        functools.partial(block_kernel, inner, items, length),
        out_shape=(
            jax.ShapeDtypeStruct((rows, D), BF16),
            jax.ShapeDtypeStruct((rows, D), F32),
            jax.ShapeDtypeStruct((slab_rows, cols), F32),
            jax.ShapeDtypeStruct((16, D), F32),
        ),
        in_specs=[in_vmem] * 7,
        out_specs=(in_vmem,) * 4,
        scratch_shapes=[
            vmem((NZ, NY, NX, slab_rows, cols), BF16),
            vmem((NZ, NY, NX, slab_rows, cols), BF16),
            vmem((NZ, 2, slab_rows, cols), BF16),
            vmem((NZ, slab_rows, cols), BF16),
            vmem((NZ - 1, slab_rows, cols), BF16),
            vmem((NZ - 1, 2, 2, slab_rows, Z_FIRST_COLS), BF16),
            vmem((2, slab_rows, Z_FIRST_COLS), BF16),
            vmem((slab_rows, Z_FIRST_COLS), BF16),
            vmem((rows, D), BF16),
            vmem((D, rows), BF16),
            vmem((rows, D), BF16),
            vmem((D, rows), BF16),
            vmem((D, rows), BF16),
            vmem((rows, 3 * HEAD_COLS), BF16),
            vmem((rows, 3 * HEAD_COLS), BF16),
            vmem((rows, HEAD_COLS), BF16),
            vmem((rows, HEAD_COLS), BF16),
            vmem((items, length, length), F32),
            vmem((items, heads, length, length), F32),
            vmem((rows, D), F32),
            vmem((rows, UNIT_COLS), F32),
            vmem((rows, UNIT_COLS), BF16),
            vmem((rows, UNIT_COLS), BF16),
            vmem((rows, D), F32),
            vmem((rows, D), BF16),
            vmem((2, rows, D), BF16),
            vmem((2, rows, D), BF16),
            vmem((2, 16, D), F32),
            vmem((NZ, 16, D), F32),
            dma((gather_units, 3, NZ - 1)),
            dma((gather_units, 3, NZ - 1)),
            dma((scatter_units, 3, NZ - 1)),
            dma((scatter_units, 3, NZ - 1)),
            dma((4, items)),
            dma((4, items)),
            dma((2 + NZ - 1,)),
            dma((2 + NZ - 1,)),
        ],
        compiler_params=pltpu.CompilerParams(
            collective_id=0, has_side_effects=True, vmem_limit_bytes=60 << 20
        ),
    )(tokens, cotangent, task_mask, group_ids, slab, norm_bias, column_bias)


def adam_update(weight_now, gradient, first_now, second_now, step_rate, weight_decay):
    first_new = BETA_FIRST * first_now + (1.0 - BETA_FIRST) * gradient
    second_new = BETA_SECOND * second_now + (1.0 - BETA_SECOND) * gradient * gradient
    first_fixed = first_new / (1.0 - BETA_FIRST**STEP)
    second_fixed = second_new / (1.0 - BETA_SECOND**STEP)
    weight_new = weight_now - step_rate * (
        first_fixed / (jnp.sqrt(second_fixed) + EPS_ADAM) + weight_decay * weight_now
    )
    return (weight_new, first_new, second_new)


def local(
    tokens,
    cotangent,
    task_mask,
    group_ids,
    matrices,
    matrix_first,
    matrix_second,
    matrix_average,
    norm_bias,
    norm_first,
    norm_second,
    norm_average,
    column_bias,
    column_first,
    column_second,
    column_average,
):
    inner = lax.axis_size("dp") // OUTER
    groups = [[outer * inner + i for i in range(inner)] for outer in range(OUTER)]
    slab = matrices
    if inner > 1:
        slab = lax.all_gather(
            matrices.astype(BF16), "dp", axis=0, tiled=True, axis_index_groups=groups
        ).astype(F32)
    output, input_grad, matrix_grad, vectors = run_block(
        inner, tokens, cotangent, task_mask, group_ids, slab, norm_bias, column_bias.reshape(1, -1)
    )
    if inner > 1:
        matrix_grad = lax.psum_scatter(
            matrix_grad, "dp", scatter_dimension=0, tiled=True, axis_index_groups=groups
        )
        vectors = jnp.sum(lax.all_gather(vectors, "dp", axis=0, axis_index_groups=groups), 0)
    norm_grad = vectors[:6]
    column_grad = vectors[6:9].reshape(-1)
    matrix_updated, matrix_moment, matrix_squares = adam_update(
        matrices, matrix_grad, matrix_first, matrix_second, RATE_MATRIX, DECAY_MATRIX
    )
    norm_updated, norm_moment, norm_squares = adam_update(
        norm_bias, norm_grad, norm_first, norm_second, RATE_VECTOR, 0.0
    )
    column_updated, column_moment, column_squares = adam_update(
        column_bias, column_grad, column_first, column_second, RATE_VECTOR, 0.0
    )
    matrix_smoothed = AVERAGE_KEEP * matrix_average + (1.0 - AVERAGE_KEEP) * matrix_updated
    norm_smoothed = AVERAGE_KEEP * norm_average + (1.0 - AVERAGE_KEEP) * norm_updated
    column_smoothed = AVERAGE_KEEP * column_average + (1.0 - AVERAGE_KEEP) * column_updated
    return (
        output,
        input_grad,
        matrix_grad,
        matrix_updated,
        matrix_moment,
        matrix_squares,
        matrix_smoothed,
        norm_grad,
        norm_updated,
        norm_moment,
        norm_squares,
        norm_smoothed,
        column_grad,
        column_updated,
        column_moment,
        column_squares,
        column_smoothed,
    )


def solution(mesh):
    placed = (
        P("dp", None),
        P("dp", None),
        P("dp", None),
        P("dp", None),
        P("dp", "mp"),
        P("dp", "mp"),
        P("dp", "mp"),
        P("dp", "mp"),
        P(),
        P(),
        P(),
        P(),
        P("mp"),
        P("mp"),
        P("mp"),
        P("mp"),
    )
    return jax.shard_map(
        local,
        mesh=mesh,
        in_specs=placed,
        out_specs=(
            P("dp", None),
            P("dp", None),
            P("dp", "mp"),
            P("dp", "mp"),
            P("dp", "mp"),
            P("dp", "mp"),
            P("dp", "mp"),
            P(),
            P(),
            P(),
            P(),
            P(),
            P("mp"),
            P("mp"),
            P("mp"),
            P("mp"),
            P("mp"),
        ),
        check_vma=False,
    )
```

```python
import functools

import jax
import jax.numpy as jnp
from jax import lax
from jax.experimental import pallas as pl
from jax.experimental.pallas import tpu as pltpu
from jax.sharding import PartitionSpec as P

MESH = pl.DeviceIdType.MESH

D = 768
HEADS = 12
HD = 64
FF = 3072
STEP = 10


NORM_EPSILON = 1e-06
NEGATIVE = -1e30
GELU_SCALE = 0.7978845608028654
GELU_CUBIC = 0.044715
BETA_FIRST = 0.9
BETA_SECOND = 0.999
EPS_ADAM = 1e-08
RATE_MATRIX = 0.1
RATE_VECTOR = 0.3
DECAY_MATRIX = 0.1
AVERAGE_KEEP = 0.7


NZ, NY, NX = 4, 2, 2
OUTER = NZ * NY * NX
COL_TILE = 256
F32, BF16 = jnp.float32, jnp.bfloat16


class Place:
    def __init__(self, inner):
        index = lax.axis_index("dp")
        outer = index // inner
        self.inner = inner
        self.rest = index % inner
        self.core = lax.axis_index("mp")
        self.x = outer % NX
        self.y = (outer // NX) % NY
        self.z = outer // (NX * NY)
        self.partner_z = self.z + 1 - 2 * (self.z % 2)
        self.near_pair = pl.ds(2 * (self.z // 2), 2)
        self.far_pair = pl.ds(2 - 2 * (self.z // 2), 2)

    def device(self, z, y, x):
        return (((z * NY + y) * NX + x) * self.inner + self.rest, self.core)

    def along_z(self, step):
        return self.device((self.z + step) % NZ, self.y, self.x)

    def across_y(self):
        return self.device(self.z, 1 - self.y, self.x)

    def across_x(self):
        return self.device(self.z, self.y, 1 - self.x)

    def sibling(self):
        return (self.device(self.z, self.y, self.x)[0], 1 - self.core)

    def greet(self):
        barrier = pltpu.get_barrier_semaphore()
        peers = [self.along_z(step) for step in range(1, NZ)]
        peers += [self.across_y(), self.across_x(), self.sibling()]
        for peer in peers:
            pl.semaphore_signal(barrier, inc=1, device_id=peer, device_id_type=MESH)
        pl.semaphore_wait(barrier, len(peers))


def remote(src, dst, send_sem, recv_sem, peer):
    return pltpu.make_async_remote_copy(
        src_ref=src,
        dst_ref=dst,
        send_sem=send_sem,
        recv_sem=recv_sem,
        device_id=peer,
        device_id_type=MESH,
    )


class Mover:
    line = "abc"

    def __init__(self, place, units, full, send_sem, recv_sem):
        self.place, self.units, self.full = place, units, full
        self.send_sem, self.recv_sem = send_sem, recv_sem
        self.inner_z = (place.z == 1) | (place.z == 2)
        self.outer_z = (place.z == 0) | (place.z == 3)

    def stages(self, unit):
        found = []
        route = self.units[unit][2]
        for spot, axis in enumerate(route):
            for name in self.line if axis == "z" else axis:
                found.append((name, route[:spot], route[spot + 1 :]))
        return found

    def peer(self, name):
        p = self.place
        if name == "x":
            return p.across_x()
        if name == "y":
            return p.across_y()
        return p.device(p.partner_z if name in "ac" else NZ - 1 - p.z, p.y, p.x)

    def block(self, unit, whole, z, y, x):
        start, width, _ = self.units[unit]
        index = [slice(None) if name in whole else here for name, here in (("z", z), ("y", y), ("x", x))]
        return tuple(index) + (slice(None), pl.ds(start, width))

    def copy(self, unit, stage, src, dst, name):
        return remote(src, dst, self.send_sem.at[unit, stage], self.recv_sem.at[unit, stage], self.peer(name))

    def begin(self, unit, stage):
        name = self.stages(unit)[stage][0]
        self.guarded(self.sender(name), lambda: self.leaving(unit, stage).start())

    def settle(self, unit, stage):
        name = self.stages(unit)[stage][0]
        self.guarded(self.receiver(name), lambda: self.arriving(unit, stage).wait_recv())

    @staticmethod
    def guarded(condition, action):
        if condition is None:
            action()
        else:
            pl.when(condition)(action)

    def drain(self):
        for unit in range(len(self.units)):
            for stage, (name, _, _) in enumerate(self.stages(unit)):
                self.guarded(self.sender(name), lambda: self.leaving(unit, stage).wait_send())


class Gather(Mover):
    def sender(self, name):
        return self.inner_z if name in "bc" else None

    def receiver(self, name):
        return {"b": self.inner_z, "c": self.outer_z}.get(name)

    def leaving(self, unit, stage):
        p = self.place
        name, before, _ = self.stages(unit)[stage]
        z = {"b": p.near_pair, "c": p.far_pair}.get(name, p.z)
        mine = self.full.at[self.block(unit, before, z, p.y, p.x)]
        return self.copy(unit, stage, mine, mine, name)

    def arriving(self, unit, stage):
        p = self.place
        name, before, _ = self.stages(unit)[stage]
        z = {"a": p.partner_z, "b": p.far_pair, "c": p.far_pair}.get(name, p.z)
        y = 1 - p.y if name == "y" else p.y
        x = 1 - p.x if name == "x" else p.x
        theirs = self.full.at[self.block(unit, before, z, y, x)]
        return self.copy(unit, stage, theirs, theirs, name)


class Scatter(Mover):
    line = "cba"

    def __init__(self, place, units, full, landings, result, send_sem, recv_sem):
        super().__init__(place, units, full, send_sem, recv_sem)
        self.landings, self.result = landings, result

    def sender(self, name):
        return {"b": self.inner_z, "c": self.outer_z}.get(name)

    def receiver(self, name):
        return self.inner_z if name in "bc" else None

    def landing(self, unit, stage):
        _, width, route = self.units[unit]
        got = self.landings[int(route[0] == "z")][stage]
        lead = (slice(None),) * (len(got.shape) - 1)
        return got.at[lead + (pl.ds(LANDING[unit], width),)]

    def leaving(self, unit, stage):
        p = self.place
        name, _, after = self.stages(unit)[stage]
        z = {"a": p.partner_z, "b": p.far_pair, "c": p.far_pair}.get(name, p.z)
        y = 1 - p.y if name == "y" else p.y
        x = 1 - p.x if name == "x" else p.x
        away = self.full.at[self.block(unit, after, z, y, x)]
        return self.copy(unit, stage, away, self.landing(unit, stage), name)

    arriving = leaving

    def add(self, unit, stage):
        p = self.place
        steps = self.stages(unit)
        name, _, after = steps[stage]

        def action():
            self.arriving(unit, stage).wait_recv()
            z = {"b": p.near_pair, "c": p.far_pair}.get(name, p.z)
            part = self.block(unit, after, z, p.y, p.x)
            total = self.full[part].astype(F32) + self.landing(unit, stage)[...].astype(F32)
            if stage + 1 == len(steps):
                start, width, _ = self.units[unit]
                self.result[:, pl.ds(start, width)] = total
            else:
                self.full[part] = total.astype(BF16)

        self.guarded(self.receiver(name), action)


def rows_dot(left, right):
    return jnp.dot(left, right, preferred_element_type=F32)


def dot_rt(left, right):
    return lax.dot_general(left, right, (((1,), (1,)), ((), ())), preferred_element_type=F32)


def dot_lt(left, right):
    return lax.dot_general(left, right, (((0,), (0,)), ((), ())), preferred_element_type=F32)


def normalized(values):
    center = values - jnp.mean(values, -1, keepdims=True)
    spread = jnp.mean(center * center, -1, keepdims=True)
    scale = lax.rsqrt(spread + NORM_EPSILON)
    return center * scale, scale


def total_rows(values):
    return jnp.sum(values, 0, keepdims=True)


GATHER_UNITS = (
    (0, 128, "zxy"),
    (128, 128, "zyx"),
    (256, 128, "zxy"),
    (384, 128, "zyx"),
    (512, 128, "zxy"),
    (640, 128, "zyx"),
    (768, 128, "zxy"),
    (896, 128, "zyx"),
    (1024, 128, "zxy"),
    (1152, 128, "zyx"),
    (1280, 128, "zxy"),
    (1408, 128, "zyx"),
    (1536, 256, "zyx"),
    (1792, 256, "zxy"),
    (2048, 256, "zyx"),
    (2304, 128, "yxz"),
    (2432, 256, "zxy"),
    (2688, 128, "zyx"),
    (2816, 128, "xyz"),
    (2944, 128, "zxy"),
    (3072, 128, "zyx"),
    (3200, 128, "zxy"),
    (3328, 128, "xyz"),
    (3456, 128, "yxz"),
    (3584, 128, "zyx"),
    (3712, 128, "zxy"),
    (3840, 128, "xyz"),
    (3968, 128, "yxz"),
    (4096, 128, "zyx"),
    (4224, 128, "xyz"),
    (4352, 128, "zxy"),
    (4480, 128, "yxz"),
)
SCATTER_UNITS = (
    (3072, 128, "zxy"),
    (3200, 128, "zyx"),
    (3328, 256, "yxz"),
    (3584, 256, "xyz"),
    (3840, 256, "yxz"),
    (4096, 128, "xyz"),
    (4224, 128, "zxy"),
    (4352, 128, "zyx"),
    (4480, 128, "zxy"),
    (1536, 256, "xyz"),
    (1792, 128, "zyx"),
    (1920, 128, "yxz"),
    (2048, 128, "zxy"),
    (2176, 128, "yxz"),
    (2304, 256, "xyz"),
    (2560, 256, "yxz"),
    (2816, 128, "zyx"),
    (2944, 128, "xyz"),
    (1152, 256, "yxz"),
    (1408, 128, "xyz"),
    (0, 128, "xyz"),
    (128, 128, "yxz"),
    (256, 128, "xyz"),
    (384, 128, "zxy"),
    (512, 128, "yxz"),
    (640, 128, "zyx"),
    (768, 128, "xyz"),
    (896, 128, "yxz"),
    (1024, 128, "xyz"),
)
LANDING = (
    0, 128, 0, 256, 512, 768, 256, 384, 512, 896, 640, 1152,
    768, 1280, 1408, 1664, 896, 1920, 2048, 2304, 2432, 2560, 2688, 1024,
    2816, 1152, 2944, 3072, 3200,
)
LATE_COLS, EARLY_COLS = 3328, 1280
PLAN = (
    ("g", 0, 0), ("g", 1, 0), ("g", 2, 0), ("g", 3, 0), ("g", 4, 0), ("g", 15, 0), ("g", 18, 0), ("g", 22, 0),
    ("g", 23, 0), ("g", 5, 0), ("g", 26, 0), ("g", 27, 0), ("ln1", 0), ("g", 6, 0), ("g", 29, 0), ("g", 31, 0),
    ("ln1", 1), ("g", 7, 0), ("g", 8, 0), ("caps", 0), ("g", 0, 1), ("g", 9, 0), ("g", 10, 0), ("tr", 0),
    ("g", 1, 1), ("g", 2, 1), ("g", 11, 0), ("g", 12, 0), ("g", 15, 1), ("g", 3, 1), ("g", 18, 1), ("g", 22, 1),
    ("g", 23, 1), ("g", 26, 1), ("g", 27, 1), ("tr", 1), ("g", 4, 1), ("g", 5, 1), ("g", 13, 0), ("g", 6, 1),
    ("g", 29, 1), ("g", 31, 1), ("g", 14, 0), ("g", 7, 1), ("g", 0, 2), ("g", 8, 1), ("g", 9, 1), ("g", 1, 2),
    ("g", 10, 1), ("g", 11, 1), ("g", 2, 2), ("g", 12, 1), ("g", 3, 2), ("g", 13, 1), ("g", 4, 2), ("g", 14, 1),
    ("g", 5, 2), ("g", 0, 3), ("g", 6, 2), ("g", 1, 3), ("g", 7, 2), ("g", 2, 3), ("g", 8, 2), ("g", 3, 3),
    ("g", 9, 2), ("g", 4, 3), ("g", 10, 2), ("g", 0, 4), ("g", 5, 3), ("g", 11, 2), ("g", 1, 4), ("g", 6, 3),
    ("g", 2, 4), ("g", 16, 0), ("g", 7, 3), ("g", 12, 2), ("g", 3, 4), ("g", 8, 3), ("g", 4, 4), ("g", 9, 3),
    ("g", 13, 2), ("g", 10, 3), ("g", 11, 3), ("g", 14, 2), ("g", 16, 1), ("g", 5, 4), ("g", 17, 0),
    ("g", 12, 3), ("g", 19, 0), ("g", 6, 4), ("g", 20, 0), ("g", 21, 0), ("g", 24, 0), ("g", 13, 3),
    ("g", 25, 0), ("g", 16, 2), ("g", 14, 3), ("g", 17, 1), ("g", 28, 0), ("g", 19, 1), ("g", 30, 0),
    ("g", 20, 1), ("g", 7, 4), ("g", 21, 1), ("g", 24, 1), ("g", 8, 4), ("g", 15, 2), ("g", 25, 1),
    ("g", 17, 2), ("g", 10, 4), ("g", 16, 3), ("g", 19, 2), ("g", 28, 1), ("g", 30, 1), ("g", 20, 2),
    ("g", 21, 2), ("g", 9, 4), ("g", 15, 3), ("g", 24, 2), ("g", 17, 3), ("g", 25, 2), ("g", 11, 4),
    ("g", 19, 3), ("g", 28, 2), ("g", 20, 3), ("g", 30, 2), ("g", 21, 3), ("g", 13, 4), ("g", 18, 2),
    ("g", 24, 3), ("g", 12, 4), ("g", 25, 3), ("g", 22, 2), ("g", 28, 3), ("g", 15, 4), ("g", 30, 3),
    ("g", 18, 3), ("g", 22, 3), ("g", 16, 4), ("g", 23, 2), ("g", 14, 4), ("g", 26, 2), ("g", 18, 4), ("gf", 0),
    ("gf", 1), ("gf", 2), ("gf", 3), ("gf", 4), ("gf", 5), ("gf", 6), ("gf", 7), ("gf", 8), ("qkv", 0),
    ("g", 23, 3), ("qkv", 1), ("att", 0, 0), ("g", 22, 4), ("g", 26, 3), ("att", 0, 1), ("g", 19, 4),
    ("att", 0, 2), ("g", 17, 4), ("g", 21, 4), ("g", 27, 2), ("gf", 9), ("gf", 10), ("gf", 11), ("op0", 0),
    ("g", 20, 4), ("g", 23, 4), ("att", 1, 0), ("att", 1, 1), ("g", 26, 4), ("att", 1, 2), ("g", 27, 3),
    ("ln2", 0), ("op0", 1), ("g", 25, 4), ("g", 29, 2), ("g", 24, 4), ("g", 30, 4), ("g", 31, 2), ("g", 27, 4),
    ("g", 28, 4), ("g", 29, 3), ("ln2", 1), ("g", 31, 3), ("tr", 2), ("gf", 12), ("up", 0), ("gf", 13),
    ("up", 1), ("gf", 14), ("up", 2), ("gf", 15), ("gf", 16), ("up", 3), ("g", 29, 4), ("gf", 17), ("up", 4),
    ("gf", 18), ("gf", 19), ("up", 5), ("gd", 0), ("g", 31, 4), ("gd", 1), ("s", 0, 0), ("gd", 2), ("gd", 3),
    ("s", 3, 0), ("gd", 4), ("s", 1, 0), ("s", 2, 0), ("gd", 5), ("gf", 20), ("gf", 21), ("pre", 0), ("gf", 22),
    ("gf", 23), ("pre", 1), ("gf", 24), ("gf", 25), ("pre", 2), ("s", 6, 0), ("gf", 26), ("gf", 27), ("pre", 3),
    ("s", 0, 1), ("s", 5, 0), ("gf", 28), ("gf", 29), ("pre", 4), ("s", 4, 0), ("s", 7, 0), ("gf", 30),
    ("gf", 31), ("pre", 5), ("da2", 0), ("s", 1, 1), ("s", 9, 0), ("da2", 1), ("s", 8, 0), ("s", 3, 1),
    ("s", 0, 2), ("s", 2, 1), ("s", 6, 1), ("s", 5, 1), ("s", 1, 2), ("ln2b", 0), ("s", 7, 1), ("s", 10, 0),
    ("ln2b", 1), ("s", 6, 2), ("s", 4, 1), ("s", 8, 1), ("s", 11, 0), ("gout", 0), ("s", 0, 3), ("s", 9, 1),
    ("s", 3, 2), ("s", 1, 3), ("do", 0), ("s", 7, 2), ("do", 1), ("s", 5, 2), ("s", 14, 0), ("attb", 0, 0),
    ("s", 2, 2), ("s", 10, 1), ("s", 8, 2), ("s", 13, 0), ("attb", 0, 1), ("s", 6, 3), ("s", 0, 4), ("s", 4, 2),
    ("s", 3, 3), ("s", 11, 1), ("attb", 0, 2), ("s", 1, 4), ("s", 5, 3), ("s", 7, 3), ("s", 9, 2), ("s", 10, 2),
    ("s", 15, 0), ("attb", 1, 0), ("s", 3, 4), ("s", 2, 3), ("s", 5, 4), ("s", 13, 1), ("s", 0, 5), ("s", 8, 3),
    ("s", 14, 1), ("s", 7, 4), ("attb", 1, 1), ("s", 6, 4), ("s", 4, 3), ("s", 11, 2), ("s", 1, 5), ("s", 9, 3),
    ("s", 2, 4), ("s", 12, 0), ("s", 17, 0), ("attb", 1, 2), ("s", 10, 3), ("s", 3, 5), ("s", 8, 4),
    ("s", 13, 2), ("s", 5, 5), ("s", 7, 5), ("s", 19, 0), ("gp", 0), ("s", 4, 4), ("s", 11, 3), ("s", 2, 5),
    ("s", 15, 1), ("s", 16, 0), ("s", 9, 4), ("s", 18, 0), ("gp", 1), ("s", 17, 1), ("gp", 2), ("s", 6, 5),
    ("s", 11, 4), ("s", 14, 2), ("s", 12, 1), ("s", 10, 4), ("s", 13, 3), ("s", 8, 5), ("s", 20, 0), ("da1", 0),
    ("s", 4, 5), ("s", 19, 1), ("da1", 1), ("s", 23, 0), ("op2", 0), ("s", 22, 0), ("op2", 1), ("s", 10, 5),
    ("s", 15, 2), ("s", 16, 1), ("s", 9, 5), ("s", 21, 0), ("s", 11, 5), ("s", 12, 2), ("s", 26, 0),
    ("s", 13, 4), ("s", 14, 3), ("s", 18, 1), ("ln1b", 0), ("s", 17, 2), ("s", 20, 1), ("s", 25, 0),
    ("ln1b", 1), ("s", 16, 2), ("s", 19, 2), ("s", 15, 3), ("s", 22, 1), ("s", 14, 4), ("s", 23, 1),
    ("s", 24, 0), ("s", 28, 0), ("op2s", 0), ("vec", 0), ("s", 13, 5), ("s", 12, 3), ("s", 21, 1), ("s", 26, 1),
    ("s", 17, 3), ("s", 20, 2), ("s", 15, 4), ("s", 27, 0), ("s", 22, 2), ("s", 18, 2), ("s", 25, 1),
    ("s", 23, 2), ("s", 16, 3), ("s", 17, 4), ("vec", 1), ("s", 19, 3), ("s", 24, 1), ("s", 28, 1),
    ("s", 14, 5), ("s", 26, 2), ("s", 12, 4), ("s", 20, 3), ("s", 15, 5), ("s", 21, 2), ("s", 25, 2),
    ("s", 22, 3), ("s", 19, 4), ("s", 27, 1), ("s", 20, 4), ("s", 24, 2), ("s", 18, 3), ("s", 16, 4),
    ("vec", 2), ("s", 22, 4), ("s", 17, 5), ("s", 23, 3), ("s", 28, 2), ("s", 12, 5), ("s", 26, 3),
    ("s", 27, 2), ("s", 21, 3), ("s", 16, 5), ("s", 18, 4), ("s", 23, 4), ("s", 25, 3), ("s", 19, 5),
    ("s", 26, 4), ("s", 20, 5), ("s", 21, 4), ("s", 24, 3), ("s", 22, 5), ("s", 23, 5), ("vec", 3),
    ("s", 25, 4), ("s", 28, 3), ("fout", 0), ("s", 27, 3), ("fout", 1), ("s", 18, 5), ("s", 26, 5),
    ("s", 24, 4), ("s", 21, 5), ("s", 25, 5), ("s", 28, 4), ("s", 27, 4), ("s", 24, 5), ("s", 28, 5),
    ("s", 27, 5),
)

HEAD_COLS, UNIT_COLS = 384, 1536
Q0, K0, V0, O0, U0, W0 = 0, 384, 768, 1152, 1536, 3072


def block_kernel(inner, items, length, tokens, cotangent, task_mask, group_ids, matrices, norm, column, *rest):
    (out, input_grad, matrix_grad, vectors) = rest[:4]
    (full, grads) = rest[4:6]
    landings = (rest[6:11], rest[11:16])
    (act_one, act_one_t, act_two, act_two_t, cot_t, proj, grad_proj, heads, grad_heads) = rest[16:25]
    (caps, probs, residual, slope, hidden, grad_pre, grad_res, grad_low, ex_send, ex_recv) = rest[25:35]
    (vec_got, vec_z, g_send, g_recv, s_send, s_recv, es, er, vs, vr) = rest[35:]
    place = Place(inner)
    gather = Gather(place, GATHER_UNITS, full, g_send, g_recv)
    scatter = Scatter(place, SCATTER_UNITS, grads, landings, matrix_grad, s_send, s_recv)

    def weight(start, width):
        return full[:, :, :, :, pl.ds(start, width)].reshape(D, width)

    def put_grad(start, width, value):
        grads[:, :, :, :, pl.ds(start, width)] = value.astype(BF16).reshape(grads.shape[:4] + (width,))

    def rows_of(item):
        return pl.ds(item * length, length)

    def add_vector(row, first, value):
        cols = pl.ds(first, value.shape[1])
        vectors[row : row + 1, cols] = vectors[row : row + 1, cols] + value

    def exchange(turn, item):
        part = rows_of(item)
        return remote(
            ex_send.at[turn % 2, part],
            ex_recv.at[turn % 2, part],
            es.at[turn, item],
            er.at[turn, item],
            place.sibling(),
        )

    def fill_part(turn, item, value):
        if turn >= 2:
            exchange(turn - 2, item).wait_send()
        ex_send[turn % 2, rows_of(item)] = value.astype(BF16)

    def both(turn, item):
        exchange(turn, item).wait_recv()
        part = rows_of(item)
        return ex_send[turn % 2, part].astype(F32) + ex_recv[turn % 2, part].astype(F32)

    def norm_one(item):
        part = rows_of(item)
        unit_x, _ = normalized(tokens[part].astype(F32))
        act_one[part] = (unit_x * norm[0:1] + norm[1:2]).astype(BF16)
        add_vector(5, 0, total_rows(cotangent[part].astype(F32)))

    def masks(_):
        key_index = lax.broadcasted_iota(jnp.int32, (length, length), 0)
        query_index = lax.broadcasted_iota(jnp.int32, (length, length), 1)
        same = key_index == query_index
        slots = task_mask.shape[1]
        slot_same = lax.broadcasted_iota(jnp.int32, (slots, slots), 0) == lax.broadcasted_iota(
            jnp.int32, (slots, slots), 1
        )
        for item in range(items):
            query_ids = group_ids[item : item + 1, :]
            key_ids = jnp.sum(jnp.where(same, query_ids, 0), axis=1, keepdims=True)
            filled = jnp.sum(jnp.where(slot_same, task_mask[item : item + 1, :], 0), axis=1, keepdims=True)
            live = jnp.concatenate([filled, jnp.ones((length - slots, 1), jnp.int32)], axis=0)
            odd_key = jnp.where((key_ids == 0) | (key_ids % 2 == 1), 1, 0)
            earlier = (odd_key == 1) & (key_ids <= query_ids)
            visible = (earlier | (key_ids == query_ids)) & (live == 1)
            caps[item] = jnp.where(visible | same, 3.0e38, NEGATIVE)

    def turned(which):
        source, target = ((act_one, act_one_t), (cotangent, cot_t), (act_two, act_two_t))[which]
        target[...] = source[...].T

    def project(item):
        part = rows_of(item)
        for start, scale, bias in ((Q0, HD**-0.5, 0), (K0, 1.0, None), (V0, 1.0, HEAD_COLS)):
            value = rows_dot(act_one[part], weight(start, HEAD_COLS))
            if bias is not None:
                value = value + column[pl.ds(bias, HEAD_COLS)].reshape(1, HEAD_COLS)
            value = value.astype(BF16)
            if scale != 1.0:
                value = value * jnp.asarray(scale, BF16)
            proj[part, start : start + HEAD_COLS] = value

    lane = lax.broadcasted_iota(jnp.int32, (length, 128), 1)
    first_half = lane < HD

    def lanes(start, pair):
        return pl.ds(start + pair * 128, 128)

    def attend(item, pair):
        part = rows_of(item)
        query, key, value = (proj[part, lanes(start, pair)] for start in (Q0, K0, V0))
        sides = []
        for side in range(2):
            own = first_half if side == 0 else ~first_half
            scores = dot_rt(jnp.where(own, key, jnp.zeros_like(key)), query)
            scores = jnp.minimum(scores, caps[item])
            weights = jnp.exp(scores - jnp.max(scores, 0, keepdims=True))
            prob = weights * (1.0 / jnp.sum(weights, 0, keepdims=True))
            probs[item, pair * 2 + side] = prob
            sides.append(dot_lt(prob.astype(BF16), value))
        heads[part, lanes(0, pair)] = jnp.where(first_half, sides[0], sides[1]).astype(BF16)

    def heads_out(item):
        fill_part(0, item, dot_rt(heads[rows_of(item)], weight(O0, HEAD_COLS)))
        exchange(0, item).start()

    def norm_two(item):
        part = rows_of(item)
        value = tokens[part].astype(F32) + both(0, item) + norm[4:5]
        residual[part] = value
        unit_x, _ = normalized(value)
        act_two[part] = (unit_x * norm[2:3] + norm[3:4]).astype(BF16)

    def up(index):
        start = index * COL_TILE
        cols = pl.ds(start, COL_TILE)
        unit = rows_dot(act_two[...], weight(U0 + start, COL_TILE))
        unit = unit + column[pl.ds(2 * HEAD_COLS + start, COL_TILE)].reshape(1, COL_TILE)
        square = unit * unit
        bent = jnp.tanh(unit * (GELU_SCALE + (GELU_SCALE * GELU_CUBIC) * square))
        half = 0.5 * (1.0 + bent)
        hidden[:, cols] = (unit * half).astype(BF16)
        slope[:, cols] = half + 0.5 * unit * (1.0 - bent * bent) * (
            GELU_SCALE + (3.0 * GELU_SCALE * GELU_CUBIC) * square
        )

    def down_grad(index):
        start = index * COL_TILE
        put_grad(W0 + start, COL_TILE, rows_dot(cot_t[...], hidden[:, pl.ds(start, COL_TILE)]))

    def pre_grad(index):
        start = index * COL_TILE
        cols = pl.ds(start, COL_TILE)
        value = rows_dot(cotangent[...], weight(W0 + start, COL_TILE))
        low = (value * slope[:, cols]).astype(BF16)
        grad_pre[:, cols] = low
        row, first = divmod(2 * HEAD_COLS + start, D)
        add_vector(6 + row, first, total_rows(low.astype(F32)))
        put_grad(U0 + start, COL_TILE, rows_dot(act_two_t[...], low))

    def units_back(item):
        fill_part(1, item, dot_rt(grad_pre[rows_of(item)], weight(U0, UNIT_COLS)))
        exchange(1, item).start()

    def norm_back(incoming, values, gain):
        unit_x, scale = normalized(values)
        pulled = incoming * gain
        inner_mean = jnp.mean(pulled, -1, keepdims=True)
        cross_mean = jnp.mean(pulled * unit_x, -1, keepdims=True)
        return scale * (pulled - inner_mean - unit_x * cross_mean), total_rows(incoming * unit_x), total_rows(incoming)

    def norm_two_back(item):
        part = rows_of(item)
        value, gain_sum, shift_sum = norm_back(both(1, item), residual[part], norm[2:3])
        value = cotangent[part].astype(F32) + value
        grad_res[part] = value
        grad_low[part] = value.astype(BF16)
        add_vector(2, 0, gain_sum)
        add_vector(3, 0, shift_sum)
        add_vector(4, 0, total_rows(value))

    def out_grad(_):
        put_grad(O0, HEAD_COLS, dot_lt(grad_low[...], heads[...]))

    def heads_back(item):
        part = rows_of(item)
        grad_heads[part] = rows_dot(grad_low[part], weight(O0, HEAD_COLS)).astype(BF16)

    def attend_back(item, pair):
        part = rows_of(item)
        query, key, value = (proj[part, lanes(start, pair)] for start in (Q0, K0, V0))
        grad = grad_heads[part, lanes(0, pair)]
        sides = []
        for side in range(2):
            own = first_half if side == 0 else ~first_half
            prob = probs[item, pair * 2 + side]
            grad_prob = dot_rt(jnp.where(own, value, jnp.zeros_like(value)), grad)
            inner_sum = jnp.sum(prob * grad_prob, 0, keepdims=True)
            low = (prob * (grad_prob - inner_sum)).astype(BF16)
            sides.append(
                (dot_lt(low, key) * (HD**-0.5), rows_dot(low, query), rows_dot(prob.astype(BF16), grad))
            )
        for start, left, right in zip((Q0, K0, V0), sides[0], sides[1]):
            low = jnp.where(first_half, left, right).astype(BF16)
            grad_proj[part, lanes(start, pair)] = low
            if start != K0:
                add_vector(6, (0 if start == Q0 else HEAD_COLS) + pair * 128, total_rows(low.astype(F32)))

    def proj_grad(index):
        cols = pl.ds(index * HEAD_COLS, HEAD_COLS)
        put_grad(index * HEAD_COLS, HEAD_COLS, rows_dot(act_one_t[...], grad_proj[:, cols]))

    def heads_in(item):
        fill_part(2, item, dot_rt(grad_proj[rows_of(item)], weight(Q0, 3 * HEAD_COLS)))
        exchange(2, item).start()

    def units_out(item):
        fill_part(3, item, dot_rt(hidden[rows_of(item)], weight(W0, UNIT_COLS)))

    def send_units(_):
        for item in range(items):
            exchange(3, item).start()

    def norm_one_back(item):
        part = rows_of(item)
        value, gain_sum, shift_sum = norm_back(both(2, item), tokens[part].astype(F32), norm[0:1])
        input_grad[part] = grad_res[part] + value
        add_vector(0, 0, gain_sum)
        add_vector(1, 0, shift_sum)

    def finish_out(item):
        part = rows_of(item)
        out[part] = (residual[part] + both(3, item) + norm[5:6]).astype(BF16)

    def vec_copy(stage, owner_z=None, step=0):
        if stage < 2:
            peer = (place.across_x(), place.across_y())[stage]
            return remote(vectors, vec_got.at[stage], vs.at[stage], vr.at[stage], peer)
        block = vec_z.at[owner_z]
        return remote(block, block, vs.at[1 + step], vr.at[1 + step], place.along_z(step))

    def small_sums(stage):
        if stage in (1, 2):
            vec_copy(stage - 1).wait()
            vectors[...] = vectors[...] + vec_got[stage - 1]
        if stage < 2:
            vec_copy(stage).start()
        elif stage == 2:
            vec_z[place.z] = vectors[...]
            for step in range(1, NZ):
                vec_copy(2, place.z, step).start()
        else:
            for step in range(1, NZ):
                vec_copy(2, (place.z - step) % NZ, step).wait_recv()
                vec_copy(2, place.z, step).wait_send()
            vectors[...] = (vec_z[0] + vec_z[1]) + (vec_z[2] + vec_z[3])

    pieces = {
        "ln1": norm_one,
        "caps": masks,
        "tr": turned,
        "qkv": project,
        "att": attend,
        "op0": heads_out,
        "ln2": norm_two,
        "up": up,
        "gd": down_grad,
        "pre": pre_grad,
        "da2": units_back,
        "ln2b": norm_two_back,
        "gout": out_grad,
        "do": heads_back,
        "attb": attend_back,
        "gp": proj_grad,
        "da1": heads_in,
        "op2": units_out,
        "op2s": send_units,
        "ln1b": norm_one_back,
        "fout": finish_out,
        "vec": small_sums,
    }

    vectors[...] = jnp.zeros_like(vectors)
    place.greet()
    for kind, *what in PLAN:
        if kind == "g":
            unit, stage = what
            if stage == 0:
                cols = pl.ds(*GATHER_UNITS[unit][:2])
                full[place.z, place.y, place.x, :, cols] = matrices[:, cols].astype(BF16)
            else:
                gather.settle(unit, stage - 1)
            gather.begin(unit, stage)
        elif kind == "gf":
            gather.settle(what[0], 4)
        elif kind == "s":
            unit, stage = what
            if stage > 0:
                scatter.add(unit, stage - 1)
            if stage < 5:
                scatter.begin(unit, stage)
        else:
            pieces[kind](*what)
    gather.drain()
    scatter.drain()
    for turn in (2, 3):
        for item in range(items):
            exchange(turn, item).wait_send()


def run_block(inner, tokens, cotangent, task_mask, group_ids, slab, norm_bias, column_bias):
    rows = tokens.shape[0]
    items, length = group_ids.shape
    slab_rows, cols = slab.shape
    heads = HEAD_COLS // HD
    gather_units, scatter_units = len(GATHER_UNITS), len(SCATTER_UNITS)
    dma = pltpu.SemaphoreType.DMA
    vmem = pltpu.VMEM
    in_vmem = pl.BlockSpec(memory_space=pltpu.VMEM)
    return pl.pallas_call(
        functools.partial(block_kernel, inner, items, length),
        out_shape=(
            jax.ShapeDtypeStruct((rows, D), BF16),
            jax.ShapeDtypeStruct((rows, D), F32),
            jax.ShapeDtypeStruct((slab_rows, cols), F32),
            jax.ShapeDtypeStruct((16, D), F32),
        ),
        in_specs=[in_vmem] * 7,
        out_specs=(in_vmem,) * 4,
        scratch_shapes=[
            vmem((NZ, NY, NX, slab_rows, cols), BF16),
            vmem((NZ, NY, NX, slab_rows, cols), BF16),
            vmem((NZ, 2, slab_rows, LATE_COLS), BF16),
            vmem((NZ, slab_rows, LATE_COLS), BF16),
            vmem((2, slab_rows, LATE_COLS), BF16),
            vmem((2, slab_rows, LATE_COLS), BF16),
            vmem((slab_rows, LATE_COLS), BF16),
            vmem((2, NY, NX, slab_rows, EARLY_COLS), BF16),
            vmem((2, NY, NX, slab_rows, EARLY_COLS), BF16),
            vmem((NY, NX, slab_rows, EARLY_COLS), BF16),
            vmem((2, slab_rows, EARLY_COLS), BF16),
            vmem((slab_rows, EARLY_COLS), BF16),
            vmem((rows, D), BF16),
            vmem((D, rows), BF16),
            vmem((rows, D), BF16),
            vmem((D, rows), BF16),
            vmem((D, rows), BF16),
            vmem((rows, 3 * HEAD_COLS), BF16),
            vmem((rows, 3 * HEAD_COLS), BF16),
            vmem((rows, HEAD_COLS), BF16),
            vmem((rows, HEAD_COLS), BF16),
            vmem((items, length, length), F32),
            vmem((items, heads, length, length), F32),
            vmem((rows, D), F32),
            vmem((rows, UNIT_COLS), F32),
            vmem((rows, UNIT_COLS), BF16),
            vmem((rows, UNIT_COLS), BF16),
            vmem((rows, D), F32),
            vmem((rows, D), BF16),
            vmem((2, rows, D), BF16),
            vmem((2, rows, D), BF16),
            vmem((2, 16, D), F32),
            vmem((NZ, 16, D), F32),
            dma((gather_units, 5)),
            dma((gather_units, 5)),
            dma((scatter_units, 5)),
            dma((scatter_units, 5)),
            dma((4, items)),
            dma((4, items)),
            dma((2 + NZ - 1,)),
            dma((2 + NZ - 1,)),
        ],
        compiler_params=pltpu.CompilerParams(
            collective_id=0, has_side_effects=True, vmem_limit_bytes=60 << 20
        ),
    )(tokens, cotangent, task_mask, group_ids, slab, norm_bias, column_bias)


def adam_update(weight_now, gradient, first_now, second_now, step_rate, weight_decay):
    first_new = BETA_FIRST * first_now + (1.0 - BETA_FIRST) * gradient
    second_new = BETA_SECOND * second_now + (1.0 - BETA_SECOND) * gradient * gradient
    first_fixed = first_new / (1.0 - BETA_FIRST**STEP)
    second_fixed = second_new / (1.0 - BETA_SECOND**STEP)
    weight_new = weight_now - step_rate * (
        first_fixed / (jnp.sqrt(second_fixed) + EPS_ADAM) + weight_decay * weight_now
    )
    return (weight_new, first_new, second_new)


def local(
    tokens,
    cotangent,
    task_mask,
    group_ids,
    matrices,
    matrix_first,
    matrix_second,
    matrix_average,
    norm_bias,
    norm_first,
    norm_second,
    norm_average,
    column_bias,
    column_first,
    column_second,
    column_average,
):
    inner = lax.axis_size("dp") // OUTER
    groups = [[outer * inner + i for i in range(inner)] for outer in range(OUTER)]
    slab = matrices
    if inner > 1:
        slab = lax.all_gather(
            matrices.astype(BF16), "dp", axis=0, tiled=True, axis_index_groups=groups
        ).astype(F32)
    output, input_grad, matrix_grad, vectors = run_block(
        inner, tokens, cotangent, task_mask, group_ids, slab, norm_bias, column_bias
    )
    if inner > 1:
        matrix_grad = lax.psum_scatter(
            matrix_grad, "dp", scatter_dimension=0, tiled=True, axis_index_groups=groups
        )
        vectors = jnp.sum(lax.all_gather(vectors, "dp", axis=0, axis_index_groups=groups), 0)
    norm_grad = vectors[:6]
    column_grad = vectors[6:9].reshape(-1)
    matrix_updated, matrix_moment, matrix_squares = adam_update(
        matrices, matrix_grad, matrix_first, matrix_second, RATE_MATRIX, DECAY_MATRIX
    )
    norm_updated, norm_moment, norm_squares = adam_update(
        norm_bias, norm_grad, norm_first, norm_second, RATE_VECTOR, 0.0
    )
    column_updated, column_moment, column_squares = adam_update(
        column_bias, column_grad, column_first, column_second, RATE_VECTOR, 0.0
    )
    matrix_smoothed = AVERAGE_KEEP * matrix_average + (1.0 - AVERAGE_KEEP) * matrix_updated
    norm_smoothed = AVERAGE_KEEP * norm_average + (1.0 - AVERAGE_KEEP) * norm_updated
    column_smoothed = AVERAGE_KEEP * column_average + (1.0 - AVERAGE_KEEP) * column_updated
    return (
        output,
        input_grad,
        matrix_grad,
        matrix_updated,
        matrix_moment,
        matrix_squares,
        matrix_smoothed,
        norm_grad,
        norm_updated,
        norm_moment,
        norm_squares,
        norm_smoothed,
        column_grad,
        column_updated,
        column_moment,
        column_squares,
        column_smoothed,
    )


def solution(mesh):
    placed = (
        P("dp", None),
        P("dp", None),
        P("dp", None),
        P("dp", None),
        P("dp", "mp"),
        P("dp", "mp"),
        P("dp", "mp"),
        P("dp", "mp"),
        P(),
        P(),
        P(),
        P(),
        P("mp"),
        P("mp"),
        P("mp"),
        P("mp"),
    )
    return jax.shard_map(
        local,
        mesh=mesh,
        in_specs=placed,
        out_specs=(
            P("dp", None),
            P("dp", None),
            P("dp", "mp"),
            P("dp", "mp"),
            P("dp", "mp"),
            P("dp", "mp"),
            P("dp", "mp"),
            P(),
            P(),
            P(),
            P(),
            P(),
            P("mp"),
            P("mp"),
            P("mp"),
            P("mp"),
            P("mp"),
        ),
        check_vma=False,
    )
```

```python
import functools

import jax
import jax.numpy as jnp
from jax import lax
from jax.experimental import pallas as pl
from jax.experimental.pallas import tpu as pltpu
from jax.sharding import PartitionSpec as P

MESH = pl.DeviceIdType.MESH

D = 768
HEADS = 12
HD = 64
FF = 3072
STEP = 10


NORM_EPSILON = 1e-06
NEGATIVE = -1e30
GELU_SCALE = 0.7978845608028654
GELU_CUBIC = 0.044715
BETA_FIRST = 0.9
BETA_SECOND = 0.999
EPS_ADAM = 1e-08
RATE_MATRIX = 0.1
RATE_VECTOR = 0.3
DECAY_MATRIX = 0.1
AVERAGE_KEEP = 0.7


NZ, NY, NX = 4, 2, 2
OUTER = NZ * NY * NX
COL_TILE = 256
F32, BF16 = jnp.float32, jnp.bfloat16


class Place:
    def __init__(self, inner):
        index = lax.axis_index("dp")
        outer = index // inner
        self.inner = inner
        self.rest = index % inner
        self.core = lax.axis_index("mp")
        self.x = outer % NX
        self.y = (outer // NX) % NY
        self.z = outer // (NX * NY)
        self.partner_z = self.z + 1 - 2 * (self.z % 2)
        self.near_pair = pl.ds(2 * (self.z // 2), 2)
        self.far_pair = pl.ds(2 - 2 * (self.z // 2), 2)

    def device(self, z, y, x):
        return (((z * NY + y) * NX + x) * self.inner + self.rest, self.core)

    def along_z(self, step):
        return self.device((self.z + step) % NZ, self.y, self.x)

    def across_y(self):
        return self.device(self.z, 1 - self.y, self.x)

    def across_x(self):
        return self.device(self.z, self.y, 1 - self.x)

    def sibling(self):
        return (self.device(self.z, self.y, self.x)[0], 1 - self.core)

    def greet(self):
        barrier = pltpu.get_barrier_semaphore()
        peers = [self.along_z(step) for step in range(1, NZ)]
        peers += [self.across_y(), self.across_x(), self.sibling()]
        for peer in peers:
            pl.semaphore_signal(barrier, inc=1, device_id=peer, device_id_type=MESH)
        pl.semaphore_wait(barrier, len(peers))


def remote(src, dst, send_sem, recv_sem, peer):
    return pltpu.make_async_remote_copy(
        src_ref=src,
        dst_ref=dst,
        send_sem=send_sem,
        recv_sem=recv_sem,
        device_id=peer,
        device_id_type=MESH,
    )


class Mover:
    line = "abc"

    def __init__(self, place, units, full, send_sem, recv_sem):
        self.place, self.units, self.full = place, units, full
        self.send_sem, self.recv_sem = send_sem, recv_sem
        self.inner_z = (place.z == 1) | (place.z == 2)
        self.outer_z = (place.z == 0) | (place.z == 3)

    def stages(self, unit):
        found = []
        route = self.units[unit][2]
        for spot, axis in enumerate(route):
            for name in self.line if axis == "z" else axis:
                found.append((name, route[:spot], route[spot + 1 :]))
        return found

    def peer(self, name):
        p = self.place
        if name == "x":
            return p.across_x()
        if name == "y":
            return p.across_y()
        return p.device(p.partner_z if name in "ac" else NZ - 1 - p.z, p.y, p.x)

    def block(self, unit, whole, z, y, x):
        start, width, _ = self.units[unit]
        index = [slice(None) if name in whole else here for name, here in (("z", z), ("y", y), ("x", x))]
        return tuple(index) + (slice(None), pl.ds(start, width))

    def copy(self, unit, stage, src, dst, name):
        return remote(src, dst, self.send_sem.at[unit, stage], self.recv_sem.at[unit, stage], self.peer(name))

    def begin(self, unit, stage):
        name = self.stages(unit)[stage][0]
        self.guarded(self.sender(name), lambda: self.leaving(unit, stage).start())

    def settle(self, unit, stage):
        name = self.stages(unit)[stage][0]
        self.guarded(self.receiver(name), lambda: self.arriving(unit, stage).wait_recv())

    @staticmethod
    def guarded(condition, action):
        if condition is None:
            action()
        else:
            pl.when(condition)(action)

    def drain(self):
        for unit in range(len(self.units)):
            for stage, (name, _, _) in enumerate(self.stages(unit)):
                self.guarded(self.sender(name), lambda: self.leaving(unit, stage).wait_send())


class Gather(Mover):
    def sender(self, name):
        return self.inner_z if name in "bc" else None

    def receiver(self, name):
        return {"b": self.inner_z, "c": self.outer_z}.get(name)

    def leaving(self, unit, stage):
        p = self.place
        name, before, _ = self.stages(unit)[stage]
        z = {"b": p.near_pair, "c": p.far_pair}.get(name, p.z)
        mine = self.full.at[self.block(unit, before, z, p.y, p.x)]
        return self.copy(unit, stage, mine, mine, name)

    def arriving(self, unit, stage):
        p = self.place
        name, before, _ = self.stages(unit)[stage]
        z = {"a": p.partner_z, "b": p.far_pair, "c": p.far_pair}.get(name, p.z)
        y = 1 - p.y if name == "y" else p.y
        x = 1 - p.x if name == "x" else p.x
        theirs = self.full.at[self.block(unit, before, z, y, x)]
        return self.copy(unit, stage, theirs, theirs, name)


class Scatter(Mover):
    line = "cba"

    def __init__(self, place, units, full, landings, result, send_sem, recv_sem):
        super().__init__(place, units, full, send_sem, recv_sem)
        self.landings, self.result = landings, result

    def sender(self, name):
        return {"b": self.inner_z, "c": self.outer_z}.get(name)

    def receiver(self, name):
        return self.inner_z if name in "bc" else None

    def landing(self, unit, stage):
        _, width, route = self.units[unit]
        got = self.landings[int(route[0] == "z")][stage]
        lead = (slice(None),) * (len(got.shape) - 1)
        return got.at[lead + (pl.ds(LANDING[unit], width),)]

    def leaving(self, unit, stage):
        p = self.place
        name, _, after = self.stages(unit)[stage]
        z = {"a": p.partner_z, "b": p.far_pair, "c": p.far_pair}.get(name, p.z)
        y = 1 - p.y if name == "y" else p.y
        x = 1 - p.x if name == "x" else p.x
        away = self.full.at[self.block(unit, after, z, y, x)]
        return self.copy(unit, stage, away, self.landing(unit, stage), name)

    arriving = leaving

    def add(self, unit, stage):
        p = self.place
        steps = self.stages(unit)
        name, _, after = steps[stage]

        def action():
            self.arriving(unit, stage).wait_recv()
            z = {"b": p.near_pair, "c": p.far_pair}.get(name, p.z)
            part = self.block(unit, after, z, p.y, p.x)
            total = self.full[part].astype(F32) + self.landing(unit, stage)[...].astype(F32)
            if stage + 1 == len(steps):
                start, width, _ = self.units[unit]
                self.result[:, pl.ds(start, width)] = total
            else:
                self.full[part] = total.astype(BF16)

        self.guarded(self.receiver(name), action)


def rows_dot(left, right):
    return jnp.dot(left, right, preferred_element_type=F32)


def dot_rt(left, right):
    return lax.dot_general(left, right, (((1,), (1,)), ((), ())), preferred_element_type=F32)


def dot_lt(left, right):
    return lax.dot_general(left, right, (((0,), (0,)), ((), ())), preferred_element_type=F32)


def normalized(values):
    center = values - jnp.mean(values, -1, keepdims=True)
    spread = jnp.mean(center * center, -1, keepdims=True)
    scale = lax.rsqrt(spread + NORM_EPSILON)
    return center * scale, scale


def total_rows(values):
    return jnp.sum(values, 0, keepdims=True)


GATHER_UNITS = (
    (0, 128, "zyx"),
    (128, 128, "zxy"),
    (256, 128, "zyx"),
    (384, 128, "zxy"),
    (512, 128, "zyx"),
    (640, 128, "zxy"),
    (768, 128, "zyx"),
    (896, 128, "zxy"),
    (1024, 128, "zyx"),
    (1152, 128, "zxy"),
    (1280, 128, "zyx"),
    (1408, 128, "zxy"),
    (1536, 256, "zyx"),
    (1792, 256, "zxy"),
    (2048, 256, "zyx"),
    (2304, 256, "zxy"),
    (2560, 256, "zyx"),
    (2816, 256, "zxy"),
    (3072, 128, "zxy"),
    (3200, 128, "yxz"),
    (3328, 128, "xyz"),
    (3456, 128, "yxz"),
    (3584, 128, "xyz"),
    (3712, 128, "zyx"),
    (3840, 128, "yxz"),
    (3968, 128, "xyz"),
    (4096, 128, "zxy"),
    (4224, 128, "yxz"),
    (4352, 128, "zyx"),
    (4480, 128, "xyz"),
)
SCATTER_UNITS = (
    (3072, 128, "zxy"),
    (3200, 128, "zyx"),
    (3328, 128, "zxy"),
    (3456, 128, "zyx"),
    (3584, 128, "zxy"),
    (3712, 128, "zyx"),
    (3840, 128, "yxz"),
    (3968, 128, "zxy"),
    (4096, 128, "xyz"),
    (4224, 128, "zyx"),
    (4352, 128, "zxy"),
    (4480, 128, "yxz"),
    (1536, 256, "xyz"),
    (1792, 128, "yxz"),
    (1920, 128, "zyx"),
    (2048, 256, "yxz"),
    (2304, 256, "xyz"),
    (2560, 256, "yxz"),
    (2816, 256, "xyz"),
    (1152, 256, "yxz"),
    (1408, 128, "xyz"),
    (0, 128, "xyz"),
    (128, 128, "yxz"),
    (256, 128, "xyz"),
    (384, 128, "yxz"),
    (512, 128, "xyz"),
    (640, 128, "yxz"),
    (768, 128, "xyz"),
    (896, 128, "yxz"),
    (1024, 128, "xyz"),
)
LANDING = (
    0, 128, 256, 384, 512, 640, 0, 768, 128, 896, 1024, 256,
    384, 640, 1152, 768, 1024, 1280, 1536, 1792, 2048, 2176, 2304, 2432,
    2560, 2688, 2816, 2944, 3072, 3200,
)
LATE_COLS, EARLY_COLS = 3328, 1280
PLAN = (
    ("g", 0, 0), ("g", 1, 0), ("g", 2, 0), ("g", 19, 0), ("g", 20, 0), ("g", 21, 0), ("g", 3, 0), ("g", 22, 0),
    ("g", 24, 0), ("g", 25, 0), ("g", 27, 0), ("g", 29, 0), ("g", 4, 0), ("ln1", 0), ("g", 5, 0), ("ln1", 1),
    ("g", 6, 0), ("caps", 0), ("g", 7, 0), ("g", 8, 0), ("tr", 0), ("g", 9, 0), ("g", 10, 0), ("tr", 1),
    ("g", 0, 1), ("g", 1, 1), ("g", 11, 0), ("g", 12, 0), ("g", 2, 1), ("g", 19, 1), ("g", 20, 1), ("g", 21, 1),
    ("g", 22, 1), ("g", 24, 1), ("g", 25, 1), ("g", 3, 1), ("g", 13, 0), ("g", 27, 1), ("g", 29, 1),
    ("g", 4, 1), ("g", 5, 1), ("g", 14, 0), ("g", 6, 1), ("g", 7, 1), ("g", 15, 0), ("g", 8, 1), ("g", 9, 1),
    ("g", 16, 0), ("g", 10, 1), ("g", 11, 1), ("g", 0, 2), ("g", 12, 1), ("g", 1, 2), ("g", 13, 1), ("g", 2, 2),
    ("g", 14, 1), ("g", 3, 2), ("g", 15, 1), ("g", 4, 2), ("g", 16, 1), ("g", 5, 2), ("g", 0, 3), ("g", 6, 2),
    ("g", 1, 3), ("g", 7, 2), ("g", 2, 3), ("g", 8, 2), ("g", 3, 3), ("g", 9, 2), ("g", 4, 3), ("g", 10, 2),
    ("g", 5, 3), ("g", 11, 2), ("g", 0, 4), ("g", 6, 3), ("g", 17, 0), ("g", 1, 4), ("g", 7, 3), ("g", 12, 2),
    ("g", 2, 4), ("g", 8, 3), ("g", 3, 4), ("g", 9, 3), ("g", 13, 2), ("g", 4, 4), ("g", 10, 3), ("g", 5, 4),
    ("g", 11, 3), ("g", 14, 2), ("g", 6, 4), ("g", 17, 1), ("g", 15, 2), ("g", 12, 3), ("g", 16, 2),
    ("g", 13, 3), ("g", 7, 4), ("g", 18, 0), ("g", 23, 0), ("g", 8, 4), ("g", 17, 2), ("g", 14, 3),
    ("g", 15, 3), ("g", 26, 0), ("g", 28, 0), ("g", 19, 2), ("g", 16, 3), ("g", 18, 1), ("g", 9, 4),
    ("g", 23, 1), ("g", 10, 4), ("g", 20, 2), ("g", 17, 3), ("g", 26, 1), ("g", 21, 2), ("g", 28, 1),
    ("g", 18, 2), ("g", 19, 3), ("g", 23, 2), ("g", 11, 4), ("g", 22, 2), ("g", 20, 3), ("g", 26, 2),
    ("g", 28, 2), ("g", 12, 4), ("g", 21, 3), ("g", 18, 3), ("g", 24, 2), ("g", 23, 3), ("g", 19, 4),
    ("g", 22, 3), ("g", 13, 4), ("g", 26, 3), ("g", 28, 3), ("g", 14, 4), ("g", 20, 4), ("g", 24, 3), ("gf", 0),
    ("gf", 1), ("gf", 2), ("gf", 3), ("gf", 4), ("gf", 5), ("gf", 6), ("gf", 7), ("gf", 8), ("qkv", 0),
    ("qkv", 1), ("att", 0, 0), ("g", 16, 4), ("g", 21, 4), ("att", 0, 1), ("g", 15, 4), ("att", 0, 2),
    ("g", 22, 4), ("att", 1, 0), ("att", 1, 1), ("att", 1, 2), ("g", 17, 4), ("g", 24, 4), ("gf", 9),
    ("gf", 10), ("gf", 11), ("op0", 0), ("g", 23, 4), ("op0", 1), ("g", 25, 2), ("g", 27, 2), ("g", 29, 2),
    ("ln2", 0), ("g", 18, 4), ("g", 25, 3), ("ln2", 1), ("g", 28, 4), ("tr", 2), ("g", 26, 4), ("g", 27, 3),
    ("gf", 12), ("up", 0), ("gf", 13), ("up", 1), ("g", 29, 3), ("g", 25, 4), ("gf", 15), ("up", 3), ("gf", 14),
    ("up", 2), ("gd", 0), ("s", 0, 0), ("s", 1, 0), ("gd", 1), ("g", 27, 4), ("gd", 2), ("gd", 3), ("s", 6, 0),
    ("g", 29, 4), ("gf", 17), ("up", 5), ("gd", 5), ("s", 11, 0), ("gf", 16), ("up", 4), ("gd", 4), ("s", 0, 1),
    ("s", 2, 0), ("s", 8, 0), ("gf", 18), ("gf", 19), ("pre", 0), ("s", 12, 0), ("gf", 20), ("gf", 21),
    ("pre", 1), ("s", 13, 0), ("gf", 22), ("gf", 23), ("pre", 2), ("s", 1, 1), ("s", 3, 0), ("s", 15, 0),
    ("gf", 24), ("gf", 25), ("pre", 3), ("s", 16, 0), ("gf", 26), ("gf", 27), ("pre", 4), ("s", 0, 2),
    ("s", 6, 1), ("s", 8, 1), ("s", 4, 0), ("gf", 28), ("gf", 29), ("pre", 5), ("s", 11, 1), ("s", 1, 2),
    ("da2", 0), ("da2", 1), ("s", 17, 0), ("s", 2, 1), ("s", 5, 0), ("s", 13, 1), ("s", 12, 1), ("s", 3, 1),
    ("s", 18, 0), ("s", 7, 0), ("s", 0, 3), ("ln2b", 0), ("s", 2, 2), ("s", 15, 1), ("s", 4, 1), ("s", 8, 2),
    ("s", 16, 1), ("ln2b", 1), ("s", 1, 3), ("s", 3, 2), ("s", 6, 2), ("s", 11, 2), ("gout", 0), ("s", 5, 1),
    ("s", 9, 0), ("s", 13, 2), ("s", 19, 0), ("do", 0), ("do", 1), ("s", 20, 0), ("attb", 0, 0), ("s", 4, 2),
    ("s", 7, 1), ("s", 17, 1), ("attb", 0, 1), ("s", 2, 3), ("s", 8, 3), ("s", 10, 0), ("s", 12, 2),
    ("s", 5, 2), ("s", 18, 1), ("s", 0, 4), ("s", 3, 3), ("attb", 0, 2), ("s", 1, 4), ("s", 6, 3), ("s", 11, 3),
    ("s", 16, 2), ("s", 7, 2), ("s", 15, 2), ("attb", 1, 0), ("s", 8, 4), ("s", 9, 1), ("attb", 1, 1),
    ("s", 4, 3), ("s", 6, 4), ("s", 11, 4), ("s", 13, 3), ("s", 20, 1), ("attb", 1, 2), ("s", 17, 2),
    ("s", 2, 4), ("s", 19, 1), ("s", 1, 5), ("s", 10, 1), ("gp", 0), ("s", 0, 5), ("s", 4, 4), ("s", 9, 2),
    ("s", 12, 3), ("s", 13, 4), ("s", 3, 4), ("s", 18, 2), ("s", 21, 0), ("s", 22, 0), ("s", 23, 0), ("gp", 1),
    ("s", 5, 3), ("s", 20, 2), ("s", 2, 5), ("s", 24, 0), ("s", 25, 0), ("s", 26, 0), ("s", 16, 3), ("gp", 2),
    ("s", 4, 5), ("s", 14, 0), ("da1", 0), ("s", 7, 3), ("s", 3, 5), ("s", 10, 2), ("s", 19, 2), ("s", 28, 0),
    ("da1", 1), ("s", 15, 3), ("s", 8, 5), ("s", 12, 4), ("s", 27, 0), ("op2", 0), ("s", 6, 5), ("s", 11, 5),
    ("s", 22, 1), ("s", 5, 4), ("s", 16, 4), ("s", 21, 1), ("op2", 1), ("s", 17, 3), ("s", 9, 3), ("s", 13, 5),
    ("s", 15, 4), ("s", 24, 1), ("s", 23, 1), ("ln1b", 0), ("s", 18, 3), ("s", 20, 3), ("s", 29, 0),
    ("ln1b", 1), ("s", 7, 4), ("s", 17, 4), ("s", 25, 1), ("s", 26, 1), ("op2s", 0), ("s", 14, 1), ("vec", 0),
    ("s", 28, 1), ("s", 10, 3), ("s", 18, 4), ("s", 27, 1), ("s", 20, 4), ("s", 21, 2), ("s", 19, 3),
    ("s", 9, 4), ("s", 22, 2), ("s", 12, 5), ("s", 5, 5), ("s", 16, 5), ("s", 23, 2), ("s", 15, 5), ("s", 7, 5),
    ("s", 24, 2), ("s", 17, 5), ("s", 14, 2), ("s", 18, 5), ("s", 25, 2), ("s", 20, 5), ("vec", 1),
    ("s", 19, 4), ("s", 21, 3), ("s", 27, 2), ("s", 22, 3), ("s", 29, 1), ("fout", 0), ("s", 23, 3),
    ("fout", 1), ("s", 24, 3), ("s", 26, 2), ("s", 28, 2), ("s", 14, 3), ("s", 21, 4), ("s", 10, 4),
    ("s", 25, 3), ("s", 9, 5), ("s", 22, 4), ("s", 19, 5), ("s", 29, 2), ("s", 23, 4), ("s", 27, 3),
    ("s", 24, 4), ("s", 26, 3), ("vec", 2), ("s", 14, 4), ("s", 28, 3), ("s", 10, 5), ("s", 21, 5),
    ("s", 25, 4), ("s", 22, 5), ("s", 29, 3), ("s", 23, 5), ("s", 27, 4), ("s", 24, 5), ("s", 26, 4),
    ("s", 14, 5), ("s", 28, 4), ("s", 25, 5), ("s", 29, 4), ("s", 27, 5), ("s", 26, 5), ("vec", 3),
    ("s", 28, 5), ("s", 29, 5),
)

HEAD_COLS, UNIT_COLS = 384, 1536
Q0, K0, V0, O0, U0, W0 = 0, 384, 768, 1152, 1536, 3072


def block_kernel(
    inner, items, length, tokens_hbm, cotangent_hbm, task_mask, group_ids, matrices_hbm, norm, column, *rest
):
    (out_hbm, input_grad_hbm, matrix_grad, vectors) = rest[:4]
    (full, grads) = rest[4:6]
    landings = (rest[6:11], rest[11:16])
    (act_one, act_one_t, act_two, act_two_t, cot_t, proj, grad_proj, heads, grad_heads) = rest[16:25]
    (caps, probs, residual, slope, hidden, grad_pre, grad_res, grad_low, ex_send, ex_recv) = rest[25:35]
    (vec_got, vec_z, g_send, g_recv, s_send, s_recv, es, er, vs, vr) = rest[35:45]
    (tokens, cotangent, matrices, out, input_grad, in_sem, out_sem) = rest[45:]
    loads = [
        pltpu.make_async_copy(source, target, in_sem.at[spot])
        for spot, (source, target) in enumerate(
            ((matrices_hbm, matrices), (tokens_hbm, tokens), (cotangent_hbm, cotangent))
        )
    ]
    for load in loads:
        load.start()
    place = Place(inner)
    gather = Gather(place, GATHER_UNITS, full, g_send, g_recv)
    scatter = Scatter(place, SCATTER_UNITS, grads, landings, matrix_grad, s_send, s_recv)

    def weight(start, width):
        return full[:, :, :, :, pl.ds(start, width)].reshape(D, width)

    def put_grad(start, width, value):
        grads[:, :, :, :, pl.ds(start, width)] = value.astype(BF16).reshape(grads.shape[:4] + (width,))

    def rows_of(item):
        return pl.ds(item * length, length)

    def store(which, item):
        part = rows_of(item)
        source, target = ((out, out_hbm), (input_grad, input_grad_hbm))[which]
        return pltpu.make_async_copy(source.at[part], target.at[part], out_sem.at[which, item])

    def add_vector(row, first, value):
        cols = pl.ds(first, value.shape[1])
        vectors[row : row + 1, cols] = vectors[row : row + 1, cols] + value

    def exchange(turn, item):
        part = rows_of(item)
        return remote(
            ex_send.at[turn % 2, part],
            ex_recv.at[turn % 2, part],
            es.at[turn, item],
            er.at[turn, item],
            place.sibling(),
        )

    def fill_part(turn, item, value):
        if turn >= 2:
            exchange(turn - 2, item).wait_send()
        ex_send[turn % 2, rows_of(item)] = value.astype(BF16)

    def both(turn, item):
        exchange(turn, item).wait_recv()
        part = rows_of(item)
        return ex_send[turn % 2, part].astype(F32) + ex_recv[turn % 2, part].astype(F32)

    def norm_one(item):
        part = rows_of(item)
        unit_x, _ = normalized(tokens[part].astype(F32))
        act_one[part] = (unit_x * norm[0:1] + norm[1:2]).astype(BF16)
        add_vector(5, 0, total_rows(cotangent[part].astype(F32)))

    def masks(_):
        key_index = lax.broadcasted_iota(jnp.int32, (length, length), 0)
        query_index = lax.broadcasted_iota(jnp.int32, (length, length), 1)
        same = key_index == query_index
        slots = task_mask.shape[1]
        slot_same = lax.broadcasted_iota(jnp.int32, (slots, slots), 0) == lax.broadcasted_iota(
            jnp.int32, (slots, slots), 1
        )
        for item in range(items):
            query_ids = group_ids[item : item + 1, :]
            key_ids = jnp.sum(jnp.where(same, query_ids, 0), axis=1, keepdims=True)
            filled = jnp.sum(jnp.where(slot_same, task_mask[item : item + 1, :], 0), axis=1, keepdims=True)
            live = jnp.concatenate([filled, jnp.ones((length - slots, 1), jnp.int32)], axis=0)
            odd_key = jnp.where((key_ids == 0) | (key_ids % 2 == 1), 1, 0)
            earlier = (odd_key == 1) & (key_ids <= query_ids)
            visible = (earlier | (key_ids == query_ids)) & (live == 1)
            caps[item] = jnp.where(visible | same, 3.0e38, NEGATIVE)

    def turned(which):
        source, target = ((act_one, act_one_t), (cotangent, cot_t), (act_two, act_two_t))[which]
        target[...] = source[...].T

    def project(item):
        part = rows_of(item)
        for start, scale, bias in ((Q0, HD**-0.5, 0), (K0, 1.0, None), (V0, 1.0, HEAD_COLS)):
            value = rows_dot(act_one[part], weight(start, HEAD_COLS))
            if bias is not None:
                value = value + column[pl.ds(bias, HEAD_COLS)].reshape(1, HEAD_COLS)
            value = value.astype(BF16)
            if scale != 1.0:
                value = value * jnp.asarray(scale, BF16)
            proj[part, start : start + HEAD_COLS] = value

    lane = lax.broadcasted_iota(jnp.int32, (length, 128), 1)
    first_half = lane < HD

    def lanes(start, pair):
        return pl.ds(start + pair * 128, 128)

    def attend(item, pair):
        part = rows_of(item)
        query, key, value = (proj[part, lanes(start, pair)] for start in (Q0, K0, V0))
        sides = []
        for side in range(2):
            own = first_half if side == 0 else ~first_half
            scores = dot_rt(jnp.where(own, key, jnp.zeros_like(key)), query)
            scores = jnp.minimum(scores, caps[item])
            weights = jnp.exp(scores - jnp.max(scores, 0, keepdims=True))
            prob = weights * (1.0 / jnp.sum(weights, 0, keepdims=True))
            probs[item, pair * 2 + side] = prob
            sides.append(dot_lt(prob.astype(BF16), value))
        heads[part, lanes(0, pair)] = jnp.where(first_half, sides[0], sides[1]).astype(BF16)

    def heads_out(item):
        fill_part(0, item, dot_rt(heads[rows_of(item)], weight(O0, HEAD_COLS)))
        exchange(0, item).start()

    def norm_two(item):
        part = rows_of(item)
        value = tokens[part].astype(F32) + both(0, item) + norm[4:5]
        residual[part] = value
        unit_x, _ = normalized(value)
        act_two[part] = (unit_x * norm[2:3] + norm[3:4]).astype(BF16)

    def up(index):
        start = index * COL_TILE
        cols = pl.ds(start, COL_TILE)
        unit = rows_dot(act_two[...], weight(U0 + start, COL_TILE))
        unit = unit + column[pl.ds(2 * HEAD_COLS + start, COL_TILE)].reshape(1, COL_TILE)
        square = unit * unit
        bent = jnp.tanh(unit * (GELU_SCALE + (GELU_SCALE * GELU_CUBIC) * square))
        half = 0.5 * (1.0 + bent)
        hidden[:, cols] = (unit * half).astype(BF16)
        slope[:, cols] = half + 0.5 * unit * (1.0 - bent * bent) * (
            GELU_SCALE + (3.0 * GELU_SCALE * GELU_CUBIC) * square
        )

    def down_grad(index):
        start = index * COL_TILE
        put_grad(W0 + start, COL_TILE, rows_dot(cot_t[...], hidden[:, pl.ds(start, COL_TILE)]))

    def pre_grad(index):
        start = index * COL_TILE
        cols = pl.ds(start, COL_TILE)
        value = rows_dot(cotangent[...], weight(W0 + start, COL_TILE))
        low = (value * slope[:, cols]).astype(BF16)
        grad_pre[:, cols] = low
        row, first = divmod(2 * HEAD_COLS + start, D)
        add_vector(6 + row, first, total_rows(low.astype(F32)))
        put_grad(U0 + start, COL_TILE, rows_dot(act_two_t[...], low))

    def units_back(item):
        fill_part(1, item, dot_rt(grad_pre[rows_of(item)], weight(U0, UNIT_COLS)))
        exchange(1, item).start()

    def norm_back(incoming, values, gain):
        unit_x, scale = normalized(values)
        pulled = incoming * gain
        inner_mean = jnp.mean(pulled, -1, keepdims=True)
        cross_mean = jnp.mean(pulled * unit_x, -1, keepdims=True)
        return scale * (pulled - inner_mean - unit_x * cross_mean), total_rows(incoming * unit_x), total_rows(incoming)

    def norm_two_back(item):
        part = rows_of(item)
        value, gain_sum, shift_sum = norm_back(both(1, item), residual[part], norm[2:3])
        value = cotangent[part].astype(F32) + value
        grad_res[part] = value
        grad_low[part] = value.astype(BF16)
        add_vector(2, 0, gain_sum)
        add_vector(3, 0, shift_sum)
        add_vector(4, 0, total_rows(value))

    def out_grad(_):
        put_grad(O0, HEAD_COLS, dot_lt(grad_low[...], heads[...]))

    def heads_back(item):
        part = rows_of(item)
        grad_heads[part] = rows_dot(grad_low[part], weight(O0, HEAD_COLS)).astype(BF16)

    def attend_back(item, pair):
        part = rows_of(item)
        query, key, value = (proj[part, lanes(start, pair)] for start in (Q0, K0, V0))
        grad = grad_heads[part, lanes(0, pair)]
        sides = []
        for side in range(2):
            own = first_half if side == 0 else ~first_half
            prob = probs[item, pair * 2 + side]
            grad_prob = dot_rt(jnp.where(own, value, jnp.zeros_like(value)), grad)
            inner_sum = jnp.sum(prob * grad_prob, 0, keepdims=True)
            low = (prob * (grad_prob - inner_sum)).astype(BF16)
            sides.append(
                (dot_lt(low, key) * (HD**-0.5), rows_dot(low, query), rows_dot(prob.astype(BF16), grad))
            )
        for start, left, right in zip((Q0, K0, V0), sides[0], sides[1]):
            low = jnp.where(first_half, left, right).astype(BF16)
            grad_proj[part, lanes(start, pair)] = low
            if start != K0:
                add_vector(6, (0 if start == Q0 else HEAD_COLS) + pair * 128, total_rows(low.astype(F32)))

    def proj_grad(index):
        cols = pl.ds(index * HEAD_COLS, HEAD_COLS)
        put_grad(index * HEAD_COLS, HEAD_COLS, rows_dot(act_one_t[...], grad_proj[:, cols]))

    def heads_in(item):
        fill_part(2, item, dot_rt(grad_proj[rows_of(item)], weight(Q0, 3 * HEAD_COLS)))
        exchange(2, item).start()

    def units_out(item):
        fill_part(3, item, dot_rt(hidden[rows_of(item)], weight(W0, UNIT_COLS)))

    def send_units(_):
        for item in range(items):
            exchange(3, item).start()

    def norm_one_back(item):
        part = rows_of(item)
        value, gain_sum, shift_sum = norm_back(both(2, item), tokens[part].astype(F32), norm[0:1])
        input_grad[part] = grad_res[part] + value
        store(1, item).start()
        add_vector(0, 0, gain_sum)
        add_vector(1, 0, shift_sum)

    def finish_out(item):
        part = rows_of(item)
        out[part] = (residual[part] + both(3, item) + norm[5:6]).astype(BF16)
        store(0, item).start()

    def vec_copy(stage, owner_z=None, step=0):
        if stage < 2:
            peer = (place.across_x(), place.across_y())[stage]
            return remote(vectors, vec_got.at[stage], vs.at[stage], vr.at[stage], peer)
        block = vec_z.at[owner_z]
        return remote(block, block, vs.at[1 + step], vr.at[1 + step], place.along_z(step))

    def small_sums(stage):
        if stage in (1, 2):
            vec_copy(stage - 1).wait()
            vectors[...] = vectors[...] + vec_got[stage - 1]
        if stage < 2:
            vec_copy(stage).start()
        elif stage == 2:
            vec_z[place.z] = vectors[...]
            for step in range(1, NZ):
                vec_copy(2, place.z, step).start()
        else:
            for step in range(1, NZ):
                vec_copy(2, (place.z - step) % NZ, step).wait_recv()
                vec_copy(2, place.z, step).wait_send()
            vectors[...] = (vec_z[0] + vec_z[1]) + (vec_z[2] + vec_z[3])

    pieces = {
        "ln1": norm_one,
        "caps": masks,
        "tr": turned,
        "qkv": project,
        "att": attend,
        "op0": heads_out,
        "ln2": norm_two,
        "up": up,
        "gd": down_grad,
        "pre": pre_grad,
        "da2": units_back,
        "ln2b": norm_two_back,
        "gout": out_grad,
        "do": heads_back,
        "attb": attend_back,
        "gp": proj_grad,
        "da1": heads_in,
        "op2": units_out,
        "op2s": send_units,
        "ln1b": norm_one_back,
        "fout": finish_out,
        "vec": small_sums,
    }

    vectors[...] = jnp.zeros_like(vectors)
    place.greet()
    for load in loads:
        load.wait()
    for kind, *what in PLAN:
        if kind == "g":
            unit, stage = what
            if stage == 0:
                cols = pl.ds(*GATHER_UNITS[unit][:2])
                full[place.z, place.y, place.x, :, cols] = matrices[:, cols].astype(BF16)
            else:
                gather.settle(unit, stage - 1)
            gather.begin(unit, stage)
        elif kind == "gf":
            gather.settle(what[0], 4)
        elif kind == "s":
            unit, stage = what
            if stage > 0:
                scatter.add(unit, stage - 1)
            if stage < 5:
                scatter.begin(unit, stage)
        else:
            pieces[kind](*what)
    for which in range(2):
        for item in range(items):
            store(which, item).wait()
    gather.drain()
    scatter.drain()
    for turn in (2, 3):
        for item in range(items):
            exchange(turn, item).wait_send()


def run_block(inner, tokens, cotangent, task_mask, group_ids, slab, norm_bias, column_bias):
    rows = tokens.shape[0]
    items, length = group_ids.shape
    slab_rows, cols = slab.shape
    heads = HEAD_COLS // HD
    gather_units, scatter_units = len(GATHER_UNITS), len(SCATTER_UNITS)
    dma = pltpu.SemaphoreType.DMA
    vmem = pltpu.VMEM
    in_vmem = pl.BlockSpec(memory_space=pltpu.VMEM)
    anywhere = pl.BlockSpec(memory_space=pl.ANY)
    return pl.pallas_call(
        functools.partial(block_kernel, inner, items, length),
        out_shape=(
            jax.ShapeDtypeStruct((rows, D), BF16),
            jax.ShapeDtypeStruct((rows, D), F32),
            jax.ShapeDtypeStruct((slab_rows, cols), F32),
            jax.ShapeDtypeStruct((16, D), F32),
        ),
        in_specs=[anywhere, anywhere, in_vmem, in_vmem, anywhere, in_vmem, in_vmem],
        out_specs=(anywhere, anywhere, in_vmem, in_vmem),
        scratch_shapes=[
            vmem((NZ, NY, NX, slab_rows, cols), BF16),
            vmem((NZ, NY, NX, slab_rows, cols), BF16),
            vmem((NZ, 2, slab_rows, LATE_COLS), BF16),
            vmem((NZ, slab_rows, LATE_COLS), BF16),
            vmem((2, slab_rows, LATE_COLS), BF16),
            vmem((2, slab_rows, LATE_COLS), BF16),
            vmem((slab_rows, LATE_COLS), BF16),
            vmem((2, NY, NX, slab_rows, EARLY_COLS), BF16),
            vmem((2, NY, NX, slab_rows, EARLY_COLS), BF16),
            vmem((NY, NX, slab_rows, EARLY_COLS), BF16),
            vmem((2, slab_rows, EARLY_COLS), BF16),
            vmem((slab_rows, EARLY_COLS), BF16),
            vmem((rows, D), BF16),
            vmem((D, rows), BF16),
            vmem((rows, D), BF16),
            vmem((D, rows), BF16),
            vmem((D, rows), BF16),
            vmem((rows, 3 * HEAD_COLS), BF16),
            vmem((rows, 3 * HEAD_COLS), BF16),
            vmem((rows, HEAD_COLS), BF16),
            vmem((rows, HEAD_COLS), BF16),
            vmem((items, length, length), F32),
            vmem((items, heads, length, length), F32),
            vmem((rows, D), F32),
            vmem((rows, UNIT_COLS), F32),
            vmem((rows, UNIT_COLS), BF16),
            vmem((rows, UNIT_COLS), BF16),
            vmem((rows, D), F32),
            vmem((rows, D), BF16),
            vmem((2, rows, D), BF16),
            vmem((2, rows, D), BF16),
            vmem((2, 16, D), F32),
            vmem((NZ, 16, D), F32),
            dma((gather_units, 5)),
            dma((gather_units, 5)),
            dma((scatter_units, 5)),
            dma((scatter_units, 5)),
            dma((4, items)),
            dma((4, items)),
            dma((2 + NZ - 1,)),
            dma((2 + NZ - 1,)),
            vmem((rows, D), BF16),
            vmem((rows, D), BF16),
            vmem((slab_rows, cols), F32),
            vmem((rows, D), BF16),
            vmem((rows, D), F32),
            dma((3,)),
            dma((2, items)),
        ],
        compiler_params=pltpu.CompilerParams(
            collective_id=0, has_side_effects=True, vmem_limit_bytes=60 << 20
        ),
    )(tokens, cotangent, task_mask, group_ids, slab, norm_bias, column_bias)


def adam_update(weight_now, gradient, first_now, second_now, step_rate, weight_decay):
    first_new = BETA_FIRST * first_now + (1.0 - BETA_FIRST) * gradient
    second_new = BETA_SECOND * second_now + (1.0 - BETA_SECOND) * gradient * gradient
    first_fixed = first_new / (1.0 - BETA_FIRST**STEP)
    second_fixed = second_new / (1.0 - BETA_SECOND**STEP)
    weight_new = weight_now - step_rate * (
        first_fixed / (jnp.sqrt(second_fixed) + EPS_ADAM) + weight_decay * weight_now
    )
    return (weight_new, first_new, second_new)


FINISH_STEPS = 4


def finish_kernel(*refs):
    (out_in, dx_in, grad, vectors, mats, mat_m, mat_n, mat_a) = refs[:8]
    (norm, norm_m, norm_n, norm_a, col, col_m, col_n, col_a) = refs[8:16]
    results = refs[16:]
    results[0][...] = out_in[...]
    results[1][...] = dx_in[...]

    def update(targets, gradient, old, decay, rate, average):
        new, first, second = adam_update(*old[:1], gradient, *old[1:], rate, decay)
        for target, value in zip(
            targets, (gradient, new, first, second, AVERAGE_KEEP * average + (1.0 - AVERAGE_KEEP) * new)
        ):
            target(value)

    def whole(ref):
        def store(value):
            ref[...] = value

        return store

    update(
        [whole(ref) for ref in results[2:7]],
        grad[...],
        (mats[...], mat_m[...], mat_n[...]),
        DECAY_MATRIX,
        RATE_MATRIX,
        mat_a[...],
    )

    @pl.when(pl.program_id(0) == 0)
    def _():
        update(
            [whole(ref) for ref in results[7:12]],
            vectors[0:6, :],
            (norm[...], norm_m[...], norm_n[...]),
            0.0,
            RATE_VECTOR,
            norm_a[...],
        )
        for row in range(3):
            part = pl.ds(row * D, D)

            def piece(ref, part=part):
                def store(value):
                    ref[part] = value.reshape(D)

                return store

            update(
                [piece(ref) for ref in results[12:17]],
                vectors[6 + row : 7 + row, :],
                tuple(ref[part].reshape(1, D) for ref in (col, col_m, col_n)),
                0.0,
                RATE_VECTOR,
                col_a[part].reshape(1, D),
            )


def finish(output, input_grad, matrix_grad, vectors, matrix_set, norm_set, column_set):
    rows = output.shape[0] // FINISH_STEPS
    slab_rows, cols = matrix_grad.shape
    token_block = pl.BlockSpec((rows, D), lambda step: (step, 0))
    matrix_block = pl.BlockSpec((slab_rows, cols // FINISH_STEPS), lambda step: (0, step))

    def small(array):
        return pl.BlockSpec(array.shape, lambda step: (0,) * array.ndim)

    shape = jax.ShapeDtypeStruct
    norm_bias, column_bias = norm_set[0], column_set[0]
    return pl.pallas_call(
        finish_kernel,
        grid=(FINISH_STEPS,),
        out_shape=[shape(output.shape, output.dtype), shape(input_grad.shape, F32)]
        + [shape(matrix_grad.shape, F32)] * 5
        + [shape(norm_bias.shape, F32)] * 5
        + [shape(column_bias.shape, F32)] * 5,
        in_specs=[token_block, token_block, matrix_block, small(vectors)]
        + [matrix_block] * 4
        + [small(norm_bias)] * 4
        + [small(column_bias)] * 4,
        out_specs=[token_block, token_block]
        + [matrix_block] * 5
        + [small(norm_bias)] * 5
        + [small(column_bias)] * 5,
        compiler_params=pltpu.CompilerParams(vmem_limit_bytes=32 << 20),
    )(output, input_grad, matrix_grad, vectors, *matrix_set, *norm_set, *column_set)


def local(
    tokens,
    cotangent,
    task_mask,
    group_ids,
    matrices,
    matrix_first,
    matrix_second,
    matrix_average,
    norm_bias,
    norm_first,
    norm_second,
    norm_average,
    column_bias,
    column_first,
    column_second,
    column_average,
):
    inner = lax.axis_size("dp") // OUTER
    groups = [[outer * inner + i for i in range(inner)] for outer in range(OUTER)]
    slab = matrices
    if inner > 1:
        slab = lax.all_gather(
            matrices.astype(BF16), "dp", axis=0, tiled=True, axis_index_groups=groups
        ).astype(F32)
    output, input_grad, matrix_grad, vectors = run_block(
        inner, tokens, cotangent, task_mask, group_ids, slab, norm_bias, column_bias
    )
    if inner > 1:
        matrix_grad = lax.psum_scatter(
            matrix_grad, "dp", scatter_dimension=0, tiled=True, axis_index_groups=groups
        )
        vectors = jnp.sum(lax.all_gather(vectors, "dp", axis=0, axis_index_groups=groups), 0)
    return tuple(
        finish(
            output,
            input_grad,
            matrix_grad,
            vectors,
            (matrices, matrix_first, matrix_second, matrix_average),
            (norm_bias, norm_first, norm_second, norm_average),
            (column_bias, column_first, column_second, column_average),
        )
    )


def solution(mesh):
    placed = (
        P("dp", None),
        P("dp", None),
        P("dp", None),
        P("dp", None),
        P("dp", "mp"),
        P("dp", "mp"),
        P("dp", "mp"),
        P("dp", "mp"),
        P(),
        P(),
        P(),
        P(),
        P("mp"),
        P("mp"),
        P("mp"),
        P("mp"),
    )
    return jax.shard_map(
        local,
        mesh=mesh,
        in_specs=placed,
        out_specs=(
            P("dp", None),
            P("dp", None),
            P("dp", "mp"),
            P("dp", "mp"),
            P("dp", "mp"),
            P("dp", "mp"),
            P("dp", "mp"),
            P(),
            P(),
            P(),
            P(),
            P(),
            P("mp"),
            P("mp"),
            P("mp"),
            P("mp"),
            P("mp"),
        ),
        check_vma=False,
    )
```

```python
import functools

import jax
import jax.numpy as jnp
from jax import lax
from jax.experimental import pallas as pl
from jax.experimental.pallas import tpu as pltpu
from jax.sharding import PartitionSpec as P

MESH = pl.DeviceIdType.MESH

D = 768
HEADS = 12
HD = 64
FF = 3072
STEP = 10


NORM_EPSILON = 1e-06
NEGATIVE = -1e30
GELU_SCALE = 0.7978845608028654
GELU_CUBIC = 0.044715
BETA_FIRST = 0.9
BETA_SECOND = 0.999
EPS_ADAM = 1e-08
RATE_MATRIX = 0.1
RATE_VECTOR = 0.3
DECAY_MATRIX = 0.1
AVERAGE_KEEP = 0.7


NZ, NY, NX = 4, 2, 2
OUTER = NZ * NY * NX
COL_TILE = 256
F32, BF16 = jnp.float32, jnp.bfloat16


class Place:
    def __init__(self, inner):
        index = lax.axis_index("dp")
        outer = index // inner
        self.inner = inner
        self.rest = index % inner
        self.core = lax.axis_index("mp")
        self.x = outer % NX
        self.y = (outer // NX) % NY
        self.z = outer // (NX * NY)
        self.partner_z = self.z + 1 - 2 * (self.z % 2)
        self.near_pair = pl.ds(2 * (self.z // 2), 2)
        self.far_pair = pl.ds(2 - 2 * (self.z // 2), 2)

    def device(self, z, y, x):
        return (((z * NY + y) * NX + x) * self.inner + self.rest, self.core)

    def along_z(self, step):
        return self.device((self.z + step) % NZ, self.y, self.x)

    def across_y(self):
        return self.device(self.z, 1 - self.y, self.x)

    def across_x(self):
        return self.device(self.z, self.y, 1 - self.x)

    def sibling(self):
        return (self.device(self.z, self.y, self.x)[0], 1 - self.core)

    def greet(self):
        barrier = pltpu.get_barrier_semaphore()
        peers = [self.along_z(step) for step in range(1, NZ)]
        peers += [self.across_y(), self.across_x(), self.sibling()]
        for peer in peers:
            pl.semaphore_signal(barrier, inc=1, device_id=peer, device_id_type=MESH)
        pl.semaphore_wait(barrier, len(peers))


def remote(src, dst, send_sem, recv_sem, peer):
    return pltpu.make_async_remote_copy(
        src_ref=src,
        dst_ref=dst,
        send_sem=send_sem,
        recv_sem=recv_sem,
        device_id=peer,
        device_id_type=MESH,
    )


class Mover:
    line = "abc"

    def __init__(self, place, units, full, send_sem, recv_sem):
        self.place, self.units, self.full = place, units, full
        self.send_sem, self.recv_sem = send_sem, recv_sem
        self.inner_z = (place.z == 1) | (place.z == 2)
        self.outer_z = (place.z == 0) | (place.z == 3)

    def stages(self, unit):
        found = []
        route = self.units[unit][2]
        for spot, axis in enumerate(route):
            for name in self.line if axis == "z" else axis:
                found.append((name, route[:spot], route[spot + 1 :]))
        return found

    def peer(self, name):
        p = self.place
        if name == "x":
            return p.across_x()
        if name == "y":
            return p.across_y()
        return p.device(p.partner_z if name in "ac" else NZ - 1 - p.z, p.y, p.x)

    def block(self, unit, whole, z, y, x):
        start, width, _ = self.units[unit]
        index = [slice(None) if name in whole else here for name, here in (("z", z), ("y", y), ("x", x))]
        return tuple(index) + (slice(None), pl.ds(start, width))

    def copy(self, unit, stage, src, dst, name):
        return remote(src, dst, self.send_sem.at[unit, stage], self.recv_sem.at[unit, stage], self.peer(name))

    def begin(self, unit, stage):
        name = self.stages(unit)[stage][0]
        self.guarded(self.sender(name), lambda: self.leaving(unit, stage).start())

    def settle(self, unit, stage):
        name = self.stages(unit)[stage][0]
        self.guarded(self.receiver(name), lambda: self.arriving(unit, stage).wait_recv())

    @staticmethod
    def guarded(condition, action):
        if condition is None:
            action()
        else:
            pl.when(condition)(action)

    def drain(self):
        for unit in range(len(self.units)):
            for stage, (name, _, _) in enumerate(self.stages(unit)):
                self.guarded(self.sender(name), lambda: self.leaving(unit, stage).wait_send())


class Gather(Mover):
    def sender(self, name):
        return self.inner_z if name in "bc" else None

    def receiver(self, name):
        return {"b": self.inner_z, "c": self.outer_z}.get(name)

    def leaving(self, unit, stage):
        p = self.place
        name, before, _ = self.stages(unit)[stage]
        z = {"b": p.near_pair, "c": p.far_pair}.get(name, p.z)
        mine = self.full.at[self.block(unit, before, z, p.y, p.x)]
        return self.copy(unit, stage, mine, mine, name)

    def arriving(self, unit, stage):
        p = self.place
        name, before, _ = self.stages(unit)[stage]
        z = {"a": p.partner_z, "b": p.far_pair, "c": p.far_pair}.get(name, p.z)
        y = 1 - p.y if name == "y" else p.y
        x = 1 - p.x if name == "x" else p.x
        theirs = self.full.at[self.block(unit, before, z, y, x)]
        return self.copy(unit, stage, theirs, theirs, name)


class Scatter(Mover):
    line = "cba"

    def __init__(self, place, units, full, landings, result, send_sem, recv_sem):
        super().__init__(place, units, full, send_sem, recv_sem)
        self.landings, self.result = landings, result

    def sender(self, name):
        return {"b": self.inner_z, "c": self.outer_z}.get(name)

    def receiver(self, name):
        return self.inner_z if name in "bc" else None

    def landing(self, unit, stage):
        _, width, route = self.units[unit]
        got = self.landings[int(route[0] == "z")][stage]
        lead = (slice(None),) * (len(got.shape) - 1)
        return got.at[lead + (pl.ds(LANDING[unit], width),)]

    def leaving(self, unit, stage):
        p = self.place
        name, _, after = self.stages(unit)[stage]
        z = {"a": p.partner_z, "b": p.far_pair, "c": p.far_pair}.get(name, p.z)
        y = 1 - p.y if name == "y" else p.y
        x = 1 - p.x if name == "x" else p.x
        away = self.full.at[self.block(unit, after, z, y, x)]
        return self.copy(unit, stage, away, self.landing(unit, stage), name)

    arriving = leaving

    def add(self, unit, stage):
        p = self.place
        steps = self.stages(unit)
        name, _, after = steps[stage]

        def action():
            self.arriving(unit, stage).wait_recv()
            z = {"b": p.near_pair, "c": p.far_pair}.get(name, p.z)
            part = self.block(unit, after, z, p.y, p.x)
            total = self.full[part].astype(F32) + self.landing(unit, stage)[...].astype(F32)
            if stage + 1 == len(steps):
                start, width, _ = self.units[unit]
                self.result[:, pl.ds(start, width)] = total
            else:
                self.full[part] = total.astype(BF16)

        self.guarded(self.receiver(name), action)


def rows_dot(left, right):
    return jnp.dot(left, right, preferred_element_type=F32)


def dot_rt(left, right):
    return lax.dot_general(left, right, (((1,), (1,)), ((), ())), preferred_element_type=F32)


def dot_lt(left, right):
    return lax.dot_general(left, right, (((0,), (0,)), ((), ())), preferred_element_type=F32)


def normalized(values):
    center = values - jnp.mean(values, -1, keepdims=True)
    spread = jnp.mean(center * center, -1, keepdims=True)
    scale = lax.rsqrt(spread + NORM_EPSILON)
    return center * scale, scale


def total_rows(values):
    return jnp.sum(values, 0, keepdims=True)


GATHER_UNITS = (
    (0, 128, "zxy"),
    (128, 128, "zxy"),
    (256, 128, "zyx"),
    (384, 128, "zxy"),
    (512, 128, "zyx"),
    (640, 128, "zxy"),
    (768, 128, "zxy"),
    (896, 128, "zyx"),
    (1024, 256, "zyx"),
    (1280, 128, "yxz"),
    (1408, 384, "zyx"),
    (1792, 256, "zxy"),
    (2048, 256, "zyx"),
    (2304, 256, "zxy"),
    (2560, 256, "zyx"),
    (2816, 128, "zyx"),
    (2944, 128, "zyx"),
    (3072, 128, "zxy"),
    (3200, 256, "yxz"),
    (3456, 128, "zyx"),
    (3584, 128, "xyz"),
    (3712, 128, "zyx"),
    (3840, 128, "yxz"),
    (3968, 256, "xyz"),
    (4224, 256, "yxz"),
    (4480, 128, "xyz"),
)
SCATTER_UNITS = (
    (3072, 256, "zxy"),
    (3328, 128, "zxy"),
    (3456, 128, "yxz"),
    (3584, 256, "yxz"),
    (3840, 128, "yxz"),
    (3968, 128, "zxy"),
    (4096, 128, "yxz"),
    (4224, 128, "zxy"),
    (4352, 256, "yxz"),
    (1536, 256, "xyz"),
    (1792, 256, "yxz"),
    (2048, 256, "zxy"),
    (2304, 256, "xyz"),
    (2560, 256, "zyx"),
    (2816, 256, "xyz"),
    (1152, 384, "yxz"),
    (0, 128, "xyz"),
    (128, 256, "yxz"),
    (384, 128, "yxz"),
    (512, 128, "xyz"),
    (640, 128, "yxz"),
    (768, 128, "xyz"),
    (896, 128, "zyx"),
    (1024, 128, "xyz"),
)
LANDING = (
    0, 256, 0, 128, 384, 384, 512, 512, 640, 896, 1152, 640,
    1408, 896, 1664, 1920, 2304, 2432, 2688, 2816, 2944, 3072, 1152, 3200,
)
LATE_COLS, EARLY_COLS = 3328, 1280
PLAN = (
    ("g", 0, 0), ("g", 1, 0), ("g", 2, 0), ("g", 3, 0), ("g", 4, 0), ("g", 5, 0), ("g", 6, 0), ("g", 7, 0),
    ("g", 8, 0), ("g", 10, 0), ("g", 11, 0), ("g", 12, 0), ("g", 13, 0), ("g", 14, 0), ("g", 15, 0),
    ("g", 16, 0), ("g", 17, 0), ("g", 19, 0), ("g", 21, 0), ("g", 9, 0), ("g", 18, 0), ("g", 0, 1),
    ("g", 20, 0), ("g", 1, 1), ("g", 22, 0), ("g", 2, 1), ("g", 3, 1), ("g", 23, 0), ("g", 4, 1), ("g", 24, 0),
    ("g", 5, 1), ("g", 25, 0), ("g", 6, 1), ("g", 7, 1), ("ln1", 0), ("ln1", 1), ("caps", 0), ("g", 8, 1),
    ("tr", 0), ("g", 9, 1), ("g", 10, 1), ("tr", 1), ("g", 0, 2), ("g", 11, 1), ("g", 18, 1), ("g", 1, 2),
    ("g", 12, 1), ("g", 20, 1), ("g", 22, 1), ("g", 2, 2), ("g", 13, 1), ("g", 23, 1), ("g", 3, 2),
    ("g", 14, 1), ("g", 24, 1), ("g", 15, 1), ("g", 4, 2), ("g", 16, 1), ("g", 25, 1), ("g", 17, 1),
    ("g", 5, 2), ("g", 19, 1), ("g", 21, 1), ("g", 6, 2), ("g", 0, 3), ("g", 7, 2), ("g", 1, 3), ("g", 9, 2),
    ("g", 2, 3), ("g", 8, 2), ("g", 3, 3), ("g", 4, 3), ("g", 5, 3), ("g", 10, 2), ("g", 6, 3), ("g", 7, 3),
    ("g", 11, 2), ("g", 0, 4), ("g", 9, 3), ("g", 12, 2), ("g", 1, 4), ("g", 2, 4), ("g", 8, 3), ("g", 13, 2),
    ("g", 3, 4), ("g", 4, 4), ("g", 14, 2), ("g", 5, 4), ("g", 10, 3), ("g", 15, 2), ("g", 7, 4), ("g", 16, 2),
    ("g", 6, 4), ("g", 11, 3), ("g", 17, 2), ("g", 19, 2), ("g", 12, 3), ("g", 21, 2), ("g", 13, 3),
    ("g", 18, 2), ("g", 14, 3), ("g", 9, 4), ("g", 15, 3), ("g", 16, 3), ("g", 17, 3), ("g", 19, 3),
    ("g", 8, 4), ("g", 21, 3), ("g", 20, 2), ("g", 18, 3), ("g", 22, 2), ("g", 11, 4), ("g", 23, 2),
    ("g", 13, 4), ("g", 20, 3), ("g", 24, 2), ("g", 17, 4), ("g", 22, 3), ("g", 10, 4), ("g", 25, 2),
    ("g", 23, 3), ("g", 18, 4), ("gf", 0), ("gf", 1), ("gf", 2), ("gf", 3), ("gf", 4), ("gf", 5), ("gf", 6),
    ("gf", 7), ("gf", 8), ("qkv", 0), ("qkv", 1), ("att", 0, 0), ("g", 24, 3), ("att", 0, 1), ("g", 12, 4),
    ("g", 20, 4), ("g", 25, 3), ("att", 0, 2), ("att", 1, 0), ("g", 14, 4), ("g", 22, 4), ("att", 1, 1),
    ("att", 1, 2), ("g", 15, 4), ("g", 16, 4), ("gf", 9), ("gf", 10), ("op0", 0), ("g", 19, 4), ("op0", 1),
    ("g", 23, 4), ("g", 21, 4), ("ln2", 0), ("ln2", 1), ("g", 24, 4), ("tr", 2), ("up", 0), ("gf", 11),
    ("up", 1), ("gf", 12), ("up", 2), ("g", 25, 4), ("gf", 14), ("up", 4), ("gd", 0), ("s", 0, 0), ("gd", 1),
    ("s", 2, 0), ("gf", 13), ("up", 3), ("gd", 2), ("s", 3, 0), ("gd", 3), ("gd", 4), ("gf", 17), ("gf", 18),
    ("pre", 0), ("s", 1, 0), ("s", 4, 0), ("s", 9, 0), ("gf", 15), ("gf", 16), ("up", 5), ("gd", 5), ("gf", 22),
    ("gf", 23), ("pre", 3), ("s", 5, 0), ("s", 6, 0), ("s", 12, 0), ("gf", 19), ("pre", 1), ("s", 2, 1),
    ("gf", 24), ("pre", 4), ("gf", 25), ("pre", 5), ("s", 7, 0), ("s", 8, 0), ("gf", 20), ("gf", 21),
    ("pre", 2), ("da2", 0), ("da2", 1), ("s", 11, 0), ("s", 0, 1), ("s", 3, 1), ("s", 10, 0), ("s", 9, 1),
    ("s", 1, 1), ("s", 4, 1), ("s", 14, 0), ("s", 13, 0), ("ln2b", 0), ("s", 5, 1), ("s", 6, 1), ("ln2b", 1),
    ("s", 7, 1), ("s", 12, 1), ("gout", 0), ("s", 0, 2), ("s", 2, 2), ("do", 0), ("do", 1), ("s", 8, 1),
    ("attb", 0, 0), ("s", 1, 2), ("s", 3, 2), ("s", 15, 0), ("attb", 0, 1), ("s", 4, 2), ("s", 11, 1),
    ("s", 5, 2), ("attb", 0, 2), ("s", 10, 1), ("attb", 1, 0), ("s", 7, 2), ("attb", 1, 1), ("s", 9, 2),
    ("s", 13, 1), ("s", 6, 2), ("s", 14, 1), ("attb", 1, 2), ("s", 0, 3), ("s", 2, 3), ("s", 8, 2),
    ("s", 12, 2), ("s", 1, 3), ("gp", 0), ("s", 11, 2), ("s", 3, 3), ("s", 16, 0), ("s", 4, 3), ("s", 10, 2),
    ("s", 17, 0), ("gp", 1), ("s", 5, 3), ("s", 19, 0), ("gp", 2), ("s", 0, 4), ("s", 1, 4), ("s", 7, 3),
    ("s", 21, 0), ("s", 22, 0), ("da1", 0), ("s", 9, 3), ("s", 13, 2), ("s", 2, 4), ("s", 6, 3), ("s", 15, 1),
    ("s", 3, 4), ("s", 8, 3), ("s", 4, 4), ("s", 5, 4), ("s", 14, 2), ("s", 12, 3), ("s", 16, 1), ("s", 18, 0),
    ("da1", 1), ("s", 23, 0), ("s", 20, 0), ("op2", 0), ("s", 9, 4), ("s", 11, 3), ("s", 6, 4), ("s", 7, 4),
    ("s", 19, 1), ("op2", 1), ("s", 8, 4), ("s", 10, 3), ("s", 17, 1), ("s", 0, 5), ("s", 12, 4), ("s", 1, 5),
    ("s", 21, 1), ("s", 5, 5), ("ln1b", 0), ("s", 22, 1), ("s", 16, 2), ("ln1b", 1), ("op2s", 0), ("s", 13, 3),
    ("s", 2, 5), ("s", 15, 2), ("s", 10, 4), ("s", 3, 5), ("s", 18, 1), ("s", 4, 5), ("vec", 0), ("s", 14, 3),
    ("s", 23, 1), ("s", 9, 5), ("s", 20, 1), ("s", 6, 5), ("s", 7, 5), ("s", 8, 5), ("s", 11, 4), ("s", 22, 2),
    ("s", 12, 5), ("s", 19, 2), ("s", 16, 3), ("s", 21, 2), ("s", 17, 2), ("s", 15, 3), ("s", 13, 4),
    ("s", 14, 4), ("s", 10, 5), ("s", 18, 2), ("vec", 1), ("s", 23, 2), ("fout", 0), ("s", 11, 5), ("s", 16, 4),
    ("s", 22, 3), ("s", 19, 3), ("s", 20, 2), ("fout", 1), ("s", 21, 3), ("s", 13, 5), ("s", 17, 3),
    ("s", 14, 5), ("s", 15, 4), ("s", 18, 3), ("s", 23, 3), ("s", 22, 4), ("s", 16, 5), ("s", 19, 4),
    ("vec", 2), ("s", 20, 3), ("s", 21, 4), ("s", 17, 4), ("s", 15, 5), ("s", 18, 4), ("s", 22, 5),
    ("s", 23, 4), ("s", 19, 5), ("s", 21, 5), ("s", 20, 4), ("vec", 3), ("s", 17, 5), ("s", 18, 5),
    ("s", 23, 5), ("s", 20, 5),
)

HEAD_COLS, UNIT_COLS = 384, 1536
Q0, K0, V0, O0, U0, W0 = 0, 384, 768, 1152, 1536, 3072


def block_kernel(
    inner, items, length, tokens_hbm, cotangent_hbm, task_mask, group_ids, matrices_hbm, norm, column, *rest
):
    (out_hbm, input_grad_hbm, matrix_grad, vectors) = rest[:4]
    (full, grads) = rest[4:6]
    landings = (rest[6:11], rest[11:16])
    (act_one, act_one_t, act_two, act_two_t, cot_t, proj, grad_proj, heads, grad_heads) = rest[16:25]
    (caps, probs, residual, slope, hidden, grad_pre, grad_res, grad_low, ex_send, ex_recv) = rest[25:35]
    (vec_got, vec_z, g_send, g_recv, s_send, s_recv, es, er, vs, vr) = rest[35:45]
    (tokens, cotangent, matrices, out, input_grad, in_sem, out_sem) = rest[45:]
    loads = [
        pltpu.make_async_copy(source, target, in_sem.at[spot])
        for spot, (source, target) in enumerate(
            ((matrices_hbm, matrices), (tokens_hbm, tokens), (cotangent_hbm, cotangent))
        )
    ]
    for load in loads:
        load.start()
    place = Place(inner)
    gather = Gather(place, GATHER_UNITS, full, g_send, g_recv)
    scatter = Scatter(place, SCATTER_UNITS, grads, landings, matrix_grad, s_send, s_recv)

    def weight(start, width):
        return full[:, :, :, :, pl.ds(start, width)].reshape(D, width)

    def put_grad(start, width, value):
        grads[:, :, :, :, pl.ds(start, width)] = value.astype(BF16).reshape(grads.shape[:4] + (width,))

    def rows_of(item):
        return pl.ds(item * length, length)

    def store(which, item):
        part = rows_of(item)
        source, target = ((out, out_hbm), (input_grad, input_grad_hbm))[which]
        return pltpu.make_async_copy(source.at[part], target.at[part], out_sem.at[which, item])

    def add_vector(row, first, value):
        cols = pl.ds(first, value.shape[1])
        vectors[row : row + 1, cols] = vectors[row : row + 1, cols] + value

    def exchange(turn, item):
        part = rows_of(item)
        return remote(
            ex_send.at[turn % 2, part],
            ex_recv.at[turn % 2, part],
            es.at[turn, item],
            er.at[turn, item],
            place.sibling(),
        )

    def fill_part(turn, item, value):
        if turn >= 2:
            exchange(turn - 2, item).wait_send()
        ex_send[turn % 2, rows_of(item)] = value.astype(BF16)

    def both(turn, item):
        exchange(turn, item).wait_recv()
        part = rows_of(item)
        return ex_send[turn % 2, part].astype(F32) + ex_recv[turn % 2, part].astype(F32)

    def norm_one(item):
        part = rows_of(item)
        unit_x, _ = normalized(tokens[part].astype(F32))
        act_one[part] = (unit_x * norm[0:1] + norm[1:2]).astype(BF16)
        add_vector(5, 0, total_rows(cotangent[part].astype(F32)))

    def masks(_):
        key_index = lax.broadcasted_iota(jnp.int32, (length, length), 0)
        query_index = lax.broadcasted_iota(jnp.int32, (length, length), 1)
        same = key_index == query_index
        slots = task_mask.shape[1]
        slot_same = lax.broadcasted_iota(jnp.int32, (slots, slots), 0) == lax.broadcasted_iota(
            jnp.int32, (slots, slots), 1
        )
        for item in range(items):
            query_ids = group_ids[item : item + 1, :]
            key_ids = jnp.sum(jnp.where(same, query_ids, 0), axis=1, keepdims=True)
            filled = jnp.sum(jnp.where(slot_same, task_mask[item : item + 1, :], 0), axis=1, keepdims=True)
            live = jnp.concatenate([filled, jnp.ones((length - slots, 1), jnp.int32)], axis=0)
            odd_key = jnp.where((key_ids == 0) | (key_ids % 2 == 1), 1, 0)
            earlier = (odd_key == 1) & (key_ids <= query_ids)
            visible = (earlier | (key_ids == query_ids)) & (live == 1)
            caps[item] = jnp.where(visible | same, 3.0e38, NEGATIVE)

    def turned(which):
        source, target = ((act_one, act_one_t), (cotangent, cot_t), (act_two, act_two_t))[which]
        target[...] = source[...].T

    def project(item):
        part = rows_of(item)
        for start, scale, bias in ((Q0, HD**-0.5, 0), (K0, 1.0, None), (V0, 1.0, HEAD_COLS)):
            value = rows_dot(act_one[part], weight(start, HEAD_COLS))
            if bias is not None:
                value = value + column[pl.ds(bias, HEAD_COLS)].reshape(1, HEAD_COLS)
            value = value.astype(BF16)
            if scale != 1.0:
                value = value * jnp.asarray(scale, BF16)
            proj[part, start : start + HEAD_COLS] = value

    lane = lax.broadcasted_iota(jnp.int32, (length, 128), 1)
    first_half = lane < HD

    def lanes(start, pair):
        return pl.ds(start + pair * 128, 128)

    def attend(item, pair):
        part = rows_of(item)
        query, key, value = (proj[part, lanes(start, pair)] for start in (Q0, K0, V0))
        sides = []
        for side in range(2):
            own = first_half if side == 0 else ~first_half
            scores = dot_rt(jnp.where(own, key, jnp.zeros_like(key)), query)
            scores = jnp.minimum(scores, caps[item])
            weights = jnp.exp(scores - jnp.max(scores, 0, keepdims=True))
            prob = weights * (1.0 / jnp.sum(weights, 0, keepdims=True))
            probs[item, pair * 2 + side] = prob
            sides.append(dot_lt(prob.astype(BF16), value))
        heads[part, lanes(0, pair)] = jnp.where(first_half, sides[0], sides[1]).astype(BF16)

    def heads_out(item):
        fill_part(0, item, dot_rt(heads[rows_of(item)], weight(O0, HEAD_COLS)))
        exchange(0, item).start()

    def norm_two(item):
        part = rows_of(item)
        value = tokens[part].astype(F32) + both(0, item) + norm[4:5]
        residual[part] = value
        unit_x, _ = normalized(value)
        act_two[part] = (unit_x * norm[2:3] + norm[3:4]).astype(BF16)

    def up(index):
        start = index * COL_TILE
        cols = pl.ds(start, COL_TILE)
        unit = rows_dot(act_two[...], weight(U0 + start, COL_TILE))
        unit = unit + column[pl.ds(2 * HEAD_COLS + start, COL_TILE)].reshape(1, COL_TILE)
        square = unit * unit
        bent = jnp.tanh(unit * (GELU_SCALE + (GELU_SCALE * GELU_CUBIC) * square))
        half = 0.5 * (1.0 + bent)
        hidden[:, cols] = (unit * half).astype(BF16)
        slope[:, cols] = half + 0.5 * unit * (1.0 - bent * bent) * (
            GELU_SCALE + (3.0 * GELU_SCALE * GELU_CUBIC) * square
        )

    def down_grad(index):
        start = index * COL_TILE
        put_grad(W0 + start, COL_TILE, rows_dot(cot_t[...], hidden[:, pl.ds(start, COL_TILE)]))

    def pre_grad(index):
        start = index * COL_TILE
        cols = pl.ds(start, COL_TILE)
        value = rows_dot(cotangent[...], weight(W0 + start, COL_TILE))
        low = (value * slope[:, cols]).astype(BF16)
        grad_pre[:, cols] = low
        row, first = divmod(2 * HEAD_COLS + start, D)
        add_vector(6 + row, first, total_rows(low.astype(F32)))
        put_grad(U0 + start, COL_TILE, rows_dot(act_two_t[...], low))

    def units_back(item):
        fill_part(1, item, dot_rt(grad_pre[rows_of(item)], weight(U0, UNIT_COLS)))
        exchange(1, item).start()

    def norm_back(incoming, values, gain):
        unit_x, scale = normalized(values)
        pulled = incoming * gain
        inner_mean = jnp.mean(pulled, -1, keepdims=True)
        cross_mean = jnp.mean(pulled * unit_x, -1, keepdims=True)
        return scale * (pulled - inner_mean - unit_x * cross_mean), total_rows(incoming * unit_x), total_rows(incoming)

    def norm_two_back(item):
        part = rows_of(item)
        value, gain_sum, shift_sum = norm_back(both(1, item), residual[part], norm[2:3])
        value = cotangent[part].astype(F32) + value
        grad_res[part] = value
        grad_low[part] = value.astype(BF16)
        add_vector(2, 0, gain_sum)
        add_vector(3, 0, shift_sum)
        add_vector(4, 0, total_rows(value))

    def out_grad(_):
        put_grad(O0, HEAD_COLS, dot_lt(grad_low[...], heads[...]))

    def heads_back(item):
        part = rows_of(item)
        grad_heads[part] = rows_dot(grad_low[part], weight(O0, HEAD_COLS)).astype(BF16)

    def attend_back(item, pair):
        part = rows_of(item)
        query, key, value = (proj[part, lanes(start, pair)] for start in (Q0, K0, V0))
        grad = grad_heads[part, lanes(0, pair)]
        sides = []
        for side in range(2):
            own = first_half if side == 0 else ~first_half
            prob = probs[item, pair * 2 + side]
            grad_prob = dot_rt(jnp.where(own, value, jnp.zeros_like(value)), grad)
            inner_sum = jnp.sum(prob * grad_prob, 0, keepdims=True)
            low = (prob * (grad_prob - inner_sum)).astype(BF16)
            sides.append(
                (dot_lt(low, key) * (HD**-0.5), rows_dot(low, query), rows_dot(prob.astype(BF16), grad))
            )
        for start, left, right in zip((Q0, K0, V0), sides[0], sides[1]):
            low = jnp.where(first_half, left, right).astype(BF16)
            grad_proj[part, lanes(start, pair)] = low
            if start != K0:
                add_vector(6, (0 if start == Q0 else HEAD_COLS) + pair * 128, total_rows(low.astype(F32)))

    def proj_grad(index):
        cols = pl.ds(index * HEAD_COLS, HEAD_COLS)
        put_grad(index * HEAD_COLS, HEAD_COLS, rows_dot(act_one_t[...], grad_proj[:, cols]))

    def heads_in(item):
        fill_part(2, item, dot_rt(grad_proj[rows_of(item)], weight(Q0, 3 * HEAD_COLS)))
        exchange(2, item).start()

    def units_out(item):
        fill_part(3, item, dot_rt(hidden[rows_of(item)], weight(W0, UNIT_COLS)))

    def send_units(_):
        for item in range(items):
            exchange(3, item).start()

    def norm_one_back(item):
        part = rows_of(item)
        value, gain_sum, shift_sum = norm_back(both(2, item), tokens[part].astype(F32), norm[0:1])
        input_grad[part] = grad_res[part] + value
        store(1, item).start()
        add_vector(0, 0, gain_sum)
        add_vector(1, 0, shift_sum)

    def finish_out(item):
        part = rows_of(item)
        out[part] = (residual[part] + both(3, item) + norm[5:6]).astype(BF16)
        store(0, item).start()

    def vec_copy(stage, owner_z=None, step=0):
        if stage < 2:
            peer = (place.across_x(), place.across_y())[stage]
            return remote(vectors, vec_got.at[stage], vs.at[stage], vr.at[stage], peer)
        block = vec_z.at[owner_z]
        return remote(block, block, vs.at[1 + step], vr.at[1 + step], place.along_z(step))

    def small_sums(stage):
        if stage in (1, 2):
            vec_copy(stage - 1).wait()
            vectors[...] = vectors[...] + vec_got[stage - 1]
        if stage < 2:
            vec_copy(stage).start()
        elif stage == 2:
            vec_z[place.z] = vectors[...]
            for step in range(1, NZ):
                vec_copy(2, place.z, step).start()
        else:
            for step in range(1, NZ):
                vec_copy(2, (place.z - step) % NZ, step).wait_recv()
                vec_copy(2, place.z, step).wait_send()
            vectors[...] = (vec_z[0] + vec_z[1]) + (vec_z[2] + vec_z[3])

    pieces = {
        "ln1": norm_one,
        "caps": masks,
        "tr": turned,
        "qkv": project,
        "att": attend,
        "op0": heads_out,
        "ln2": norm_two,
        "up": up,
        "gd": down_grad,
        "pre": pre_grad,
        "da2": units_back,
        "ln2b": norm_two_back,
        "gout": out_grad,
        "do": heads_back,
        "attb": attend_back,
        "gp": proj_grad,
        "da1": heads_in,
        "op2": units_out,
        "op2s": send_units,
        "ln1b": norm_one_back,
        "fout": finish_out,
        "vec": small_sums,
    }

    vectors[...] = jnp.zeros_like(vectors)
    place.greet()
    for load in loads:
        load.wait()
    for kind, *what in PLAN:
        if kind == "g":
            unit, stage = what
            if stage == 0:
                cols = pl.ds(*GATHER_UNITS[unit][:2])
                full[place.z, place.y, place.x, :, cols] = matrices[:, cols].astype(BF16)
            else:
                gather.settle(unit, stage - 1)
            gather.begin(unit, stage)
        elif kind == "gf":
            gather.settle(what[0], 4)
        elif kind == "s":
            unit, stage = what
            if stage > 0:
                scatter.add(unit, stage - 1)
            if stage < 5:
                scatter.begin(unit, stage)
        else:
            pieces[kind](*what)
    for which in range(2):
        for item in range(items):
            store(which, item).wait()
    gather.drain()
    scatter.drain()
    for turn in (2, 3):
        for item in range(items):
            exchange(turn, item).wait_send()


def run_block(inner, tokens, cotangent, task_mask, group_ids, slab, norm_bias, column_bias):
    rows = tokens.shape[0]
    items, length = group_ids.shape
    slab_rows, cols = slab.shape
    heads = HEAD_COLS // HD
    gather_units, scatter_units = len(GATHER_UNITS), len(SCATTER_UNITS)
    dma = pltpu.SemaphoreType.DMA
    vmem = pltpu.VMEM
    in_vmem = pl.BlockSpec(memory_space=pltpu.VMEM)
    anywhere = pl.BlockSpec(memory_space=pl.ANY)
    return pl.pallas_call(
        functools.partial(block_kernel, inner, items, length),
        out_shape=(
            jax.ShapeDtypeStruct((rows, D), BF16),
            jax.ShapeDtypeStruct((rows, D), F32),
            jax.ShapeDtypeStruct((slab_rows, cols), F32),
            jax.ShapeDtypeStruct((16, D), F32),
        ),
        in_specs=[anywhere, anywhere, in_vmem, in_vmem, anywhere, in_vmem, in_vmem],
        out_specs=(anywhere, anywhere, in_vmem, in_vmem),
        scratch_shapes=[
            vmem((NZ, NY, NX, slab_rows, cols), BF16),
            vmem((NZ, NY, NX, slab_rows, cols), BF16),
            vmem((NZ, 2, slab_rows, LATE_COLS), BF16),
            vmem((NZ, slab_rows, LATE_COLS), BF16),
            vmem((2, slab_rows, LATE_COLS), BF16),
            vmem((2, slab_rows, LATE_COLS), BF16),
            vmem((slab_rows, LATE_COLS), BF16),
            vmem((2, NY, NX, slab_rows, EARLY_COLS), BF16),
            vmem((2, NY, NX, slab_rows, EARLY_COLS), BF16),
            vmem((NY, NX, slab_rows, EARLY_COLS), BF16),
            vmem((2, slab_rows, EARLY_COLS), BF16),
            vmem((slab_rows, EARLY_COLS), BF16),
            vmem((rows, D), BF16),
            vmem((D, rows), BF16),
            vmem((rows, D), BF16),
            vmem((D, rows), BF16),
            vmem((D, rows), BF16),
            vmem((rows, 3 * HEAD_COLS), BF16),
            vmem((rows, 3 * HEAD_COLS), BF16),
            vmem((rows, HEAD_COLS), BF16),
            vmem((rows, HEAD_COLS), BF16),
            vmem((items, length, length), F32),
            vmem((items, heads, length, length), F32),
            vmem((rows, D), F32),
            vmem((rows, UNIT_COLS), F32),
            vmem((rows, UNIT_COLS), BF16),
            vmem((rows, UNIT_COLS), BF16),
            vmem((rows, D), F32),
            vmem((rows, D), BF16),
            vmem((2, rows, D), BF16),
            vmem((2, rows, D), BF16),
            vmem((2, 16, D), F32),
            vmem((NZ, 16, D), F32),
            dma((gather_units, 5)),
            dma((gather_units, 5)),
            dma((scatter_units, 5)),
            dma((scatter_units, 5)),
            dma((4, items)),
            dma((4, items)),
            dma((2 + NZ - 1,)),
            dma((2 + NZ - 1,)),
            vmem((rows, D), BF16),
            vmem((rows, D), BF16),
            vmem((slab_rows, cols), F32),
            vmem((rows, D), BF16),
            vmem((rows, D), F32),
            dma((3,)),
            dma((2, items)),
        ],
        compiler_params=pltpu.CompilerParams(
            collective_id=0, has_side_effects=True, vmem_limit_bytes=60 << 20
        ),
    )(tokens, cotangent, task_mask, group_ids, slab, norm_bias, column_bias)


def adam_update(weight_now, gradient, first_now, second_now, step_rate, weight_decay):
    first_new = BETA_FIRST * first_now + (1.0 - BETA_FIRST) * gradient
    second_new = BETA_SECOND * second_now + (1.0 - BETA_SECOND) * gradient * gradient
    first_fixed = first_new / (1.0 - BETA_FIRST**STEP)
    second_fixed = second_new / (1.0 - BETA_SECOND**STEP)
    weight_new = weight_now - step_rate * (
        first_fixed / (jnp.sqrt(second_fixed) + EPS_ADAM) + weight_decay * weight_now
    )
    return (weight_new, first_new, second_new)


FINISH_STEPS = 4


def finish_kernel(*refs):
    (out_in, dx_in, grad, vectors, mats, mat_m, mat_n, mat_a) = refs[:8]
    (norm, norm_m, norm_n, norm_a, col, col_m, col_n, col_a) = refs[8:16]
    results = refs[16:]
    results[0][...] = out_in[...]
    results[1][...] = dx_in[...]

    def update(targets, gradient, old, decay, rate, average):
        new, first, second = adam_update(*old[:1], gradient, *old[1:], rate, decay)
        for target, value in zip(
            targets, (gradient, new, first, second, AVERAGE_KEEP * average + (1.0 - AVERAGE_KEEP) * new)
        ):
            target(value)

    def whole(ref):
        def store(value):
            ref[...] = value

        return store

    update(
        [whole(ref) for ref in results[2:7]],
        grad[...],
        (mats[...], mat_m[...], mat_n[...]),
        DECAY_MATRIX,
        RATE_MATRIX,
        mat_a[...],
    )

    @pl.when(pl.program_id(0) == 0)
    def _():
        update(
            [whole(ref) for ref in results[7:12]],
            vectors[0:6, :],
            (norm[...], norm_m[...], norm_n[...]),
            0.0,
            RATE_VECTOR,
            norm_a[...],
        )
        for row in range(3):
            part = pl.ds(row * D, D)

            def piece(ref, part=part):
                def store(value):
                    ref[part] = value.reshape(D)

                return store

            update(
                [piece(ref) for ref in results[12:17]],
                vectors[6 + row : 7 + row, :],
                tuple(ref[part].reshape(1, D) for ref in (col, col_m, col_n)),
                0.0,
                RATE_VECTOR,
                col_a[part].reshape(1, D),
            )


def finish(output, input_grad, matrix_grad, vectors, matrix_set, norm_set, column_set):
    rows = output.shape[0] // FINISH_STEPS
    slab_rows, cols = matrix_grad.shape
    token_block = pl.BlockSpec((rows, D), lambda step: (step, 0))
    matrix_block = pl.BlockSpec((slab_rows, cols // FINISH_STEPS), lambda step: (0, step))

    def small(array):
        return pl.BlockSpec(array.shape, lambda step: (0,) * array.ndim)

    shape = jax.ShapeDtypeStruct
    norm_bias, column_bias = norm_set[0], column_set[0]
    return pl.pallas_call(
        finish_kernel,
        grid=(FINISH_STEPS,),
        out_shape=[shape(output.shape, output.dtype), shape(input_grad.shape, F32)]
        + [shape(matrix_grad.shape, F32)] * 5
        + [shape(norm_bias.shape, F32)] * 5
        + [shape(column_bias.shape, F32)] * 5,
        in_specs=[token_block, token_block, matrix_block, small(vectors)]
        + [matrix_block] * 4
        + [small(norm_bias)] * 4
        + [small(column_bias)] * 4,
        out_specs=[token_block, token_block]
        + [matrix_block] * 5
        + [small(norm_bias)] * 5
        + [small(column_bias)] * 5,
        compiler_params=pltpu.CompilerParams(vmem_limit_bytes=60 << 20),
    )(output, input_grad, matrix_grad, vectors, *matrix_set, *norm_set, *column_set)


def local(
    tokens,
    cotangent,
    task_mask,
    group_ids,
    matrices,
    matrix_first,
    matrix_second,
    matrix_average,
    norm_bias,
    norm_first,
    norm_second,
    norm_average,
    column_bias,
    column_first,
    column_second,
    column_average,
):
    inner = lax.axis_size("dp") // OUTER
    groups = [[outer * inner + i for i in range(inner)] for outer in range(OUTER)]
    slab = matrices
    if inner > 1:
        slab = lax.all_gather(
            matrices.astype(BF16), "dp", axis=0, tiled=True, axis_index_groups=groups
        ).astype(F32)
    output, input_grad, matrix_grad, vectors = run_block(
        inner, tokens, cotangent, task_mask, group_ids, slab, norm_bias, column_bias
    )
    if inner > 1:
        matrix_grad = lax.psum_scatter(
            matrix_grad, "dp", scatter_dimension=0, tiled=True, axis_index_groups=groups
        )
        vectors = jnp.sum(lax.all_gather(vectors, "dp", axis=0, axis_index_groups=groups), 0)
    return tuple(
        finish(
            output,
            input_grad,
            matrix_grad,
            vectors,
            (matrices, matrix_first, matrix_second, matrix_average),
            (norm_bias, norm_first, norm_second, norm_average),
            (column_bias, column_first, column_second, column_average),
        )
    )


def solution(mesh):
    placed = (
        P("dp", None),
        P("dp", None),
        P("dp", None),
        P("dp", None),
        P("dp", "mp"),
        P("dp", "mp"),
        P("dp", "mp"),
        P("dp", "mp"),
        P(),
        P(),
        P(),
        P(),
        P("mp"),
        P("mp"),
        P("mp"),
        P("mp"),
    )
    return jax.shard_map(
        local,
        mesh=mesh,
        in_specs=placed,
        out_specs=(
            P("dp", None),
            P("dp", None),
            P("dp", "mp"),
            P("dp", "mp"),
            P("dp", "mp"),
            P("dp", "mp"),
            P("dp", "mp"),
            P(),
            P(),
            P(),
            P(),
            P(),
            P("mp"),
            P("mp"),
            P("mp"),
            P("mp"),
            P("mp"),
        ),
        check_vma=False,
    )
```

```python
import functools

import jax
import jax.numpy as jnp
from jax import lax
from jax.experimental import pallas as pl
from jax.experimental.pallas import tpu as pltpu
from jax.sharding import PartitionSpec as P

MESH = pl.DeviceIdType.MESH

D = 768
HEADS = 12
HD = 64
FF = 3072
STEP = 10


NORM_EPSILON = 1e-06
NEGATIVE = -1e30
GELU_SCALE = 0.7978845608028654
GELU_CUBIC = 0.044715
BETA_FIRST = 0.9
BETA_SECOND = 0.999
EPS_ADAM = 1e-08
RATE_MATRIX = 0.1
RATE_VECTOR = 0.3
DECAY_MATRIX = 0.1
AVERAGE_KEEP = 0.7


NZ, NY, NX = 4, 2, 2
OUTER = NZ * NY * NX
COL_TILE = 256
F32, BF16 = jnp.float32, jnp.bfloat16


class Place:
    def __init__(self, inner):
        index = lax.axis_index("dp")
        outer = index // inner
        self.inner = inner
        self.rest = index % inner
        self.core = lax.axis_index("mp")
        self.x = outer % NX
        self.y = (outer // NX) % NY
        self.z = outer // (NX * NY)
        self.partner_z = self.z + 1 - 2 * (self.z % 2)
        self.near_pair = pl.ds(2 * (self.z // 2), 2)
        self.far_pair = pl.ds(2 - 2 * (self.z // 2), 2)

    def device(self, z, y, x):
        return (((z * NY + y) * NX + x) * self.inner + self.rest, self.core)

    def along_z(self, step):
        return self.device((self.z + step) % NZ, self.y, self.x)

    def across_y(self):
        return self.device(self.z, 1 - self.y, self.x)

    def across_x(self):
        return self.device(self.z, self.y, 1 - self.x)

    def sibling(self):
        return (self.device(self.z, self.y, self.x)[0], 1 - self.core)

    def greet(self):
        barrier = pltpu.get_barrier_semaphore()
        peers = [self.along_z(step) for step in range(1, NZ)]
        peers += [self.across_y(), self.across_x(), self.sibling()]
        for peer in peers:
            pl.semaphore_signal(barrier, inc=1, device_id=peer, device_id_type=MESH)
        pl.semaphore_wait(barrier, len(peers))


def remote(src, dst, send_sem, recv_sem, peer):
    return pltpu.make_async_remote_copy(
        src_ref=src,
        dst_ref=dst,
        send_sem=send_sem,
        recv_sem=recv_sem,
        device_id=peer,
        device_id_type=MESH,
    )


class Mover:
    line = "abc"

    def __init__(self, place, units, full, send_sem, recv_sem):
        self.place, self.units, self.full = place, units, full
        self.send_sem, self.recv_sem = send_sem, recv_sem
        self.inner_z = (place.z == 1) | (place.z == 2)
        self.outer_z = (place.z == 0) | (place.z == 3)

    def stages(self, unit):
        found = []
        route = self.units[unit][2]
        for spot, axis in enumerate(route):
            for name in self.line if axis == "z" else axis:
                found.append((name, route[:spot], route[spot + 1 :]))
        return found

    def peer(self, name):
        p = self.place
        if name == "x":
            return p.across_x()
        if name == "y":
            return p.across_y()
        return p.device(p.partner_z if name in "ac" else NZ - 1 - p.z, p.y, p.x)

    def block(self, unit, whole, z, y, x):
        start, width, _ = self.units[unit]
        index = [slice(None) if name in whole else here for name, here in (("z", z), ("y", y), ("x", x))]
        return tuple(index) + (slice(None), pl.ds(start, width))

    def copy(self, unit, stage, src, dst, name):
        return remote(src, dst, self.send_sem.at[unit, stage], self.recv_sem.at[unit, stage], self.peer(name))

    def begin(self, unit, stage):
        name = self.stages(unit)[stage][0]
        self.guarded(self.sender(name), lambda: self.leaving(unit, stage).start())

    def settle(self, unit, stage):
        name = self.stages(unit)[stage][0]
        self.guarded(self.receiver(name), lambda: self.arriving(unit, stage).wait_recv())

    @staticmethod
    def guarded(condition, action):
        if condition is None:
            action()
        else:
            pl.when(condition)(action)

    def drain(self):
        for unit in range(len(self.units)):
            for stage, (name, _, _) in enumerate(self.stages(unit)):
                self.guarded(self.sender(name), lambda: self.leaving(unit, stage).wait_send())


class Gather(Mover):
    def sender(self, name):
        return self.inner_z if name in "bc" else None

    def receiver(self, name):
        return {"b": self.inner_z, "c": self.outer_z}.get(name)

    def leaving(self, unit, stage):
        p = self.place
        name, before, _ = self.stages(unit)[stage]
        z = {"b": p.near_pair, "c": p.far_pair}.get(name, p.z)
        mine = self.full.at[self.block(unit, before, z, p.y, p.x)]
        return self.copy(unit, stage, mine, mine, name)

    def arriving(self, unit, stage):
        p = self.place
        name, before, _ = self.stages(unit)[stage]
        z = {"a": p.partner_z, "b": p.far_pair, "c": p.far_pair}.get(name, p.z)
        y = 1 - p.y if name == "y" else p.y
        x = 1 - p.x if name == "x" else p.x
        theirs = self.full.at[self.block(unit, before, z, y, x)]
        return self.copy(unit, stage, theirs, theirs, name)


class Scatter(Mover):
    line = "cba"

    def __init__(self, place, units, full, landings, result, send_sem, recv_sem):
        super().__init__(place, units, full, send_sem, recv_sem)
        self.landings, self.result = landings, result

    def sender(self, name):
        return {"b": self.inner_z, "c": self.outer_z}.get(name)

    def receiver(self, name):
        return self.inner_z if name in "bc" else None

    def landing(self, unit, stage):
        _, width, route = self.units[unit]
        got = self.landings[int(route[0] == "z")][stage]
        lead = (slice(None),) * (len(got.shape) - 1)
        return got.at[lead + (pl.ds(LANDING[unit], width),)]

    def leaving(self, unit, stage):
        p = self.place
        name, _, after = self.stages(unit)[stage]
        z = {"a": p.partner_z, "b": p.far_pair, "c": p.far_pair}.get(name, p.z)
        y = 1 - p.y if name == "y" else p.y
        x = 1 - p.x if name == "x" else p.x
        away = self.full.at[self.block(unit, after, z, y, x)]
        return self.copy(unit, stage, away, self.landing(unit, stage), name)

    arriving = leaving

    def add(self, unit, stage):
        p = self.place
        steps = self.stages(unit)
        name, _, after = steps[stage]

        def action():
            self.arriving(unit, stage).wait_recv()
            z = {"b": p.near_pair, "c": p.far_pair}.get(name, p.z)
            part = self.block(unit, after, z, p.y, p.x)
            total = self.full[part].astype(F32) + self.landing(unit, stage)[...].astype(F32)
            if stage + 1 == len(steps):
                start, width, _ = self.units[unit]
                self.result[:, pl.ds(start, width)] = total
            else:
                self.full[part] = total.astype(BF16)

        self.guarded(self.receiver(name), action)


def rows_dot(left, right):
    return jnp.dot(left, right, preferred_element_type=F32)


def dot_rt(left, right):
    return lax.dot_general(left, right, (((1,), (1,)), ((), ())), preferred_element_type=F32)


def dot_lt(left, right):
    return lax.dot_general(left, right, (((0,), (0,)), ((), ())), preferred_element_type=F32)


def normalized(values):
    center = values - jnp.mean(values, -1, keepdims=True)
    spread = jnp.mean(center * center, -1, keepdims=True)
    scale = lax.rsqrt(spread + NORM_EPSILON)
    return center * scale, scale


def total_rows(values):
    return jnp.sum(values, 0, keepdims=True)


GATHER_UNITS = (
    (0, 128, "zxy"),
    (128, 128, "zxy"),
    (256, 128, "zyx"),
    (384, 128, "zxy"),
    (512, 128, "zyx"),
    (640, 128, "zxy"),
    (768, 128, "zxy"),
    (896, 128, "zyx"),
    (1024, 256, "zyx"),
    (1280, 128, "yxz"),
    (1408, 384, "zyx"),
    (1792, 256, "zxy"),
    (2048, 256, "zyx"),
    (2304, 256, "zxy"),
    (2560, 256, "zyx"),
    (2816, 128, "zyx"),
    (2944, 128, "zyx"),
    (3072, 128, "zxy"),
    (3200, 256, "yxz"),
    (3456, 128, "zyx"),
    (3584, 128, "xyz"),
    (3712, 128, "zyx"),
    (3840, 128, "yxz"),
    (3968, 256, "xyz"),
    (4224, 256, "yxz"),
    (4480, 128, "xyz"),
)
SCATTER_UNITS = (
    (3072, 256, "zxy"),
    (3328, 128, "zxy"),
    (3456, 128, "yxz"),
    (3584, 256, "yxz"),
    (3840, 128, "yxz"),
    (3968, 128, "zxy"),
    (4096, 128, "yxz"),
    (4224, 128, "zxy"),
    (4352, 256, "yxz"),
    (1536, 256, "xyz"),
    (1792, 256, "yxz"),
    (2048, 256, "zxy"),
    (2304, 256, "xyz"),
    (2560, 256, "zyx"),
    (2816, 256, "xyz"),
    (1152, 384, "yxz"),
    (0, 128, "xyz"),
    (128, 256, "yxz"),
    (384, 128, "yxz"),
    (512, 128, "xyz"),
    (640, 128, "yxz"),
    (768, 128, "xyz"),
    (896, 128, "zyx"),
    (1024, 128, "xyz"),
)
LANDING = (
    0, 256, 0, 128, 384, 384, 512, 512, 640, 896, 1152, 640,
    1408, 896, 1664, 1920, 2304, 2432, 2688, 2816, 2944, 3072, 1152, 3200,
)
LATE_COLS, EARLY_COLS = 3328, 1280
PLAN = (
    ("g", 0, 0), ("g", 1, 0), ("g", 2, 0), ("g", 3, 0), ("g", 4, 0), ("g", 5, 0), ("g", 6, 0), ("g", 7, 0),
    ("g", 8, 0), ("g", 10, 0), ("g", 11, 0), ("g", 12, 0), ("g", 13, 0), ("g", 14, 0), ("g", 15, 0),
    ("g", 16, 0), ("g", 17, 0), ("g", 19, 0), ("g", 21, 0), ("g", 9, 0), ("g", 18, 0), ("g", 0, 1),
    ("g", 20, 0), ("g", 1, 1), ("g", 22, 0), ("g", 2, 1), ("g", 3, 1), ("g", 23, 0), ("g", 4, 1), ("g", 24, 0),
    ("g", 5, 1), ("g", 25, 0), ("g", 6, 1), ("g", 7, 1), ("ln1", 0), ("ln1", 1), ("caps", 0), ("g", 8, 1),
    ("tr", 0), ("g", 9, 1), ("g", 10, 1), ("tr", 1), ("g", 0, 2), ("g", 11, 1), ("g", 18, 1), ("g", 1, 2),
    ("g", 12, 1), ("g", 20, 1), ("g", 22, 1), ("g", 2, 2), ("g", 13, 1), ("g", 23, 1), ("g", 3, 2),
    ("g", 14, 1), ("g", 24, 1), ("g", 15, 1), ("g", 4, 2), ("g", 16, 1), ("g", 25, 1), ("g", 17, 1),
    ("g", 5, 2), ("g", 19, 1), ("g", 21, 1), ("g", 6, 2), ("g", 0, 3), ("g", 7, 2), ("g", 1, 3), ("g", 9, 2),
    ("g", 2, 3), ("g", 8, 2), ("g", 3, 3), ("g", 4, 3), ("g", 5, 3), ("g", 10, 2), ("g", 6, 3), ("g", 7, 3),
    ("g", 11, 2), ("g", 0, 4), ("g", 9, 3), ("g", 12, 2), ("g", 1, 4), ("g", 2, 4), ("g", 8, 3), ("g", 13, 2),
    ("g", 3, 4), ("g", 4, 4), ("g", 14, 2), ("g", 5, 4), ("g", 10, 3), ("g", 15, 2), ("g", 7, 4), ("g", 16, 2),
    ("g", 6, 4), ("g", 11, 3), ("g", 17, 2), ("g", 19, 2), ("g", 12, 3), ("g", 21, 2), ("g", 13, 3),
    ("g", 18, 2), ("g", 14, 3), ("g", 9, 4), ("g", 15, 3), ("g", 16, 3), ("g", 17, 3), ("g", 19, 3),
    ("g", 8, 4), ("g", 21, 3), ("g", 20, 2), ("g", 18, 3), ("g", 22, 2), ("g", 11, 4), ("g", 23, 2),
    ("g", 13, 4), ("g", 20, 3), ("g", 24, 2), ("g", 17, 4), ("g", 22, 3), ("g", 10, 4), ("g", 25, 2),
    ("g", 23, 3), ("g", 18, 4), ("gf", 0), ("gf", 1), ("gf", 2), ("gf", 3), ("gf", 4), ("gf", 5), ("gf", 6),
    ("gf", 7), ("gf", 8), ("qkv", 0), ("qkv", 1), ("att", 0, 0), ("g", 24, 3), ("att", 0, 1), ("g", 12, 4),
    ("g", 20, 4), ("g", 25, 3), ("att", 0, 2), ("att", 1, 0), ("g", 14, 4), ("g", 22, 4), ("att", 1, 1),
    ("att", 1, 2), ("g", 15, 4), ("g", 16, 4), ("gf", 9), ("gf", 10), ("op0", 0), ("g", 19, 4), ("op0", 1),
    ("g", 23, 4), ("g", 21, 4), ("ln2", 0), ("ln2", 1), ("g", 24, 4), ("tr", 2), ("up", 0), ("gf", 11),
    ("up", 1), ("gf", 12), ("up", 2), ("g", 25, 4), ("gf", 14), ("up", 4), ("gd", 0), ("s", 0, 0), ("gd", 1),
    ("s", 2, 0), ("gf", 13), ("up", 3), ("gd", 2), ("s", 3, 0), ("gd", 3), ("gd", 4), ("gf", 17), ("gf", 18),
    ("pre", 0), ("s", 1, 0), ("s", 4, 0), ("s", 9, 0), ("gf", 15), ("gf", 16), ("up", 5), ("gd", 5), ("gf", 22),
    ("gf", 23), ("pre", 3), ("s", 5, 0), ("s", 6, 0), ("s", 12, 0), ("gf", 19), ("pre", 1), ("s", 2, 1),
    ("gf", 24), ("pre", 4), ("gf", 25), ("pre", 5), ("s", 7, 0), ("s", 8, 0), ("gf", 20), ("gf", 21),
    ("pre", 2), ("da2", 0), ("da2", 1), ("s", 11, 0), ("s", 0, 1), ("s", 3, 1), ("s", 10, 0), ("s", 9, 1),
    ("s", 1, 1), ("s", 4, 1), ("s", 14, 0), ("s", 13, 0), ("ln2b", 0), ("s", 5, 1), ("s", 6, 1), ("ln2b", 1),
    ("s", 7, 1), ("s", 12, 1), ("gout", 0), ("s", 0, 2), ("s", 2, 2), ("do", 0), ("do", 1), ("s", 8, 1),
    ("attb", 0, 0), ("s", 1, 2), ("s", 3, 2), ("s", 15, 0), ("attb", 0, 1), ("s", 4, 2), ("s", 11, 1),
    ("s", 5, 2), ("attb", 0, 2), ("s", 10, 1), ("attb", 1, 0), ("s", 7, 2), ("attb", 1, 1), ("s", 9, 2),
    ("s", 13, 1), ("s", 6, 2), ("s", 14, 1), ("attb", 1, 2), ("s", 0, 3), ("s", 2, 3), ("s", 8, 2),
    ("s", 12, 2), ("s", 1, 3), ("gp", 0), ("s", 11, 2), ("s", 3, 3), ("s", 16, 0), ("s", 4, 3), ("s", 10, 2),
    ("s", 17, 0), ("gp", 1), ("s", 5, 3), ("s", 19, 0), ("gp", 2), ("s", 0, 4), ("s", 1, 4), ("s", 7, 3),
    ("s", 21, 0), ("s", 22, 0), ("da1", 0), ("s", 9, 3), ("s", 13, 2), ("s", 2, 4), ("s", 6, 3), ("s", 15, 1),
    ("s", 3, 4), ("s", 8, 3), ("s", 4, 4), ("s", 5, 4), ("s", 14, 2), ("s", 12, 3), ("s", 16, 1), ("s", 18, 0),
    ("da1", 1), ("s", 23, 0), ("s", 20, 0), ("op2", 0), ("s", 9, 4), ("s", 11, 3), ("s", 6, 4), ("s", 7, 4),
    ("s", 19, 1), ("op2", 1), ("s", 8, 4), ("s", 10, 3), ("s", 17, 1), ("s", 0, 5), ("s", 12, 4), ("s", 1, 5),
    ("s", 21, 1), ("s", 5, 5), ("ln1b", 0), ("s", 22, 1), ("s", 16, 2), ("ln1b", 1), ("op2s", 0), ("s", 13, 3),
    ("s", 2, 5), ("s", 15, 2), ("s", 10, 4), ("s", 3, 5), ("s", 18, 1), ("s", 4, 5), ("vec", 0), ("s", 14, 3),
    ("s", 23, 1), ("s", 9, 5), ("s", 20, 1), ("s", 6, 5), ("s", 7, 5), ("s", 8, 5), ("s", 11, 4), ("s", 22, 2),
    ("s", 12, 5), ("s", 19, 2), ("s", 16, 3), ("s", 21, 2), ("s", 17, 2), ("s", 15, 3), ("s", 13, 4),
    ("s", 14, 4), ("s", 10, 5), ("s", 18, 2), ("vec", 1), ("s", 23, 2), ("fout", 0), ("s", 11, 5), ("s", 16, 4),
    ("s", 22, 3), ("s", 19, 3), ("s", 20, 2), ("fout", 1), ("s", 21, 3), ("s", 13, 5), ("s", 17, 3),
    ("s", 14, 5), ("s", 15, 4), ("s", 18, 3), ("s", 23, 3), ("s", 22, 4), ("s", 16, 5), ("s", 19, 4),
    ("vec", 2), ("s", 20, 3), ("s", 21, 4), ("s", 17, 4), ("s", 15, 5), ("s", 18, 4), ("s", 22, 5),
    ("s", 23, 4), ("s", 19, 5), ("s", 21, 5), ("s", 20, 4), ("vec", 3), ("s", 17, 5), ("s", 18, 5),
    ("s", 23, 5), ("s", 20, 5),
)

HEAD_COLS, UNIT_COLS = 384, 1536
Q0, K0, V0, O0, U0, W0 = 0, 384, 768, 1152, 1536, 3072


def block_kernel(
    inner, items, length, tokens_hbm, cotangent_hbm, task_mask, group_ids, matrices_hbm, norm, column, *rest
):
    (out_hbm, input_grad_hbm, matrix_grad, vectors) = rest[:4]
    (full, grads) = rest[4:6]
    landings = (rest[6:11], rest[11:16])
    (act_one, act_one_t, act_two, act_two_t, cot_t, proj, grad_proj, heads, grad_heads) = rest[16:25]
    (caps, probs, residual, slope, hidden, grad_pre, grad_res, grad_low, ex_send, ex_recv) = rest[25:35]
    (vec_got, vec_z, g_send, g_recv, s_send, s_recv, es, er, vs, vr) = rest[35:45]
    (tokens, cotangent, matrices, out, input_grad, in_sem, out_sem) = rest[45:]
    loads = [
        pltpu.make_async_copy(source, target, in_sem.at[spot])
        for spot, (source, target) in enumerate(
            ((matrices_hbm, matrices), (tokens_hbm, tokens), (cotangent_hbm, cotangent))
        )
    ]
    for load in loads:
        load.start()
    place = Place(inner)
    gather = Gather(place, GATHER_UNITS, full, g_send, g_recv)
    scatter = Scatter(place, SCATTER_UNITS, grads, landings, matrix_grad, s_send, s_recv)

    def weight(start, width):
        return full[:, :, :, :, pl.ds(start, width)].reshape(D, width)

    def put_grad(start, width, value):
        grads[:, :, :, :, pl.ds(start, width)] = value.astype(BF16).reshape(grads.shape[:4] + (width,))

    def rows_of(item):
        return pl.ds(item * length, length)

    def store(which, item):
        part = rows_of(item)
        source, target = ((out, out_hbm), (input_grad, input_grad_hbm))[which]
        return pltpu.make_async_copy(source.at[part], target.at[part], out_sem.at[which, item])

    def add_vector(row, first, value):
        cols = pl.ds(first, value.shape[1])
        vectors[row : row + 1, cols] = vectors[row : row + 1, cols] + value

    def exchange(turn, item):
        part = rows_of(item)
        return remote(
            ex_send.at[turn % 2, part],
            ex_recv.at[turn % 2, part],
            es.at[turn, item],
            er.at[turn, item],
            place.sibling(),
        )

    def fill_part(turn, item, value):
        if turn >= 2:
            exchange(turn - 2, item).wait_send()
        ex_send[turn % 2, rows_of(item)] = value.astype(BF16)

    def both(turn, item):
        exchange(turn, item).wait_recv()
        part = rows_of(item)
        return ex_send[turn % 2, part].astype(F32) + ex_recv[turn % 2, part].astype(F32)

    def norm_one(item):
        part = rows_of(item)
        unit_x, _ = normalized(tokens[part].astype(F32))
        act_one[part] = (unit_x * norm[0:1] + norm[1:2]).astype(BF16)
        add_vector(5, 0, total_rows(cotangent[part].astype(F32)))

    def masks(_):
        key_index = lax.broadcasted_iota(jnp.int32, (length, length), 0)
        query_index = lax.broadcasted_iota(jnp.int32, (length, length), 1)
        same = key_index == query_index
        slots = task_mask.shape[1]
        slot_same = lax.broadcasted_iota(jnp.int32, (slots, slots), 0) == lax.broadcasted_iota(
            jnp.int32, (slots, slots), 1
        )
        for item in range(items):
            query_ids = group_ids[item : item + 1, :]
            key_ids = jnp.sum(jnp.where(same, query_ids, 0), axis=1, keepdims=True)
            filled = jnp.sum(jnp.where(slot_same, task_mask[item : item + 1, :], 0), axis=1, keepdims=True)
            live = jnp.concatenate([filled, jnp.ones((length - slots, 1), jnp.int32)], axis=0)
            odd_key = jnp.where((key_ids == 0) | (key_ids % 2 == 1), 1, 0)
            earlier = (odd_key == 1) & (key_ids <= query_ids)
            visible = (earlier | (key_ids == query_ids)) & (live == 1)
            caps[item] = jnp.where(visible | same, 3.0e38, NEGATIVE)

    def turned(which):
        source, target = ((act_one, act_one_t), (cotangent, cot_t), (act_two, act_two_t))[which]
        target[...] = source[...].T

    def project(item):
        part = rows_of(item)
        for start, scale, bias in ((Q0, HD**-0.5, 0), (K0, 1.0, None), (V0, 1.0, HEAD_COLS)):
            value = rows_dot(act_one[part], weight(start, HEAD_COLS))
            if bias is not None:
                value = value + column[pl.ds(bias, HEAD_COLS)].reshape(1, HEAD_COLS)
            value = value.astype(BF16)
            if scale != 1.0:
                value = value * jnp.asarray(scale, BF16)
            proj[part, start : start + HEAD_COLS] = value

    lane = lax.broadcasted_iota(jnp.int32, (length, 128), 1)
    first_half = lane < HD

    def lanes(start, pair):
        return pl.ds(start + pair * 128, 128)

    def attend(item, pair):
        part = rows_of(item)
        query, key, value = (proj[part, lanes(start, pair)] for start in (Q0, K0, V0))
        sides = []
        for side in range(2):
            own = first_half if side == 0 else ~first_half
            scores = dot_rt(jnp.where(own, key, jnp.zeros_like(key)), query)
            scores = jnp.minimum(scores, caps[item])
            weights = jnp.exp(scores - jnp.max(scores, 0, keepdims=True))
            prob = weights * (1.0 / jnp.sum(weights, 0, keepdims=True))
            probs[item, pair * 2 + side] = prob
            sides.append(dot_lt(prob.astype(BF16), value))
        heads[part, lanes(0, pair)] = jnp.where(first_half, sides[0], sides[1]).astype(BF16)

    def heads_out(item):
        fill_part(0, item, dot_rt(heads[rows_of(item)], weight(O0, HEAD_COLS)))
        exchange(0, item).start()

    def norm_two(item):
        part = rows_of(item)
        value = tokens[part].astype(F32) + both(0, item) + norm[4:5]
        residual[part] = value
        unit_x, _ = normalized(value)
        act_two[part] = (unit_x * norm[2:3] + norm[3:4]).astype(BF16)

    def up(index):
        start = index * COL_TILE
        cols = pl.ds(start, COL_TILE)
        unit = rows_dot(act_two[...], weight(U0 + start, COL_TILE))
        unit = unit + column[pl.ds(2 * HEAD_COLS + start, COL_TILE)].reshape(1, COL_TILE)
        square = unit * unit
        bent = jnp.tanh(unit * (GELU_SCALE + (GELU_SCALE * GELU_CUBIC) * square))
        half = 0.5 * (1.0 + bent)
        hidden[:, cols] = (unit * half).astype(BF16)
        slope[:, cols] = half + 0.5 * unit * (1.0 - bent * bent) * (
            GELU_SCALE + (3.0 * GELU_SCALE * GELU_CUBIC) * square
        )

    def down_grad(index):
        start = index * COL_TILE
        put_grad(W0 + start, COL_TILE, rows_dot(cot_t[...], hidden[:, pl.ds(start, COL_TILE)]))

    def pre_grad(index):
        start = index * COL_TILE
        cols = pl.ds(start, COL_TILE)
        value = rows_dot(cotangent[...], weight(W0 + start, COL_TILE))
        low = (value * slope[:, cols]).astype(BF16)
        grad_pre[:, cols] = low
        row, first = divmod(2 * HEAD_COLS + start, D)
        add_vector(6 + row, first, total_rows(low.astype(F32)))
        put_grad(U0 + start, COL_TILE, rows_dot(act_two_t[...], low))

    def units_back(item):
        fill_part(1, item, dot_rt(grad_pre[rows_of(item)], weight(U0, UNIT_COLS)))
        exchange(1, item).start()

    def norm_back(incoming, values, gain):
        unit_x, scale = normalized(values)
        pulled = incoming * gain
        inner_mean = jnp.mean(pulled, -1, keepdims=True)
        cross_mean = jnp.mean(pulled * unit_x, -1, keepdims=True)
        return scale * (pulled - inner_mean - unit_x * cross_mean), total_rows(incoming * unit_x), total_rows(incoming)

    def norm_two_back(item):
        part = rows_of(item)
        value, gain_sum, shift_sum = norm_back(both(1, item), residual[part], norm[2:3])
        value = cotangent[part].astype(F32) + value
        grad_res[part] = value
        grad_low[part] = value.astype(BF16)
        add_vector(2, 0, gain_sum)
        add_vector(3, 0, shift_sum)
        add_vector(4, 0, total_rows(value))

    def out_grad(_):
        put_grad(O0, HEAD_COLS, dot_lt(grad_low[...], heads[...]))

    def heads_back(item):
        part = rows_of(item)
        grad_heads[part] = rows_dot(grad_low[part], weight(O0, HEAD_COLS)).astype(BF16)

    def attend_back(item, pair):
        part = rows_of(item)
        query, key, value = (proj[part, lanes(start, pair)] for start in (Q0, K0, V0))
        grad = grad_heads[part, lanes(0, pair)]
        sides = []
        for side in range(2):
            own = first_half if side == 0 else ~first_half
            prob = probs[item, pair * 2 + side]
            grad_prob = dot_rt(jnp.where(own, value, jnp.zeros_like(value)), grad)
            inner_sum = jnp.sum(prob * grad_prob, 0, keepdims=True)
            low = (prob * (grad_prob - inner_sum)).astype(BF16)
            sides.append(
                (dot_lt(low, key) * (HD**-0.5), rows_dot(low, query), rows_dot(prob.astype(BF16), grad))
            )
        for start, left, right in zip((Q0, K0, V0), sides[0], sides[1]):
            low = jnp.where(first_half, left, right).astype(BF16)
            grad_proj[part, lanes(start, pair)] = low
            if start != K0:
                add_vector(6, (0 if start == Q0 else HEAD_COLS) + pair * 128, total_rows(low.astype(F32)))

    def proj_grad(index):
        cols = pl.ds(index * HEAD_COLS, HEAD_COLS)
        put_grad(index * HEAD_COLS, HEAD_COLS, rows_dot(act_one_t[...], grad_proj[:, cols]))

    def heads_in(item):
        fill_part(2, item, dot_rt(grad_proj[rows_of(item)], weight(Q0, 3 * HEAD_COLS)))
        exchange(2, item).start()

    def units_out(item):
        fill_part(3, item, dot_rt(hidden[rows_of(item)], weight(W0, UNIT_COLS)))

    def send_units(_):
        for item in range(items):
            exchange(3, item).start()

    def norm_one_back(item):
        part = rows_of(item)
        value, gain_sum, shift_sum = norm_back(both(2, item), tokens[part].astype(F32), norm[0:1])
        input_grad[part] = grad_res[part] + value
        store(1, item).start()
        add_vector(0, 0, gain_sum)
        add_vector(1, 0, shift_sum)

    def finish_out(item):
        part = rows_of(item)
        out[part] = (residual[part] + both(3, item) + norm[5:6]).astype(BF16)
        store(0, item).start()

    def vec_copy(stage, owner_z=None, step=0):
        if stage < 2:
            peer = (place.across_x(), place.across_y())[stage]
            return remote(vectors, vec_got.at[stage], vs.at[stage], vr.at[stage], peer)
        block = vec_z.at[owner_z]
        return remote(block, block, vs.at[1 + step], vr.at[1 + step], place.along_z(step))

    def small_sums(stage):
        if stage in (1, 2):
            vec_copy(stage - 1).wait()
            vectors[...] = vectors[...] + vec_got[stage - 1]
        if stage < 2:
            vec_copy(stage).start()
        elif stage == 2:
            vec_z[place.z] = vectors[...]
            for step in range(1, NZ):
                vec_copy(2, place.z, step).start()
        else:
            for step in range(1, NZ):
                vec_copy(2, (place.z - step) % NZ, step).wait_recv()
                vec_copy(2, place.z, step).wait_send()
            vectors[...] = (vec_z[0] + vec_z[1]) + (vec_z[2] + vec_z[3])

    pieces = {
        "ln1": norm_one,
        "caps": masks,
        "tr": turned,
        "qkv": project,
        "att": attend,
        "op0": heads_out,
        "ln2": norm_two,
        "up": up,
        "gd": down_grad,
        "pre": pre_grad,
        "da2": units_back,
        "ln2b": norm_two_back,
        "gout": out_grad,
        "do": heads_back,
        "attb": attend_back,
        "gp": proj_grad,
        "da1": heads_in,
        "op2": units_out,
        "op2s": send_units,
        "ln1b": norm_one_back,
        "fout": finish_out,
        "vec": small_sums,
    }

    vectors[...] = jnp.zeros_like(vectors)
    place.greet()
    for load in loads:
        load.wait()
    for kind, *what in PLAN:
        if kind == "g":
            unit, stage = what
            if stage == 0:
                cols = pl.ds(*GATHER_UNITS[unit][:2])
                full[place.z, place.y, place.x, :, cols] = matrices[:, cols].astype(BF16)
            else:
                gather.settle(unit, stage - 1)
            gather.begin(unit, stage)
        elif kind == "gf":
            gather.settle(what[0], 4)
        elif kind == "s":
            unit, stage = what
            if stage > 0:
                scatter.add(unit, stage - 1)
            if stage < 5:
                scatter.begin(unit, stage)
        else:
            pieces[kind](*what)
    for which in range(2):
        for item in range(items):
            store(which, item).wait()
    gather.drain()
    scatter.drain()
    for turn in (2, 3):
        for item in range(items):
            exchange(turn, item).wait_send()


def run_block(inner, tokens, cotangent, task_mask, group_ids, slab, norm_bias, column_bias):
    rows = tokens.shape[0]
    items, length = group_ids.shape
    slab_rows, cols = slab.shape
    heads = HEAD_COLS // HD
    gather_units, scatter_units = len(GATHER_UNITS), len(SCATTER_UNITS)
    dma = pltpu.SemaphoreType.DMA
    vmem = pltpu.VMEM
    in_vmem = pl.BlockSpec(memory_space=pltpu.VMEM)
    anywhere = pl.BlockSpec(memory_space=pl.ANY)
    return pl.pallas_call(
        functools.partial(block_kernel, inner, items, length),
        out_shape=(
            jax.ShapeDtypeStruct((rows, D), BF16),
            jax.ShapeDtypeStruct((rows, D), F32),
            jax.ShapeDtypeStruct((slab_rows, cols), F32),
            jax.ShapeDtypeStruct((16, D), F32),
        ),
        in_specs=[anywhere, anywhere, in_vmem, in_vmem, anywhere, in_vmem, in_vmem],
        out_specs=(anywhere, anywhere, in_vmem, in_vmem),
        scratch_shapes=[
            vmem((NZ, NY, NX, slab_rows, cols), BF16),
            vmem((NZ, NY, NX, slab_rows, cols), BF16),
            vmem((NZ, 2, slab_rows, LATE_COLS), BF16),
            vmem((NZ, slab_rows, LATE_COLS), BF16),
            vmem((2, slab_rows, LATE_COLS), BF16),
            vmem((2, slab_rows, LATE_COLS), BF16),
            vmem((slab_rows, LATE_COLS), BF16),
            vmem((2, NY, NX, slab_rows, EARLY_COLS), BF16),
            vmem((2, NY, NX, slab_rows, EARLY_COLS), BF16),
            vmem((NY, NX, slab_rows, EARLY_COLS), BF16),
            vmem((2, slab_rows, EARLY_COLS), BF16),
            vmem((slab_rows, EARLY_COLS), BF16),
            vmem((rows, D), BF16),
            vmem((D, rows), BF16),
            vmem((rows, D), BF16),
            vmem((D, rows), BF16),
            vmem((D, rows), BF16),
            vmem((rows, 3 * HEAD_COLS), BF16),
            vmem((rows, 3 * HEAD_COLS), BF16),
            vmem((rows, HEAD_COLS), BF16),
            vmem((rows, HEAD_COLS), BF16),
            vmem((items, length, length), F32),
            vmem((items, heads, length, length), F32),
            vmem((rows, D), F32),
            vmem((rows, UNIT_COLS), F32),
            vmem((rows, UNIT_COLS), BF16),
            vmem((rows, UNIT_COLS), BF16),
            vmem((rows, D), F32),
            vmem((rows, D), BF16),
            vmem((2, rows, D), BF16),
            vmem((2, rows, D), BF16),
            vmem((2, 16, D), F32),
            vmem((NZ, 16, D), F32),
            dma((gather_units, 5)),
            dma((gather_units, 5)),
            dma((scatter_units, 5)),
            dma((scatter_units, 5)),
            dma((4, items)),
            dma((4, items)),
            dma((2 + NZ - 1,)),
            dma((2 + NZ - 1,)),
            vmem((rows, D), BF16),
            vmem((rows, D), BF16),
            vmem((slab_rows, cols), F32),
            vmem((rows, D), BF16),
            vmem((rows, D), F32),
            dma((3,)),
            dma((2, items)),
        ],
        compiler_params=pltpu.CompilerParams(
            collective_id=0, has_side_effects=True, vmem_limit_bytes=60 << 20
        ),
    )(tokens, cotangent, task_mask, group_ids, slab, norm_bias, column_bias)


def adam_update(weight_now, gradient, first_now, second_now, step_rate, weight_decay):
    first_new = BETA_FIRST * first_now + (1.0 - BETA_FIRST) * gradient
    second_new = BETA_SECOND * second_now + (1.0 - BETA_SECOND) * gradient * gradient
    first_fixed = first_new / (1.0 - BETA_FIRST**STEP)
    second_fixed = second_new / (1.0 - BETA_SECOND**STEP)
    weight_new = weight_now - step_rate * (
        first_fixed / (jnp.sqrt(second_fixed) + EPS_ADAM) + weight_decay * weight_now
    )
    return (weight_new, first_new, second_new)


FINISH_PARTS = 2
STATES = 4


def finish_kernel(*refs):
    out_in, dx_in, grad_in, vec_in = refs[:4]
    matrix_in, norm_in, column_in = refs[4:8], refs[8:12], refs[12:16]
    out_res, dx_res = refs[16:18]
    matrix_res, norm_res, column_res = refs[18:23], refs[23:28], refs[28:33]
    grad, mats, fresh, vectors, norms, norm_new = refs[33:39]
    cols, col_new = refs[39:43], refs[43:48]
    dx_held, out_held, pass_sem, in_sem, part_sem, out_sem, end_sem = refs[48:]
    width = grad.shape[1] // FINISH_PARTS
    copy = pltpu.make_async_copy

    def load(part):
        where = pl.ds(part * width, width)
        moves = [copy(grad_in.at[:, where], grad.at[:, where], part_sem.at[part, 0])]
        for spot, source in enumerate(matrix_in):
            moves.append(copy(source.at[:, where], mats.at[spot, :, where], part_sem.at[part, 1 + spot]))
        return moves

    def save(part):
        where = pl.ds(part * width, width)
        moves = [copy(grad.at[:, where], matrix_res[0].at[:, where], out_sem.at[part, 0])]
        for spot in range(STATES):
            moves.append(copy(fresh.at[spot, :, where], matrix_res[1 + spot].at[:, where], out_sem.at[part, 1 + spot]))
        return moves

    loads = [load(part) for part in range(FINISH_PARTS)]
    saves = [save(part) for part in range(FINISH_PARTS)]
    small = [copy(vec_in, vectors, in_sem.at[0])]
    for spot in range(STATES):
        small.append(copy(norm_in[spot], norms.at[spot], in_sem.at[1 + spot]))
        small.append(copy(column_in[spot], cols[spot], in_sem.at[1 + STATES + spot]))
    taken = [copy(dx_in, dx_held, pass_sem.at[0]), copy(out_in, out_held, pass_sem.at[1])]
    passed = [copy(dx_held, dx_res, end_sem.at[0]), copy(out_held, out_res, end_sem.at[1])]
    for move in loads[0] + taken + small:
        move.start()
    for moves in loads[1:]:
        for move in moves:
            move.start()

    def update(gradient, old, rate, decay):
        now, first, second, average = old
        new, first, second = adam_update(now, gradient, first, second, rate, decay)
        return new, first, second, AVERAGE_KEEP * average + (1.0 - AVERAGE_KEEP) * new

    for part in range(FINISH_PARTS):
        for move in loads[part]:
            move.wait()
        where = pl.ds(part * width, width)
        old = [mats[spot, :, where] for spot in range(STATES)]
        for spot, value in enumerate(update(grad[:, where], old, RATE_MATRIX, DECAY_MATRIX)):
            fresh[spot, :, where] = value
        for move in saves[part]:
            move.start()
        if part == 0:
            for move, onward in zip(taken, passed):
                move.wait()
                onward.start()
    for move in small:
        move.wait()
    gradient = vectors[0:6, :]
    norm_new[0] = gradient
    for spot, value in enumerate(update(gradient, [norms[spot] for spot in range(STATES)], RATE_VECTOR, 0.0)):
        norm_new[1 + spot] = value
    for row in range(3):
        where = pl.ds(row * D, D)
        gradient = vectors[6 + row : 7 + row, :]
        col_new[0][where] = gradient.reshape(D)
        old = [ref[where].reshape(1, D) for ref in cols]
        for spot, value in enumerate(update(gradient, old, RATE_VECTOR, 0.0)):
            col_new[1 + spot][where] = value.reshape(D)
    ends = []
    for spot in range(1 + STATES):
        ends.append(copy(norm_new.at[spot], norm_res[spot], end_sem.at[2 + spot]))
        ends.append(copy(col_new[spot], column_res[spot], end_sem.at[3 + STATES + spot]))
    for move in ends:
        move.start()
    for move in sum(saves, []) + passed + ends:
        move.wait()


def finish(output, input_grad, matrix_grad, vectors, matrix_set, norm_set, column_set):
    slab_rows, cols = matrix_grad.shape
    shape, vmem, dma = jax.ShapeDtypeStruct, pltpu.VMEM, pltpu.SemaphoreType.DMA
    norm_bias, column_bias = norm_set[0], column_set[0]
    anywhere = pl.BlockSpec(memory_space=pl.ANY)
    return pl.pallas_call(
        finish_kernel,
        out_shape=[shape(output.shape, output.dtype), shape(input_grad.shape, F32)]
        + [shape(matrix_grad.shape, F32)] * 5
        + [shape(norm_bias.shape, F32)] * 5
        + [shape(column_bias.shape, F32)] * 5,
        in_specs=[anywhere] * 16,
        out_specs=[anywhere] * 17,
        scratch_shapes=[
            vmem((slab_rows, cols), F32),
            vmem((STATES, slab_rows, cols), F32),
            vmem((STATES, slab_rows, cols), F32),
            vmem(vectors.shape, F32),
            vmem((STATES,) + norm_bias.shape, F32),
            vmem((1 + STATES,) + norm_bias.shape, F32),
        ]
        + [vmem(column_bias.shape, F32)] * (2 * STATES + 1)
        + [
            vmem(input_grad.shape, F32),
            vmem(output.shape, output.dtype),
            dma((2,)),
            dma((1 + 2 * STATES,)),
            dma((FINISH_PARTS, 1 + STATES)),
            dma((FINISH_PARTS, 1 + STATES)),
            dma((2 + 2 * (1 + STATES),)),
        ],
        compiler_params=pltpu.CompilerParams(vmem_limit_bytes=60 << 20),
    )(output, input_grad, matrix_grad, vectors, *matrix_set, *norm_set, *column_set)


def local(
    tokens,
    cotangent,
    task_mask,
    group_ids,
    matrices,
    matrix_first,
    matrix_second,
    matrix_average,
    norm_bias,
    norm_first,
    norm_second,
    norm_average,
    column_bias,
    column_first,
    column_second,
    column_average,
):
    inner = lax.axis_size("dp") // OUTER
    groups = [[outer * inner + i for i in range(inner)] for outer in range(OUTER)]
    slab = matrices
    if inner > 1:
        slab = lax.all_gather(
            matrices.astype(BF16), "dp", axis=0, tiled=True, axis_index_groups=groups
        ).astype(F32)
    output, input_grad, matrix_grad, vectors = run_block(
        inner, tokens, cotangent, task_mask, group_ids, slab, norm_bias, column_bias
    )
    if inner > 1:
        matrix_grad = lax.psum_scatter(
            matrix_grad, "dp", scatter_dimension=0, tiled=True, axis_index_groups=groups
        )
        vectors = jnp.sum(lax.all_gather(vectors, "dp", axis=0, axis_index_groups=groups), 0)
    return tuple(
        finish(
            output,
            input_grad,
            matrix_grad,
            vectors,
            (matrices, matrix_first, matrix_second, matrix_average),
            (norm_bias, norm_first, norm_second, norm_average),
            (column_bias, column_first, column_second, column_average),
        )
    )


def solution(mesh):
    placed = (
        P("dp", None),
        P("dp", None),
        P("dp", None),
        P("dp", None),
        P("dp", "mp"),
        P("dp", "mp"),
        P("dp", "mp"),
        P("dp", "mp"),
        P(),
        P(),
        P(),
        P(),
        P("mp"),
        P("mp"),
        P("mp"),
        P("mp"),
    )
    return jax.shard_map(
        local,
        mesh=mesh,
        in_specs=placed,
        out_specs=(
            P("dp", None),
            P("dp", None),
            P("dp", "mp"),
            P("dp", "mp"),
            P("dp", "mp"),
            P("dp", "mp"),
            P("dp", "mp"),
            P(),
            P(),
            P(),
            P(),
            P(),
            P("mp"),
            P("mp"),
            P("mp"),
            P("mp"),
            P("mp"),
        ),
        check_vma=False,
    )
```

```python
import functools

import jax
import jax.numpy as jnp
from jax import lax
from jax.experimental import pallas as pl
from jax.experimental.pallas import tpu as pltpu
from jax.sharding import PartitionSpec as P

MESH = pl.DeviceIdType.MESH

D = 768
HEADS = 12
HD = 64
FF = 3072
STEP = 10


NORM_EPSILON = 1e-06
NEGATIVE = -1e30
GELU_SCALE = 0.7978845608028654
GELU_CUBIC = 0.044715
BETA_FIRST = 0.9
BETA_SECOND = 0.999
EPS_ADAM = 1e-08
RATE_MATRIX = 0.1
RATE_VECTOR = 0.3
DECAY_MATRIX = 0.1
AVERAGE_KEEP = 0.7


NZ, NY, NX = 4, 2, 2
OUTER = NZ * NY * NX
COL_TILE = 256
F32, BF16 = jnp.float32, jnp.bfloat16


class Place:
    def __init__(self, inner):
        index = lax.axis_index("dp")
        outer = index // inner
        self.inner = inner
        self.rest = index % inner
        self.core = lax.axis_index("mp")
        self.x = outer % NX
        self.y = (outer // NX) % NY
        self.z = outer // (NX * NY)
        self.partner_z = self.z + 1 - 2 * (self.z % 2)
        self.near_pair = pl.ds(2 * (self.z // 2), 2)
        self.far_pair = pl.ds(2 - 2 * (self.z // 2), 2)

    def device(self, z, y, x):
        return (((z * NY + y) * NX + x) * self.inner + self.rest, self.core)

    def along_z(self, step):
        return self.device((self.z + step) % NZ, self.y, self.x)

    def across_y(self):
        return self.device(self.z, 1 - self.y, self.x)

    def across_x(self):
        return self.device(self.z, self.y, 1 - self.x)

    def sibling(self):
        return (self.device(self.z, self.y, self.x)[0], 1 - self.core)

    def greet(self):
        barrier = pltpu.get_barrier_semaphore()
        peers = [self.along_z(step) for step in range(1, NZ)]
        peers += [self.across_y(), self.across_x(), self.sibling()]
        for peer in peers:
            pl.semaphore_signal(barrier, inc=1, device_id=peer, device_id_type=MESH)
        pl.semaphore_wait(barrier, len(peers))


def remote(src, dst, send_sem, recv_sem, peer):
    return pltpu.make_async_remote_copy(
        src_ref=src,
        dst_ref=dst,
        send_sem=send_sem,
        recv_sem=recv_sem,
        device_id=peer,
        device_id_type=MESH,
    )


class Mover:
    line = "abc"

    def __init__(self, place, units, full, send_sem, recv_sem):
        self.place, self.units, self.full = place, units, full
        self.send_sem, self.recv_sem = send_sem, recv_sem
        self.inner_z = (place.z == 1) | (place.z == 2)
        self.outer_z = (place.z == 0) | (place.z == 3)

    def stages(self, unit):
        found = []
        route = self.units[unit][2]
        for spot, axis in enumerate(route):
            for name in self.line if axis == "z" else axis:
                found.append((name, route[:spot], route[spot + 1 :]))
        return found

    def peer(self, name):
        p = self.place
        if name == "x":
            return p.across_x()
        if name == "y":
            return p.across_y()
        return p.device(p.partner_z if name in "ac" else NZ - 1 - p.z, p.y, p.x)

    def block(self, unit, whole, z, y, x):
        start, width, _ = self.units[unit]
        index = [slice(None) if name in whole else here for name, here in (("z", z), ("y", y), ("x", x))]
        return tuple(index) + (slice(None), pl.ds(start, width))

    def copy(self, unit, stage, src, dst, name):
        return remote(src, dst, self.send_sem.at[unit, stage], self.recv_sem.at[unit, stage], self.peer(name))

    def begin(self, unit, stage):
        name = self.stages(unit)[stage][0]
        self.guarded(self.sender(name), lambda: self.leaving(unit, stage).start())

    def settle(self, unit, stage):
        name = self.stages(unit)[stage][0]
        self.guarded(self.receiver(name), lambda: self.arriving(unit, stage).wait_recv())

    @staticmethod
    def guarded(condition, action):
        if condition is None:
            action()
        else:
            pl.when(condition)(action)

    def drain(self):
        for unit in range(len(self.units)):
            for stage, (name, _, _) in enumerate(self.stages(unit)):
                self.guarded(self.sender(name), lambda: self.leaving(unit, stage).wait_send())


class Gather(Mover):
    def sender(self, name):
        return self.inner_z if name in "bc" else None

    def receiver(self, name):
        return {"b": self.inner_z, "c": self.outer_z}.get(name)

    def leaving(self, unit, stage):
        p = self.place
        name, before, _ = self.stages(unit)[stage]
        z = {"b": p.near_pair, "c": p.far_pair}.get(name, p.z)
        mine = self.full.at[self.block(unit, before, z, p.y, p.x)]
        return self.copy(unit, stage, mine, mine, name)

    def arriving(self, unit, stage):
        p = self.place
        name, before, _ = self.stages(unit)[stage]
        z = {"a": p.partner_z, "b": p.far_pair, "c": p.far_pair}.get(name, p.z)
        y = 1 - p.y if name == "y" else p.y
        x = 1 - p.x if name == "x" else p.x
        theirs = self.full.at[self.block(unit, before, z, y, x)]
        return self.copy(unit, stage, theirs, theirs, name)


class Scatter(Mover):
    line = "cba"

    def __init__(self, place, units, full, landings, result, send_sem, recv_sem):
        super().__init__(place, units, full, send_sem, recv_sem)
        self.landings, self.result = landings, result

    def sender(self, name):
        return {"b": self.inner_z, "c": self.outer_z}.get(name)

    def receiver(self, name):
        return self.inner_z if name in "bc" else None

    def landing(self, unit, stage):
        _, width, route = self.units[unit]
        got = self.landings[int(route[0] == "z")][stage]
        lead = (slice(None),) * (len(got.shape) - 1)
        return got.at[lead + (pl.ds(LANDING[unit], width),)]

    def leaving(self, unit, stage):
        p = self.place
        name, _, after = self.stages(unit)[stage]
        z = {"a": p.partner_z, "b": p.far_pair, "c": p.far_pair}.get(name, p.z)
        y = 1 - p.y if name == "y" else p.y
        x = 1 - p.x if name == "x" else p.x
        away = self.full.at[self.block(unit, after, z, y, x)]
        return self.copy(unit, stage, away, self.landing(unit, stage), name)

    arriving = leaving

    def add(self, unit, stage):
        p = self.place
        steps = self.stages(unit)
        name, _, after = steps[stage]

        def action():
            self.arriving(unit, stage).wait_recv()
            z = {"b": p.near_pair, "c": p.far_pair}.get(name, p.z)
            part = self.block(unit, after, z, p.y, p.x)
            total = self.full[part].astype(F32) + self.landing(unit, stage)[...].astype(F32)
            if stage + 1 == len(steps):
                start, width, _ = self.units[unit]
                self.result[:, pl.ds(start, width)] = total
            else:
                self.full[part] = total.astype(BF16)

        self.guarded(self.receiver(name), action)


def rows_dot(left, right):
    return jnp.dot(left, right, preferred_element_type=F32)


def dot_rt(left, right):
    return lax.dot_general(left, right, (((1,), (1,)), ((), ())), preferred_element_type=F32)


def dot_lt(left, right):
    return lax.dot_general(left, right, (((0,), (0,)), ((), ())), preferred_element_type=F32)


def normalized(values):
    center = values - jnp.mean(values, -1, keepdims=True)
    spread = jnp.mean(center * center, -1, keepdims=True)
    scale = lax.rsqrt(spread + NORM_EPSILON)
    return center * scale, scale


def total_rows(values):
    return jnp.sum(values, 0, keepdims=True)


GATHER_UNITS = (
    (0, 128, "zxy"),
    (128, 128, "zxy"),
    (256, 128, "zyx"),
    (384, 128, "zxy"),
    (512, 128, "zyx"),
    (640, 128, "zxy"),
    (768, 128, "zxy"),
    (896, 128, "zyx"),
    (1024, 256, "zyx"),
    (1280, 128, "yxz"),
    (1408, 384, "zyx"),
    (1792, 256, "zxy"),
    (2048, 256, "zyx"),
    (2304, 256, "zxy"),
    (2560, 256, "zyx"),
    (2816, 128, "zyx"),
    (2944, 128, "zyx"),
    (3072, 128, "zxy"),
    (3200, 256, "yxz"),
    (3456, 128, "zyx"),
    (3584, 128, "xyz"),
    (3712, 128, "zyx"),
    (3840, 128, "yxz"),
    (3968, 256, "xyz"),
    (4224, 256, "yxz"),
    (4480, 128, "xyz"),
)
SCATTER_UNITS = (
    (3072, 256, "zxy"),
    (3328, 128, "zxy"),
    (3456, 128, "yxz"),
    (3584, 256, "yxz"),
    (3840, 128, "yxz"),
    (3968, 128, "zxy"),
    (4096, 128, "yxz"),
    (4224, 128, "zxy"),
    (4352, 256, "yxz"),
    (1536, 256, "xyz"),
    (1792, 256, "yxz"),
    (2048, 256, "zxy"),
    (2304, 256, "xyz"),
    (2560, 256, "zyx"),
    (2816, 256, "xyz"),
    (1152, 384, "yxz"),
    (0, 128, "xyz"),
    (128, 256, "yxz"),
    (384, 128, "yxz"),
    (512, 128, "xyz"),
    (640, 128, "yxz"),
    (768, 128, "xyz"),
    (896, 128, "zyx"),
    (1024, 128, "xyz"),
)
LANDING = (
    0, 256, 0, 128, 384, 384, 512, 512, 640, 896, 1152, 640,
    1408, 896, 1664, 1920, 2304, 2432, 2688, 2816, 2944, 3072, 1152, 3200,
)
LATE_COLS, EARLY_COLS = 3328, 1280
PLAN = (
    ("g", 0, 0), ("g", 1, 0), ("g", 2, 0), ("g", 3, 0), ("g", 4, 0), ("g", 5, 0), ("g", 6, 0), ("g", 7, 0),
    ("g", 8, 0), ("g", 10, 0), ("g", 11, 0), ("g", 12, 0), ("g", 13, 0), ("g", 14, 0), ("g", 9, 0),
    ("g", 18, 0), ("g", 15, 0), ("g", 20, 0), ("g", 16, 0), ("g", 22, 0), ("g", 23, 0), ("g", 17, 0),
    ("g", 24, 0), ("g", 19, 0), ("g", 25, 0), ("ln1", 0), ("g", 21, 0), ("ln1", 1), ("g", 0, 1), ("caps", 0),
    ("g", 1, 1), ("g", 2, 1), ("tr", 0), ("g", 3, 1), ("g", 4, 1), ("tr", 1), ("g", 5, 1), ("g", 6, 1),
    ("g", 7, 1), ("g", 9, 1), ("g", 18, 1), ("g", 20, 1), ("g", 22, 1), ("g", 8, 1), ("g", 23, 1), ("g", 25, 1),
    ("g", 24, 1), ("g", 10, 1), ("g", 0, 2), ("g", 11, 1), ("g", 1, 2), ("g", 12, 1), ("g", 2, 2), ("g", 13, 1),
    ("g", 3, 2), ("g", 14, 1), ("g", 15, 1), ("g", 4, 2), ("g", 16, 1), ("g", 17, 1), ("g", 5, 2), ("g", 19, 1),
    ("g", 21, 1), ("g", 6, 2), ("g", 0, 3), ("g", 7, 2), ("g", 1, 3), ("g", 9, 2), ("g", 2, 3), ("g", 8, 2),
    ("g", 3, 3), ("g", 4, 3), ("g", 5, 3), ("g", 10, 2), ("g", 6, 3), ("g", 7, 3), ("g", 11, 2), ("g", 0, 4),
    ("g", 9, 3), ("g", 12, 2), ("g", 1, 4), ("g", 2, 4), ("g", 8, 3), ("g", 13, 2), ("g", 3, 4), ("g", 4, 4),
    ("g", 14, 2), ("g", 5, 4), ("g", 10, 3), ("g", 15, 2), ("g", 7, 4), ("g", 16, 2), ("g", 6, 4), ("g", 11, 3),
    ("g", 17, 2), ("g", 19, 2), ("g", 12, 3), ("g", 21, 2), ("g", 13, 3), ("g", 18, 2), ("g", 14, 3),
    ("g", 9, 4), ("g", 15, 3), ("g", 16, 3), ("g", 17, 3), ("g", 19, 3), ("g", 8, 4), ("g", 21, 3),
    ("g", 20, 2), ("g", 18, 3), ("g", 22, 2), ("g", 11, 4), ("g", 23, 2), ("g", 13, 4), ("g", 20, 3),
    ("g", 24, 2), ("g", 17, 4), ("g", 22, 3), ("g", 10, 4), ("g", 25, 2), ("g", 23, 3), ("g", 18, 4), ("gf", 0),
    ("gf", 1), ("gf", 2), ("gf", 3), ("gf", 4), ("gf", 5), ("gf", 6), ("gf", 7), ("gf", 8), ("qkv", 0),
    ("qkv", 1), ("g", 24, 3), ("att", 0, 0), ("g", 12, 4), ("g", 20, 4), ("g", 25, 3), ("att", 0, 1),
    ("att", 0, 2), ("g", 14, 4), ("g", 22, 4), ("att", 1, 0), ("g", 15, 4), ("att", 1, 1), ("g", 16, 4),
    ("att", 1, 2), ("gf", 9), ("gf", 10), ("op0", 0), ("g", 19, 4), ("op0", 1), ("g", 21, 4), ("g", 23, 4),
    ("g", 24, 4), ("ln2", 0), ("ln2", 1), ("tr", 2), ("up", 0), ("g", 25, 4), ("gf", 11), ("up", 1), ("gf", 12),
    ("up", 2), ("gf", 14), ("up", 4), ("gd", 0), ("s", 0, 0), ("gf", 13), ("up", 3), ("gd", 1), ("s", 1, 0),
    ("s", 2, 0), ("gd", 2), ("s", 3, 0), ("gd", 3), ("s", 4, 0), ("s", 5, 0), ("gf", 15), ("gf", 16), ("up", 5),
    ("gd", 4), ("gd", 5), ("s", 6, 0), ("s", 7, 0), ("gf", 17), ("gf", 18), ("pre", 0), ("s", 9, 0), ("gf", 19),
    ("pre", 1), ("s", 8, 0), ("s", 2, 1), ("gf", 22), ("gf", 23), ("pre", 3), ("s", 12, 0), ("gf", 20),
    ("gf", 21), ("pre", 2), ("s", 11, 0), ("gf", 24), ("pre", 4), ("s", 0, 1), ("gf", 25), ("pre", 5),
    ("s", 3, 1), ("s", 10, 0), ("s", 13, 0), ("s", 1, 1), ("s", 14, 0), ("da2", 0), ("da2", 1), ("s", 9, 1),
    ("s", 4, 1), ("s", 5, 1), ("s", 2, 2), ("s", 6, 1), ("s", 7, 1), ("s", 0, 2), ("ln2b", 0), ("s", 12, 1),
    ("ln2b", 1), ("s", 1, 2), ("s", 3, 2), ("s", 8, 1), ("s", 11, 1), ("gout", 0), ("s", 5, 2), ("s", 15, 0),
    ("do", 0), ("do", 1), ("attb", 0, 0), ("s", 7, 2), ("s", 10, 1), ("s", 13, 1), ("s", 2, 3), ("s", 14, 1),
    ("attb", 0, 1), ("s", 4, 2), ("s", 6, 2), ("s", 0, 3), ("s", 9, 2), ("attb", 0, 2), ("s", 1, 3),
    ("s", 11, 2), ("s", 3, 3), ("s", 8, 2), ("s", 12, 2), ("attb", 1, 0), ("s", 5, 3), ("s", 10, 2),
    ("s", 7, 3), ("attb", 1, 1), ("s", 0, 4), ("s", 1, 4), ("s", 4, 3), ("s", 6, 3), ("s", 13, 2), ("s", 2, 4),
    ("s", 9, 3), ("attb", 1, 2), ("s", 3, 4), ("s", 5, 4), ("s", 7, 4), ("s", 11, 3), ("s", 15, 1), ("gp", 0),
    ("s", 4, 4), ("s", 0, 5), ("s", 6, 4), ("s", 8, 3), ("s", 1, 5), ("s", 14, 2), ("s", 12, 3), ("s", 16, 0),
    ("s", 17, 0), ("gp", 1), ("s", 5, 5), ("s", 7, 5), ("s", 9, 4), ("s", 10, 3), ("s", 18, 0), ("s", 19, 0),
    ("s", 20, 0), ("gp", 2), ("s", 11, 4), ("s", 21, 0), ("s", 22, 0), ("s", 23, 0), ("da1", 0), ("s", 2, 5),
    ("s", 13, 3), ("da1", 1), ("s", 3, 5), ("s", 8, 4), ("s", 4, 5), ("op2", 0), ("s", 6, 5), ("s", 12, 4),
    ("s", 15, 2), ("s", 14, 3), ("op2", 1), ("s", 9, 5), ("s", 10, 4), ("s", 16, 1), ("s", 17, 1), ("s", 22, 1),
    ("s", 8, 5), ("ln1b", 0), ("s", 12, 5), ("s", 14, 4), ("s", 18, 1), ("s", 19, 1), ("ln1b", 1), ("s", 10, 5),
    ("s", 15, 3), ("s", 21, 1), ("s", 20, 1), ("op2s", 0), ("s", 11, 5), ("vec", 0), ("s", 22, 2), ("s", 14, 5),
    ("s", 13, 4), ("s", 23, 1), ("s", 16, 2), ("s", 19, 2), ("s", 17, 2), ("s", 15, 4), ("s", 21, 2),
    ("s", 18, 2), ("s", 22, 3), ("s", 20, 2), ("s", 16, 3), ("s", 23, 2), ("vec", 1), ("s", 13, 5), ("fout", 0),
    ("s", 19, 3), ("fout", 1), ("s", 17, 3), ("s", 15, 5), ("s", 22, 4), ("s", 21, 3), ("s", 16, 4),
    ("s", 18, 3), ("s", 20, 3), ("s", 19, 4), ("s", 23, 3), ("vec", 2), ("s", 22, 5), ("s", 17, 4),
    ("s", 16, 5), ("s", 21, 4), ("s", 18, 4), ("s", 20, 4), ("s", 19, 5), ("s", 23, 4), ("s", 17, 5),
    ("s", 21, 5), ("s", 18, 5), ("s", 20, 5), ("vec", 3), ("s", 23, 5),
)

HEAD_COLS, UNIT_COLS = 384, 1536
Q0, K0, V0, O0, U0, W0 = 0, 384, 768, 1152, 1536, 3072


def block_kernel(
    inner, items, length, tokens_hbm, cotangent_hbm, task_mask, group_ids, matrices_hbm, norm, column, *rest
):
    (out_hbm, input_grad_hbm, matrix_grad, vectors) = rest[:4]
    (full, grads) = rest[4:6]
    landings = (rest[6:11], rest[11:16])
    (act_one, act_one_t, act_two, act_two_t, cot_t, proj, grad_proj, heads, grad_heads) = rest[16:25]
    (caps, probs, residual, slope, hidden, grad_pre, grad_res, grad_low, ex_send, ex_recv) = rest[25:35]
    (vec_got, vec_z, g_send, g_recv, s_send, s_recv, es, er, vs, vr) = rest[35:45]
    (tokens, cotangent, matrices, out, input_grad, in_sem, out_sem) = rest[45:]
    loads = [
        pltpu.make_async_copy(source, target, in_sem.at[spot])
        for spot, (source, target) in enumerate(
            ((matrices_hbm, matrices), (tokens_hbm, tokens), (cotangent_hbm, cotangent))
        )
    ]
    for load in loads:
        load.start()
    place = Place(inner)
    gather = Gather(place, GATHER_UNITS, full, g_send, g_recv)
    scatter = Scatter(place, SCATTER_UNITS, grads, landings, matrix_grad, s_send, s_recv)

    def weight(start, width):
        return full[:, :, :, :, pl.ds(start, width)].reshape(D, width)

    def put_grad(start, width, value):
        grads[:, :, :, :, pl.ds(start, width)] = value.astype(BF16).reshape(grads.shape[:4] + (width,))

    def rows_of(item):
        return pl.ds(item * length, length)

    def store(which, item):
        part = rows_of(item)
        source, target = ((out, out_hbm), (input_grad, input_grad_hbm))[which]
        return pltpu.make_async_copy(source.at[part], target.at[part], out_sem.at[which, item])

    def add_vector(row, first, value):
        cols = pl.ds(first, value.shape[1])
        vectors[row : row + 1, cols] = vectors[row : row + 1, cols] + value

    def exchange(turn, item):
        part = rows_of(item)
        return remote(
            ex_send.at[turn % 2, part],
            ex_recv.at[turn % 2, part],
            es.at[turn, item],
            er.at[turn, item],
            place.sibling(),
        )

    def fill_part(turn, item, value):
        if turn >= 2:
            exchange(turn - 2, item).wait_send()
        ex_send[turn % 2, rows_of(item)] = value.astype(BF16)

    def both(turn, item):
        exchange(turn, item).wait_recv()
        part = rows_of(item)
        return ex_send[turn % 2, part].astype(F32) + ex_recv[turn % 2, part].astype(F32)

    def norm_one(item):
        part = rows_of(item)
        unit_x, _ = normalized(tokens[part].astype(F32))
        act_one[part] = (unit_x * norm[0:1] + norm[1:2]).astype(BF16)
        add_vector(5, 0, total_rows(cotangent[part].astype(F32)))

    def masks(_):
        key_index = lax.broadcasted_iota(jnp.int32, (length, length), 0)
        query_index = lax.broadcasted_iota(jnp.int32, (length, length), 1)
        same = key_index == query_index
        slots = task_mask.shape[1]
        slot_same = lax.broadcasted_iota(jnp.int32, (slots, slots), 0) == lax.broadcasted_iota(
            jnp.int32, (slots, slots), 1
        )
        for item in range(items):
            query_ids = group_ids[item : item + 1, :]
            key_ids = jnp.sum(jnp.where(same, query_ids, 0), axis=1, keepdims=True)
            filled = jnp.sum(jnp.where(slot_same, task_mask[item : item + 1, :], 0), axis=1, keepdims=True)
            live = jnp.concatenate([filled, jnp.ones((length - slots, 1), jnp.int32)], axis=0)
            odd_key = jnp.where((key_ids == 0) | (key_ids % 2 == 1), 1, 0)
            earlier = (odd_key == 1) & (key_ids <= query_ids)
            visible = (earlier | (key_ids == query_ids)) & (live == 1)
            caps[item] = jnp.where(visible | same, 3.0e38, NEGATIVE)

    def turned(which):
        source, target = ((act_one, act_one_t), (cotangent, cot_t), (act_two, act_two_t))[which]
        target[...] = source[...].T

    def project(item):
        part = rows_of(item)
        for start, scale, bias in ((Q0, HD**-0.5, 0), (K0, 1.0, None), (V0, 1.0, HEAD_COLS)):
            value = rows_dot(act_one[part], weight(start, HEAD_COLS))
            if bias is not None:
                value = value + column[pl.ds(bias, HEAD_COLS)].reshape(1, HEAD_COLS)
            value = value.astype(BF16)
            if scale != 1.0:
                value = value * jnp.asarray(scale, BF16)
            proj[part, start : start + HEAD_COLS] = value

    lane = lax.broadcasted_iota(jnp.int32, (length, 128), 1)
    first_half = lane < HD

    def lanes(start, pair):
        return pl.ds(start + pair * 128, 128)

    def attend(item, pair):
        part = rows_of(item)
        query, key, value = (proj[part, lanes(start, pair)] for start in (Q0, K0, V0))
        sides = []
        for side in range(2):
            own = first_half if side == 0 else ~first_half
            scores = dot_rt(jnp.where(own, key, jnp.zeros_like(key)), query)
            scores = jnp.minimum(scores, caps[item])
            weights = jnp.exp(scores - jnp.max(scores, 0, keepdims=True))
            prob = weights * (1.0 / jnp.sum(weights, 0, keepdims=True))
            probs[item, pair * 2 + side] = prob
            sides.append(dot_lt(prob.astype(BF16), value))
        heads[part, lanes(0, pair)] = jnp.where(first_half, sides[0], sides[1]).astype(BF16)

    def heads_out(item):
        fill_part(0, item, dot_rt(heads[rows_of(item)], weight(O0, HEAD_COLS)))
        exchange(0, item).start()

    def norm_two(item):
        part = rows_of(item)
        value = tokens[part].astype(F32) + both(0, item) + norm[4:5]
        residual[part] = value
        unit_x, _ = normalized(value)
        act_two[part] = (unit_x * norm[2:3] + norm[3:4]).astype(BF16)

    def up(index):
        start = index * COL_TILE
        cols = pl.ds(start, COL_TILE)
        unit = rows_dot(act_two[...], weight(U0 + start, COL_TILE))
        unit = unit + column[pl.ds(2 * HEAD_COLS + start, COL_TILE)].reshape(1, COL_TILE)
        square = unit * unit
        bent = jnp.tanh(unit * (GELU_SCALE + (GELU_SCALE * GELU_CUBIC) * square))
        half = 0.5 * (1.0 + bent)
        hidden[:, cols] = (unit * half).astype(BF16)
        slope[:, cols] = half + 0.5 * unit * (1.0 - bent * bent) * (
            GELU_SCALE + (3.0 * GELU_SCALE * GELU_CUBIC) * square
        )

    def down_grad(index):
        start = index * COL_TILE
        put_grad(W0 + start, COL_TILE, rows_dot(cot_t[...], hidden[:, pl.ds(start, COL_TILE)]))

    def pre_grad(index):
        start = index * COL_TILE
        cols = pl.ds(start, COL_TILE)
        value = rows_dot(cotangent[...], weight(W0 + start, COL_TILE))
        low = (value * slope[:, cols]).astype(BF16)
        grad_pre[:, cols] = low
        row, first = divmod(2 * HEAD_COLS + start, D)
        add_vector(6 + row, first, total_rows(low.astype(F32)))
        put_grad(U0 + start, COL_TILE, rows_dot(act_two_t[...], low))

    def units_back(item):
        fill_part(1, item, dot_rt(grad_pre[rows_of(item)], weight(U0, UNIT_COLS)))
        exchange(1, item).start()

    def norm_back(incoming, values, gain):
        unit_x, scale = normalized(values)
        pulled = incoming * gain
        inner_mean = jnp.mean(pulled, -1, keepdims=True)
        cross_mean = jnp.mean(pulled * unit_x, -1, keepdims=True)
        return scale * (pulled - inner_mean - unit_x * cross_mean), total_rows(incoming * unit_x), total_rows(incoming)

    def norm_two_back(item):
        part = rows_of(item)
        value, gain_sum, shift_sum = norm_back(both(1, item), residual[part], norm[2:3])
        value = cotangent[part].astype(F32) + value
        grad_res[part] = value
        grad_low[part] = value.astype(BF16)
        add_vector(2, 0, gain_sum)
        add_vector(3, 0, shift_sum)
        add_vector(4, 0, total_rows(value))

    def out_grad(_):
        put_grad(O0, HEAD_COLS, dot_lt(grad_low[...], heads[...]))

    def heads_back(item):
        part = rows_of(item)
        grad_heads[part] = rows_dot(grad_low[part], weight(O0, HEAD_COLS)).astype(BF16)

    def attend_back(item, pair):
        part = rows_of(item)
        query, key, value = (proj[part, lanes(start, pair)] for start in (Q0, K0, V0))
        grad = grad_heads[part, lanes(0, pair)]
        sides = []
        for side in range(2):
            own = first_half if side == 0 else ~first_half
            prob = probs[item, pair * 2 + side]
            grad_prob = dot_rt(jnp.where(own, value, jnp.zeros_like(value)), grad)
            inner_sum = jnp.sum(prob * grad_prob, 0, keepdims=True)
            low = (prob * (grad_prob - inner_sum)).astype(BF16)
            sides.append(
                (dot_lt(low, key) * (HD**-0.5), rows_dot(low, query), rows_dot(prob.astype(BF16), grad))
            )
        for start, left, right in zip((Q0, K0, V0), sides[0], sides[1]):
            low = jnp.where(first_half, left, right).astype(BF16)
            grad_proj[part, lanes(start, pair)] = low
            if start != K0:
                add_vector(6, (0 if start == Q0 else HEAD_COLS) + pair * 128, total_rows(low.astype(F32)))

    def proj_grad(index):
        cols = pl.ds(index * HEAD_COLS, HEAD_COLS)
        put_grad(index * HEAD_COLS, HEAD_COLS, rows_dot(act_one_t[...], grad_proj[:, cols]))

    def heads_in(item):
        fill_part(2, item, dot_rt(grad_proj[rows_of(item)], weight(Q0, 3 * HEAD_COLS)))
        exchange(2, item).start()

    def units_out(item):
        fill_part(3, item, dot_rt(hidden[rows_of(item)], weight(W0, UNIT_COLS)))

    def send_units(_):
        for item in range(items):
            exchange(3, item).start()

    def norm_one_back(item):
        part = rows_of(item)
        value, gain_sum, shift_sum = norm_back(both(2, item), tokens[part].astype(F32), norm[0:1])
        input_grad[part] = grad_res[part] + value
        store(1, item).start()
        add_vector(0, 0, gain_sum)
        add_vector(1, 0, shift_sum)

    def finish_out(item):
        part = rows_of(item)
        out[part] = (residual[part] + both(3, item) + norm[5:6]).astype(BF16)
        store(0, item).start()

    def vec_copy(stage, owner_z=None, step=0):
        if stage < 2:
            peer = (place.across_x(), place.across_y())[stage]
            return remote(vectors, vec_got.at[stage], vs.at[stage], vr.at[stage], peer)
        block = vec_z.at[owner_z]
        return remote(block, block, vs.at[1 + step], vr.at[1 + step], place.along_z(step))

    def small_sums(stage):
        if stage in (1, 2):
            vec_copy(stage - 1).wait()
            vectors[...] = vectors[...] + vec_got[stage - 1]
        if stage < 2:
            vec_copy(stage).start()
        elif stage == 2:
            vec_z[place.z] = vectors[...]
            for step in range(1, NZ):
                vec_copy(2, place.z, step).start()
        else:
            for step in range(1, NZ):
                vec_copy(2, (place.z - step) % NZ, step).wait_recv()
                vec_copy(2, place.z, step).wait_send()
            vectors[...] = (vec_z[0] + vec_z[1]) + (vec_z[2] + vec_z[3])

    pieces = {
        "ln1": norm_one,
        "caps": masks,
        "tr": turned,
        "qkv": project,
        "att": attend,
        "op0": heads_out,
        "ln2": norm_two,
        "up": up,
        "gd": down_grad,
        "pre": pre_grad,
        "da2": units_back,
        "ln2b": norm_two_back,
        "gout": out_grad,
        "do": heads_back,
        "attb": attend_back,
        "gp": proj_grad,
        "da1": heads_in,
        "op2": units_out,
        "op2s": send_units,
        "ln1b": norm_one_back,
        "fout": finish_out,
        "vec": small_sums,
    }

    vectors[...] = jnp.zeros_like(vectors)
    place.greet()
    for load in loads:
        load.wait()
    for kind, *what in PLAN:
        if kind == "g":
            unit, stage = what
            if stage == 0:
                cols = pl.ds(*GATHER_UNITS[unit][:2])
                full[place.z, place.y, place.x, :, cols] = matrices[:, cols].astype(BF16)
            else:
                gather.settle(unit, stage - 1)
            gather.begin(unit, stage)
        elif kind == "gf":
            gather.settle(what[0], 4)
        elif kind == "s":
            unit, stage = what
            if stage > 0:
                scatter.add(unit, stage - 1)
            if stage < 5:
                scatter.begin(unit, stage)
        else:
            pieces[kind](*what)
    for which in range(2):
        for item in range(items):
            store(which, item).wait()
    gather.drain()
    scatter.drain()
    for turn in (2, 3):
        for item in range(items):
            exchange(turn, item).wait_send()


def run_block(inner, tokens, cotangent, task_mask, group_ids, slab, norm_bias, column_bias):
    rows = tokens.shape[0]
    items, length = group_ids.shape
    slab_rows, cols = slab.shape
    heads = HEAD_COLS // HD
    gather_units, scatter_units = len(GATHER_UNITS), len(SCATTER_UNITS)
    dma = pltpu.SemaphoreType.DMA
    vmem = pltpu.VMEM
    in_vmem = pl.BlockSpec(memory_space=pltpu.VMEM)
    anywhere = pl.BlockSpec(memory_space=pl.ANY)
    return pl.pallas_call(
        functools.partial(block_kernel, inner, items, length),
        out_shape=(
            jax.ShapeDtypeStruct((rows, D), BF16),
            jax.ShapeDtypeStruct((rows, D), F32),
            jax.ShapeDtypeStruct((slab_rows, cols), F32),
            jax.ShapeDtypeStruct((16, D), F32),
        ),
        in_specs=[anywhere, anywhere, in_vmem, in_vmem, anywhere, in_vmem, in_vmem],
        out_specs=(anywhere, anywhere, in_vmem, in_vmem),
        scratch_shapes=[
            vmem((NZ, NY, NX, slab_rows, cols), BF16),
            vmem((NZ, NY, NX, slab_rows, cols), BF16),
            vmem((NZ, 2, slab_rows, LATE_COLS), BF16),
            vmem((NZ, slab_rows, LATE_COLS), BF16),
            vmem((2, slab_rows, LATE_COLS), BF16),
            vmem((2, slab_rows, LATE_COLS), BF16),
            vmem((slab_rows, LATE_COLS), BF16),
            vmem((2, NY, NX, slab_rows, EARLY_COLS), BF16),
            vmem((2, NY, NX, slab_rows, EARLY_COLS), BF16),
            vmem((NY, NX, slab_rows, EARLY_COLS), BF16),
            vmem((2, slab_rows, EARLY_COLS), BF16),
            vmem((slab_rows, EARLY_COLS), BF16),
            vmem((rows, D), BF16),
            vmem((D, rows), BF16),
            vmem((rows, D), BF16),
            vmem((D, rows), BF16),
            vmem((D, rows), BF16),
            vmem((rows, 3 * HEAD_COLS), BF16),
            vmem((rows, 3 * HEAD_COLS), BF16),
            vmem((rows, HEAD_COLS), BF16),
            vmem((rows, HEAD_COLS), BF16),
            vmem((items, length, length), F32),
            vmem((items, heads, length, length), F32),
            vmem((rows, D), F32),
            vmem((rows, UNIT_COLS), F32),
            vmem((rows, UNIT_COLS), BF16),
            vmem((rows, UNIT_COLS), BF16),
            vmem((rows, D), F32),
            vmem((rows, D), BF16),
            vmem((2, rows, D), BF16),
            vmem((2, rows, D), BF16),
            vmem((2, 16, D), F32),
            vmem((NZ, 16, D), F32),
            dma((gather_units, 5)),
            dma((gather_units, 5)),
            dma((scatter_units, 5)),
            dma((scatter_units, 5)),
            dma((4, items)),
            dma((4, items)),
            dma((2 + NZ - 1,)),
            dma((2 + NZ - 1,)),
            vmem((rows, D), BF16),
            vmem((rows, D), BF16),
            vmem((slab_rows, cols), F32),
            vmem((rows, D), BF16),
            vmem((rows, D), F32),
            dma((3,)),
            dma((2, items)),
        ],
        compiler_params=pltpu.CompilerParams(
            collective_id=0, has_side_effects=True, vmem_limit_bytes=60 << 20
        ),
    )(tokens, cotangent, task_mask, group_ids, slab, norm_bias, column_bias)


def adam_update(weight_now, gradient, first_now, second_now, step_rate, weight_decay):
    first_new = BETA_FIRST * first_now + (1.0 - BETA_FIRST) * gradient
    second_new = BETA_SECOND * second_now + (1.0 - BETA_SECOND) * gradient * gradient
    first_fixed = first_new / (1.0 - BETA_FIRST**STEP)
    second_fixed = second_new / (1.0 - BETA_SECOND**STEP)
    weight_new = weight_now - step_rate * (
        first_fixed / (jnp.sqrt(second_fixed) + EPS_ADAM) + weight_decay * weight_now
    )
    return (weight_new, first_new, second_new)


FINISH_PARTS = 2
STATES = 4


def finish_kernel(*refs):
    out_in, dx_in, grad_in, vec_in = refs[:4]
    matrix_in, norm_in, column_in = refs[4:8], refs[8:12], refs[12:16]
    out_res, dx_res = refs[16:18]
    matrix_res, norm_res, column_res = refs[18:23], refs[23:28], refs[28:33]
    grad, mats, fresh, vectors, norms, norm_new = refs[33:39]
    cols, col_new = refs[39:43], refs[43:48]
    dx_held, out_held, pass_sem, in_sem, part_sem, out_sem, end_sem = refs[48:]
    width = grad.shape[1] // FINISH_PARTS
    copy = pltpu.make_async_copy

    def load(part):
        where = pl.ds(part * width, width)
        moves = [copy(grad_in.at[:, where], grad.at[:, where], part_sem.at[part, 0])]
        for spot, source in enumerate(matrix_in):
            moves.append(copy(source.at[:, where], mats.at[spot, :, where], part_sem.at[part, 1 + spot]))
        return moves

    def save(part):
        where = pl.ds(part * width, width)
        moves = [copy(grad.at[:, where], matrix_res[0].at[:, where], out_sem.at[part, 0])]
        for spot in range(STATES):
            moves.append(copy(fresh.at[spot, :, where], matrix_res[1 + spot].at[:, where], out_sem.at[part, 1 + spot]))
        return moves

    loads = [load(part) for part in range(FINISH_PARTS)]
    saves = [save(part) for part in range(FINISH_PARTS)]
    small = [copy(vec_in, vectors, in_sem.at[0])]
    for spot in range(STATES):
        small.append(copy(norm_in[spot], norms.at[spot], in_sem.at[1 + spot]))
        small.append(copy(column_in[spot], cols[spot], in_sem.at[1 + STATES + spot]))
    taken = [copy(dx_in, dx_held, pass_sem.at[0]), copy(out_in, out_held, pass_sem.at[1])]
    passed = [copy(dx_held, dx_res, end_sem.at[0]), copy(out_held, out_res, end_sem.at[1])]
    for move in loads[0] + taken + small:
        move.start()
    for moves in loads[1:]:
        for move in moves:
            move.start()

    def update(gradient, old, rate, decay):
        now, first, second, average = old
        new, first, second = adam_update(now, gradient, first, second, rate, decay)
        return new, first, second, AVERAGE_KEEP * average + (1.0 - AVERAGE_KEEP) * new

    for part in range(FINISH_PARTS):
        for move in loads[part]:
            move.wait()
        where = pl.ds(part * width, width)
        old = [mats[spot, :, where] for spot in range(STATES)]
        for spot, value in enumerate(update(grad[:, where], old, RATE_MATRIX, DECAY_MATRIX)):
            fresh[spot, :, where] = value
        for move in saves[part]:
            move.start()
        if part == 0:
            for move, onward in zip(taken, passed):
                move.wait()
                onward.start()
    for move in small:
        move.wait()
    gradient = vectors[0:6, :]
    norm_new[0] = gradient
    for spot, value in enumerate(update(gradient, [norms[spot] for spot in range(STATES)], RATE_VECTOR, 0.0)):
        norm_new[1 + spot] = value
    for row in range(3):
        where = pl.ds(row * D, D)
        gradient = vectors[6 + row : 7 + row, :]
        col_new[0][where] = gradient.reshape(D)
        old = [ref[where].reshape(1, D) for ref in cols]
        for spot, value in enumerate(update(gradient, old, RATE_VECTOR, 0.0)):
            col_new[1 + spot][where] = value.reshape(D)
    ends = []
    for spot in range(1 + STATES):
        ends.append(copy(norm_new.at[spot], norm_res[spot], end_sem.at[2 + spot]))
        ends.append(copy(col_new[spot], column_res[spot], end_sem.at[3 + STATES + spot]))
    for move in ends:
        move.start()
    for move in sum(saves, []) + passed + ends:
        move.wait()


def finish(output, input_grad, matrix_grad, vectors, matrix_set, norm_set, column_set):
    slab_rows, cols = matrix_grad.shape
    shape, vmem, dma = jax.ShapeDtypeStruct, pltpu.VMEM, pltpu.SemaphoreType.DMA
    norm_bias, column_bias = norm_set[0], column_set[0]
    anywhere = pl.BlockSpec(memory_space=pl.ANY)
    return pl.pallas_call(
        finish_kernel,
        out_shape=[shape(output.shape, output.dtype), shape(input_grad.shape, F32)]
        + [shape(matrix_grad.shape, F32)] * 5
        + [shape(norm_bias.shape, F32)] * 5
        + [shape(column_bias.shape, F32)] * 5,
        in_specs=[anywhere] * 16,
        out_specs=[anywhere] * 17,
        scratch_shapes=[
            vmem((slab_rows, cols), F32),
            vmem((STATES, slab_rows, cols), F32),
            vmem((STATES, slab_rows, cols), F32),
            vmem(vectors.shape, F32),
            vmem((STATES,) + norm_bias.shape, F32),
            vmem((1 + STATES,) + norm_bias.shape, F32),
        ]
        + [vmem(column_bias.shape, F32)] * (2 * STATES + 1)
        + [
            vmem(input_grad.shape, F32),
            vmem(output.shape, output.dtype),
            dma((2,)),
            dma((1 + 2 * STATES,)),
            dma((FINISH_PARTS, 1 + STATES)),
            dma((FINISH_PARTS, 1 + STATES)),
            dma((2 + 2 * (1 + STATES),)),
        ],
        compiler_params=pltpu.CompilerParams(vmem_limit_bytes=60 << 20),
    )(output, input_grad, matrix_grad, vectors, *matrix_set, *norm_set, *column_set)


def local(
    tokens,
    cotangent,
    task_mask,
    group_ids,
    matrices,
    matrix_first,
    matrix_second,
    matrix_average,
    norm_bias,
    norm_first,
    norm_second,
    norm_average,
    column_bias,
    column_first,
    column_second,
    column_average,
):
    inner = lax.axis_size("dp") // OUTER
    groups = [[outer * inner + i for i in range(inner)] for outer in range(OUTER)]
    slab = matrices
    if inner > 1:
        slab = lax.all_gather(
            matrices.astype(BF16), "dp", axis=0, tiled=True, axis_index_groups=groups
        ).astype(F32)
    output, input_grad, matrix_grad, vectors = run_block(
        inner, tokens, cotangent, task_mask, group_ids, slab, norm_bias, column_bias
    )
    if inner > 1:
        matrix_grad = lax.psum_scatter(
            matrix_grad, "dp", scatter_dimension=0, tiled=True, axis_index_groups=groups
        )
        vectors = jnp.sum(lax.all_gather(vectors, "dp", axis=0, axis_index_groups=groups), 0)
    return tuple(
        finish(
            output,
            input_grad,
            matrix_grad,
            vectors,
            (matrices, matrix_first, matrix_second, matrix_average),
            (norm_bias, norm_first, norm_second, norm_average),
            (column_bias, column_first, column_second, column_average),
        )
    )


def solution(mesh):
    placed = (
        P("dp", None),
        P("dp", None),
        P("dp", None),
        P("dp", None),
        P("dp", "mp"),
        P("dp", "mp"),
        P("dp", "mp"),
        P("dp", "mp"),
        P(),
        P(),
        P(),
        P(),
        P("mp"),
        P("mp"),
        P("mp"),
        P("mp"),
    )
    return jax.shard_map(
        local,
        mesh=mesh,
        in_specs=placed,
        out_specs=(
            P("dp", None),
            P("dp", None),
            P("dp", "mp"),
            P("dp", "mp"),
            P("dp", "mp"),
            P("dp", "mp"),
            P("dp", "mp"),
            P(),
            P(),
            P(),
            P(),
            P(),
            P("mp"),
            P("mp"),
            P("mp"),
            P("mp"),
            P("mp"),
        ),
        check_vma=False,
    )
```

```python
import functools

import jax
import jax.numpy as jnp
from jax import lax
from jax.experimental import pallas as pl
from jax.experimental.pallas import tpu as pltpu
from jax.sharding import PartitionSpec as P

MESH = pl.DeviceIdType.MESH

D = 768
HEADS = 12
HD = 64
FF = 3072
STEP = 10


NORM_EPSILON = 1e-06
NEGATIVE = -1e30
GELU_SCALE = 0.7978845608028654
GELU_CUBIC = 0.044715
BETA_FIRST = 0.9
BETA_SECOND = 0.999
EPS_ADAM = 1e-08
RATE_MATRIX = 0.1
RATE_VECTOR = 0.3
DECAY_MATRIX = 0.1
AVERAGE_KEEP = 0.7


NZ, NY, NX = 4, 2, 2
OUTER = NZ * NY * NX
COL_TILE = 256
F32, BF16 = jnp.float32, jnp.bfloat16


class Place:
    def __init__(self, inner):
        index = lax.axis_index("dp")
        outer = index // inner
        self.inner = inner
        self.rest = index % inner
        self.core = lax.axis_index("mp")
        self.x = outer % NX
        self.y = (outer // NX) % NY
        self.z = outer // (NX * NY)
        self.partner_z = self.z + 1 - 2 * (self.z % 2)
        self.near_pair = pl.ds(2 * (self.z // 2), 2)
        self.far_pair = pl.ds(2 - 2 * (self.z // 2), 2)

    def device(self, z, y, x):
        return (((z * NY + y) * NX + x) * self.inner + self.rest, self.core)

    def along_z(self, step):
        return self.device((self.z + step) % NZ, self.y, self.x)

    def across_y(self):
        return self.device(self.z, 1 - self.y, self.x)

    def across_x(self):
        return self.device(self.z, self.y, 1 - self.x)

    def sibling(self):
        return (self.device(self.z, self.y, self.x)[0], 1 - self.core)

    def greet(self):
        barrier = pltpu.get_barrier_semaphore()
        peers = [self.along_z(step) for step in range(1, NZ)]
        peers += [self.across_y(), self.across_x(), self.sibling()]
        for peer in peers:
            pl.semaphore_signal(barrier, inc=1, device_id=peer, device_id_type=MESH)
        pl.semaphore_wait(barrier, len(peers))


def remote(src, dst, send_sem, recv_sem, peer):
    return pltpu.make_async_remote_copy(
        src_ref=src,
        dst_ref=dst,
        send_sem=send_sem,
        recv_sem=recv_sem,
        device_id=peer,
        device_id_type=MESH,
    )


class Mover:
    line = "abc"

    def __init__(self, place, units, full, send_sem, recv_sem):
        self.place, self.units, self.full = place, units, full
        self.send_sem, self.recv_sem = send_sem, recv_sem
        self.inner_z = (place.z == 1) | (place.z == 2)
        self.outer_z = (place.z == 0) | (place.z == 3)

    def stages(self, unit):
        found = []
        route = self.units[unit][2]
        for spot, axis in enumerate(route):
            for name in self.line if axis == "z" else axis:
                found.append((name, route[:spot], route[spot + 1 :]))
        return found

    def peer(self, name):
        p = self.place
        if name == "x":
            return p.across_x()
        if name == "y":
            return p.across_y()
        return p.device(p.partner_z if name in "ac" else NZ - 1 - p.z, p.y, p.x)

    def block(self, unit, whole, z, y, x):
        start, width, _ = self.units[unit]
        index = [slice(None) if name in whole else here for name, here in (("z", z), ("y", y), ("x", x))]
        return tuple(index) + (slice(None), pl.ds(start, width))

    def copy(self, unit, stage, src, dst, name):
        return remote(src, dst, self.send_sem.at[unit, stage], self.recv_sem.at[unit, stage], self.peer(name))

    def begin(self, unit, stage):
        name = self.stages(unit)[stage][0]
        self.guarded(self.sender(name), lambda: self.leaving(unit, stage).start())

    def settle(self, unit, stage):
        name = self.stages(unit)[stage][0]
        self.guarded(self.receiver(name), lambda: self.arriving(unit, stage).wait_recv())

    @staticmethod
    def guarded(condition, action):
        if condition is None:
            action()
        else:
            pl.when(condition)(action)

    def drain(self):
        for unit in range(len(self.units)):
            for stage, (name, _, _) in enumerate(self.stages(unit)):
                self.guarded(self.sender(name), lambda: self.leaving(unit, stage).wait_send())


class Gather(Mover):
    def sender(self, name):
        return self.inner_z if name in "bc" else None

    def receiver(self, name):
        return {"b": self.inner_z, "c": self.outer_z}.get(name)

    def leaving(self, unit, stage):
        p = self.place
        name, before, _ = self.stages(unit)[stage]
        z = {"b": p.near_pair, "c": p.far_pair}.get(name, p.z)
        mine = self.full.at[self.block(unit, before, z, p.y, p.x)]
        return self.copy(unit, stage, mine, mine, name)

    def arriving(self, unit, stage):
        p = self.place
        name, before, _ = self.stages(unit)[stage]
        z = {"a": p.partner_z, "b": p.far_pair, "c": p.far_pair}.get(name, p.z)
        y = 1 - p.y if name == "y" else p.y
        x = 1 - p.x if name == "x" else p.x
        theirs = self.full.at[self.block(unit, before, z, y, x)]
        return self.copy(unit, stage, theirs, theirs, name)


class Scatter(Mover):
    line = "cba"

    def __init__(self, place, units, full, landings, result, send_sem, recv_sem):
        super().__init__(place, units, full, send_sem, recv_sem)
        self.landings, self.result = landings, result

    def sender(self, name):
        return {"b": self.inner_z, "c": self.outer_z}.get(name)

    def receiver(self, name):
        return self.inner_z if name in "bc" else None

    def landing(self, unit, stage):
        _, width, route = self.units[unit]
        got = self.landings[int(route[0] == "z")][stage]
        lead = (slice(None),) * (len(got.shape) - 1)
        return got.at[lead + (pl.ds(LANDING[unit], width),)]

    def leaving(self, unit, stage):
        p = self.place
        name, _, after = self.stages(unit)[stage]
        z = {"a": p.partner_z, "b": p.far_pair, "c": p.far_pair}.get(name, p.z)
        y = 1 - p.y if name == "y" else p.y
        x = 1 - p.x if name == "x" else p.x
        away = self.full.at[self.block(unit, after, z, y, x)]
        return self.copy(unit, stage, away, self.landing(unit, stage), name)

    arriving = leaving

    def add(self, unit, stage):
        p = self.place
        steps = self.stages(unit)
        name, _, after = steps[stage]

        def action():
            self.arriving(unit, stage).wait_recv()
            z = {"b": p.near_pair, "c": p.far_pair}.get(name, p.z)
            part = self.block(unit, after, z, p.y, p.x)
            total = self.full[part].astype(F32) + self.landing(unit, stage)[...].astype(F32)
            if stage + 1 == len(steps):
                start, width, _ = self.units[unit]
                self.result[:, pl.ds(start, width)] = total
            else:
                self.full[part] = total.astype(BF16)

        self.guarded(self.receiver(name), action)


def rows_dot(left, right):
    return jnp.dot(left, right, preferred_element_type=F32)


def dot_rt(left, right):
    return lax.dot_general(left, right, (((1,), (1,)), ((), ())), preferred_element_type=F32)


def dot_lt(left, right):
    return lax.dot_general(left, right, (((0,), (0,)), ((), ())), preferred_element_type=F32)


def normalized(values):
    center = values - jnp.mean(values, -1, keepdims=True)
    spread = jnp.mean(center * center, -1, keepdims=True)
    scale = lax.rsqrt(spread + NORM_EPSILON)
    return center * scale, scale


def total_rows(values):
    return jnp.sum(values, 0, keepdims=True)


GATHER_UNITS = (
    (0, 128, "zxy"),
    (128, 128, "zxy"),
    (256, 128, "zyx"),
    (384, 128, "zxy"),
    (512, 128, "zyx"),
    (640, 128, "zxy"),
    (768, 128, "zxy"),
    (896, 128, "zyx"),
    (1024, 256, "zyx"),
    (1280, 128, "yxz"),
    (1408, 384, "zyx"),
    (1792, 256, "zxy"),
    (2048, 256, "zyx"),
    (2304, 256, "zxy"),
    (2560, 256, "zyx"),
    (2816, 128, "zyx"),
    (2944, 128, "zyx"),
    (3072, 128, "zxy"),
    (3200, 256, "yxz"),
    (3456, 128, "zyx"),
    (3584, 128, "xyz"),
    (3712, 128, "zyx"),
    (3840, 128, "yxz"),
    (3968, 256, "xyz"),
    (4224, 256, "yxz"),
    (4480, 128, "xyz"),
)
SCATTER_UNITS = (
    (3072, 256, "zxy"),
    (3328, 128, "zxy"),
    (3456, 128, "yxz"),
    (3584, 256, "yxz"),
    (3840, 128, "yxz"),
    (3968, 128, "zxy"),
    (4096, 128, "yxz"),
    (4224, 128, "zxy"),
    (4352, 256, "yxz"),
    (1536, 256, "xyz"),
    (1792, 256, "yxz"),
    (2048, 256, "zxy"),
    (2304, 256, "xyz"),
    (2560, 256, "zyx"),
    (2816, 256, "xyz"),
    (1152, 384, "yxz"),
    (0, 128, "xyz"),
    (128, 256, "yxz"),
    (384, 128, "yxz"),
    (512, 128, "xyz"),
    (640, 128, "yxz"),
    (768, 128, "xyz"),
    (896, 128, "zyx"),
    (1024, 128, "xyz"),
)
LANDING = (
    0, 256, 0, 128, 384, 384, 512, 512, 640, 896, 1152, 640,
    1408, 896, 1664, 1920, 2304, 2432, 2688, 2816, 2944, 3072, 1152, 3200,
)
LATE_COLS, EARLY_COLS = 3328, 1280
PLAN = (
    ("g", 0, 0), ("g", 1, 0), ("g", 2, 0), ("g", 3, 0), ("g", 4, 0), ("g", 5, 0), ("g", 6, 0), ("g", 7, 0),
    ("g", 8, 0), ("g", 10, 0), ("g", 11, 0), ("g", 12, 0), ("g", 13, 0), ("g", 14, 0), ("g", 9, 0),
    ("g", 18, 0), ("g", 15, 0), ("g", 20, 0), ("g", 16, 0), ("g", 22, 0), ("g", 23, 0), ("g", 17, 0),
    ("g", 24, 0), ("g", 19, 0), ("g", 25, 0), ("ln1", 0), ("g", 21, 0), ("ln1", 1), ("g", 0, 1), ("caps", 0),
    ("g", 1, 1), ("g", 2, 1), ("tr", 0), ("g", 3, 1), ("g", 4, 1), ("g", 5, 1), ("tr", 1), ("g", 6, 1),
    ("g", 7, 1), ("g", 9, 1), ("g", 18, 1), ("g", 20, 1), ("g", 8, 1), ("g", 22, 1), ("g", 23, 1), ("g", 25, 1),
    ("g", 24, 1), ("g", 10, 1), ("g", 0, 2), ("g", 11, 1), ("g", 1, 2), ("g", 12, 1), ("g", 2, 2), ("g", 13, 1),
    ("g", 3, 2), ("g", 14, 1), ("g", 15, 1), ("g", 4, 2), ("g", 16, 1), ("g", 17, 1), ("g", 5, 2), ("g", 19, 1),
    ("g", 21, 1), ("g", 6, 2), ("g", 0, 3), ("g", 7, 2), ("g", 1, 3), ("g", 9, 2), ("g", 2, 3), ("g", 8, 2),
    ("g", 3, 3), ("g", 4, 3), ("g", 5, 3), ("g", 10, 2), ("g", 6, 3), ("g", 7, 3), ("g", 11, 2), ("g", 0, 4),
    ("g", 9, 3), ("g", 12, 2), ("g", 1, 4), ("g", 2, 4), ("g", 8, 3), ("g", 13, 2), ("g", 3, 4), ("g", 4, 4),
    ("g", 14, 2), ("g", 5, 4), ("g", 10, 3), ("g", 15, 2), ("g", 7, 4), ("g", 16, 2), ("g", 6, 4), ("g", 11, 3),
    ("g", 17, 2), ("g", 19, 2), ("g", 12, 3), ("g", 21, 2), ("g", 13, 3), ("g", 18, 2), ("g", 14, 3),
    ("g", 9, 4), ("g", 15, 3), ("g", 16, 3), ("g", 17, 3), ("g", 19, 3), ("g", 8, 4), ("g", 21, 3),
    ("g", 20, 2), ("g", 18, 3), ("g", 22, 2), ("g", 11, 4), ("g", 23, 2), ("g", 13, 4), ("g", 20, 3),
    ("g", 24, 2), ("g", 17, 4), ("g", 22, 3), ("g", 10, 4), ("g", 25, 2), ("g", 23, 3), ("g", 18, 4), ("gf", 0),
    ("gf", 1), ("gf", 2), ("gf", 3), ("gf", 4), ("gf", 5), ("gf", 6), ("gf", 7), ("gf", 8), ("qkv", 0),
    ("qkv", 1), ("g", 24, 3), ("att", 0, 0), ("g", 12, 4), ("g", 20, 4), ("g", 25, 3), ("att", 0, 1),
    ("att", 0, 2), ("g", 14, 4), ("g", 22, 4), ("att", 1, 0), ("g", 15, 4), ("att", 1, 1), ("g", 16, 4),
    ("att", 1, 2), ("gf", 9), ("gf", 10), ("op0", 0), ("g", 19, 4), ("op0", 1), ("g", 21, 4), ("g", 23, 4),
    ("g", 24, 4), ("ln2", 0), ("ln2", 1), ("tr", 2), ("up", 0), ("gf", 11), ("up", 1), ("g", 25, 4), ("gf", 12),
    ("up", 2), ("gf", 14), ("up", 4), ("gd", 0), ("s", 0, 0), ("gf", 13), ("up", 3), ("gd", 1), ("s", 1, 0),
    ("s", 2, 0), ("gd", 2), ("s", 3, 0), ("gd", 3), ("s", 4, 0), ("s", 5, 0), ("gf", 15), ("gf", 16), ("up", 5),
    ("gd", 4), ("gd", 5), ("s", 6, 0), ("gf", 17), ("gf", 18), ("pre", 0), ("s", 7, 0), ("s", 9, 0), ("gf", 19),
    ("pre", 1), ("s", 2, 1), ("s", 8, 0), ("gf", 22), ("gf", 23), ("pre", 3), ("s", 12, 0), ("gf", 20),
    ("gf", 21), ("pre", 2), ("s", 11, 0), ("gf", 24), ("pre", 4), ("s", 0, 1), ("gf", 25), ("pre", 5),
    ("s", 3, 1), ("s", 10, 0), ("s", 13, 0), ("s", 1, 1), ("s", 14, 0), ("da2", 0), ("da2", 1), ("s", 9, 1),
    ("s", 4, 1), ("s", 5, 1), ("s", 2, 2), ("s", 6, 1), ("s", 7, 1), ("s", 0, 2), ("ln2b", 0), ("s", 12, 1),
    ("ln2b", 1), ("s", 1, 2), ("s", 3, 2), ("s", 8, 1), ("s", 11, 1), ("gout", 0), ("s", 5, 2), ("s", 15, 0),
    ("do", 0), ("do", 1), ("attb", 0, 0), ("s", 7, 2), ("s", 10, 1), ("s", 13, 1), ("s", 2, 3), ("s", 14, 1),
    ("attb", 0, 1), ("s", 4, 2), ("s", 6, 2), ("s", 0, 3), ("s", 9, 2), ("attb", 0, 2), ("s", 1, 3),
    ("s", 11, 2), ("s", 3, 3), ("s", 8, 2), ("s", 12, 2), ("attb", 1, 0), ("s", 5, 3), ("s", 10, 2),
    ("s", 7, 3), ("attb", 1, 1), ("s", 0, 4), ("s", 1, 4), ("s", 4, 3), ("s", 6, 3), ("s", 13, 2), ("s", 2, 4),
    ("s", 9, 3), ("attb", 1, 2), ("s", 3, 4), ("s", 5, 4), ("s", 7, 4), ("s", 15, 1), ("s", 11, 3), ("gp", 0),
    ("s", 4, 4), ("s", 0, 5), ("s", 6, 4), ("s", 8, 3), ("s", 1, 5), ("s", 14, 2), ("s", 12, 3), ("s", 16, 0),
    ("s", 17, 0), ("s", 9, 4), ("gp", 1), ("s", 5, 5), ("s", 7, 5), ("s", 10, 3), ("s", 18, 0), ("s", 19, 0),
    ("s", 20, 0), ("gp", 2), ("s", 21, 0), ("s", 22, 0), ("da1", 0), ("s", 13, 3), ("s", 23, 0), ("s", 2, 5),
    ("da1", 1), ("s", 8, 4), ("s", 3, 5), ("op2", 0), ("s", 4, 5), ("s", 6, 5), ("s", 12, 4), ("s", 15, 2),
    ("s", 11, 4), ("op2", 1), ("s", 9, 5), ("s", 10, 4), ("s", 14, 3), ("s", 17, 1), ("s", 16, 1), ("s", 22, 1),
    ("ln1b", 0), ("s", 8, 5), ("s", 12, 5), ("s", 18, 1), ("s", 19, 1), ("ln1b", 1), ("s", 14, 4), ("s", 15, 3),
    ("s", 10, 5), ("op2s", 0), ("s", 20, 1), ("s", 21, 1), ("vec", 0), ("s", 13, 4), ("s", 11, 5), ("s", 22, 2),
    ("s", 23, 1), ("s", 16, 2), ("s", 14, 5), ("s", 19, 2), ("s", 15, 4), ("s", 17, 2), ("s", 21, 2),
    ("s", 18, 2), ("s", 22, 3), ("vec", 1), ("s", 16, 3), ("s", 20, 2), ("s", 13, 5), ("s", 23, 2),
    ("s", 19, 3), ("fout", 0), ("fout", 1), ("s", 15, 5), ("s", 17, 3), ("s", 22, 4), ("s", 21, 3),
    ("s", 18, 3), ("s", 16, 4), ("s", 20, 3), ("s", 19, 4), ("s", 23, 3), ("vec", 2), ("s", 22, 5),
    ("s", 17, 4), ("s", 16, 5), ("s", 21, 4), ("s", 19, 5), ("s", 18, 4), ("s", 20, 4), ("s", 23, 4),
    ("s", 17, 5), ("s", 21, 5), ("s", 18, 5), ("vec", 3), ("s", 20, 5), ("s", 23, 5),
)

HEAD_COLS, UNIT_COLS = 384, 1536
Q0, K0, V0, O0, U0, W0 = 0, 384, 768, 1152, 1536, 3072


def block_kernel(
    inner, items, length, tokens_hbm, cotangent_hbm, task_mask, group_ids, matrices_hbm, norm, column, *rest
):
    (out_hbm, input_grad_hbm, matrix_grad, vectors) = rest[:4]
    (full, grads) = rest[4:6]
    landings = (rest[6:11], rest[11:16])
    (act_one, act_one_t, act_two, act_two_t, cot_t, proj, grad_proj, heads, grad_heads) = rest[16:25]
    (caps, probs, residual, slope, hidden, grad_pre, grad_res, grad_low, ex_send, ex_recv) = rest[25:35]
    (vec_got, vec_z, g_send, g_recv, s_send, s_recv, es, er, vs, vr) = rest[35:45]
    (tokens, cotangent, matrices, out, input_grad, in_sem, out_sem) = rest[45:]
    loads = [
        pltpu.make_async_copy(source, target, in_sem.at[spot])
        for spot, (source, target) in enumerate(
            ((matrices_hbm, matrices), (tokens_hbm, tokens), (cotangent_hbm, cotangent))
        )
    ]
    for load in loads:
        load.start()
    place = Place(inner)
    gather = Gather(place, GATHER_UNITS, full, g_send, g_recv)
    scatter = Scatter(place, SCATTER_UNITS, grads, landings, matrix_grad, s_send, s_recv)

    def weight(start, width):
        return full[:, :, :, :, pl.ds(start, width)].reshape(D, width)

    def put_grad(start, width, value):
        grads[:, :, :, :, pl.ds(start, width)] = value.astype(BF16).reshape(grads.shape[:4] + (width,))

    def rows_of(item):
        return pl.ds(item * length, length)

    def store(which, item):
        part = rows_of(item)
        source, target = ((out, out_hbm), (input_grad, input_grad_hbm))[which]
        return pltpu.make_async_copy(source.at[part], target.at[part], out_sem.at[which, item])

    def add_vector(row, first, value):
        cols = pl.ds(first, value.shape[1])
        vectors[row : row + 1, cols] = vectors[row : row + 1, cols] + value

    def exchange(turn, item):
        part = rows_of(item)
        return remote(
            ex_send.at[turn % 2, part],
            ex_recv.at[turn % 2, part],
            es.at[turn, item],
            er.at[turn, item],
            place.sibling(),
        )

    def fill_part(turn, item, value):
        if turn >= 2:
            exchange(turn - 2, item).wait_send()
        ex_send[turn % 2, rows_of(item)] = value.astype(BF16)

    def both(turn, item):
        exchange(turn, item).wait_recv()
        part = rows_of(item)
        return ex_send[turn % 2, part].astype(F32) + ex_recv[turn % 2, part].astype(F32)

    def norm_one(item):
        part = rows_of(item)
        unit_x, _ = normalized(tokens[part].astype(F32))
        act_one[part] = (unit_x * norm[0:1] + norm[1:2]).astype(BF16)
        add_vector(5, 0, total_rows(cotangent[part].astype(F32)))

    def masks(_):
        key_index = lax.broadcasted_iota(jnp.int32, (length, length), 0)
        query_index = lax.broadcasted_iota(jnp.int32, (length, length), 1)
        same = key_index == query_index
        slots = task_mask.shape[1]
        slot_same = lax.broadcasted_iota(jnp.int32, (slots, slots), 0) == lax.broadcasted_iota(
            jnp.int32, (slots, slots), 1
        )
        for item in range(items):
            query_ids = group_ids[item : item + 1, :]
            key_ids = jnp.sum(jnp.where(same, query_ids, 0), axis=1, keepdims=True)
            filled = jnp.sum(jnp.where(slot_same, task_mask[item : item + 1, :], 0), axis=1, keepdims=True)
            live = jnp.concatenate([filled, jnp.ones((length - slots, 1), jnp.int32)], axis=0)
            odd_key = jnp.where((key_ids == 0) | (key_ids % 2 == 1), 1, 0)
            earlier = (odd_key == 1) & (key_ids <= query_ids)
            visible = (earlier | (key_ids == query_ids)) & (live == 1)
            caps[item] = jnp.where(visible | same, 3.0e38, NEGATIVE)

    def turned(which):
        source, target = ((act_one, act_one_t), (cotangent, cot_t), (act_two, act_two_t))[which]
        target[...] = source[...].T

    def project(item):
        part = rows_of(item)
        for start, scale, bias in ((Q0, HD**-0.5, 0), (K0, 1.0, None), (V0, 1.0, HEAD_COLS)):
            value = rows_dot(act_one[part], weight(start, HEAD_COLS))
            if bias is not None:
                value = value + column[pl.ds(bias, HEAD_COLS)].reshape(1, HEAD_COLS)
            value = value.astype(BF16)
            if scale != 1.0:
                value = value * jnp.asarray(scale, BF16)
            proj[part, start : start + HEAD_COLS] = value

    lane = lax.broadcasted_iota(jnp.int32, (length, 128), 1)
    first_half = lane < HD

    def lanes(start, pair):
        return pl.ds(start + pair * 128, 128)

    def attend(item, pair):
        part = rows_of(item)
        query, key, value = (proj[part, lanes(start, pair)] for start in (Q0, K0, V0))
        sides = []
        for side in range(2):
            own = first_half if side == 0 else ~first_half
            scores = dot_rt(jnp.where(own, key, jnp.zeros_like(key)), query)
            scores = jnp.minimum(scores, caps[item])
            weights = jnp.exp(scores - jnp.max(scores, 0, keepdims=True))
            prob = weights * (1.0 / jnp.sum(weights, 0, keepdims=True))
            probs[item, pair * 2 + side] = prob
            sides.append(dot_lt(prob.astype(BF16), value))
        heads[part, lanes(0, pair)] = jnp.where(first_half, sides[0], sides[1]).astype(BF16)

    def heads_out(item):
        fill_part(0, item, dot_rt(heads[rows_of(item)], weight(O0, HEAD_COLS)))
        exchange(0, item).start()

    def norm_two(item):
        part = rows_of(item)
        value = tokens[part].astype(F32) + both(0, item) + norm[4:5]
        residual[part] = value
        unit_x, _ = normalized(value)
        act_two[part] = (unit_x * norm[2:3] + norm[3:4]).astype(BF16)

    def up(index):
        start = index * COL_TILE
        cols = pl.ds(start, COL_TILE)
        unit = rows_dot(act_two[...], weight(U0 + start, COL_TILE))
        unit = unit + column[pl.ds(2 * HEAD_COLS + start, COL_TILE)].reshape(1, COL_TILE)
        square = unit * unit
        bent = jnp.tanh(unit * (GELU_SCALE + (GELU_SCALE * GELU_CUBIC) * square))
        half = 0.5 * (1.0 + bent)
        hidden[:, cols] = (unit * half).astype(BF16)
        slope[:, cols] = half + 0.5 * unit * (1.0 - bent * bent) * (
            GELU_SCALE + (3.0 * GELU_SCALE * GELU_CUBIC) * square
        )

    def down_grad(index):
        start = index * COL_TILE
        put_grad(W0 + start, COL_TILE, rows_dot(cot_t[...], hidden[:, pl.ds(start, COL_TILE)]))

    def pre_grad(index):
        start = index * COL_TILE
        cols = pl.ds(start, COL_TILE)
        value = rows_dot(cotangent[...], weight(W0 + start, COL_TILE))
        low = (value * slope[:, cols]).astype(BF16)
        grad_pre[:, cols] = low
        row, first = divmod(2 * HEAD_COLS + start, D)
        add_vector(6 + row, first, total_rows(low.astype(F32)))
        put_grad(U0 + start, COL_TILE, rows_dot(act_two_t[...], low))

    def units_back(item):
        fill_part(1, item, dot_rt(grad_pre[rows_of(item)], weight(U0, UNIT_COLS)))
        exchange(1, item).start()

    def norm_back(incoming, values, gain):
        unit_x, scale = normalized(values)
        pulled = incoming * gain
        inner_mean = jnp.mean(pulled, -1, keepdims=True)
        cross_mean = jnp.mean(pulled * unit_x, -1, keepdims=True)
        return scale * (pulled - inner_mean - unit_x * cross_mean), total_rows(incoming * unit_x), total_rows(incoming)

    def norm_two_back(item):
        part = rows_of(item)
        value, gain_sum, shift_sum = norm_back(both(1, item), residual[part], norm[2:3])
        value = cotangent[part].astype(F32) + value
        grad_res[part] = value
        grad_low[part] = value.astype(BF16)
        add_vector(2, 0, gain_sum)
        add_vector(3, 0, shift_sum)
        add_vector(4, 0, total_rows(value))

    def out_grad(_):
        put_grad(O0, HEAD_COLS, dot_lt(grad_low[...], heads[...]))

    def heads_back(item):
        part = rows_of(item)
        grad_heads[part] = rows_dot(grad_low[part], weight(O0, HEAD_COLS)).astype(BF16)

    def attend_back(item, pair):
        part = rows_of(item)
        query, key, value = (proj[part, lanes(start, pair)] for start in (Q0, K0, V0))
        grad = grad_heads[part, lanes(0, pair)]
        sides = []
        for side in range(2):
            own = first_half if side == 0 else ~first_half
            prob = probs[item, pair * 2 + side]
            grad_prob = dot_rt(jnp.where(own, value, jnp.zeros_like(value)), grad)
            inner_sum = jnp.sum(prob * grad_prob, 0, keepdims=True)
            low = (prob * (grad_prob - inner_sum)).astype(BF16)
            sides.append(
                (dot_lt(low, key) * (HD**-0.5), rows_dot(low, query), rows_dot(prob.astype(BF16), grad))
            )
        for start, left, right in zip((Q0, K0, V0), sides[0], sides[1]):
            low = jnp.where(first_half, left, right).astype(BF16)
            grad_proj[part, lanes(start, pair)] = low
            if start != K0:
                add_vector(6, (0 if start == Q0 else HEAD_COLS) + pair * 128, total_rows(low.astype(F32)))

    def proj_grad(index):
        cols = pl.ds(index * HEAD_COLS, HEAD_COLS)
        put_grad(index * HEAD_COLS, HEAD_COLS, rows_dot(act_one_t[...], grad_proj[:, cols]))

    def heads_in(item):
        fill_part(2, item, dot_rt(grad_proj[rows_of(item)], weight(Q0, 3 * HEAD_COLS)))
        exchange(2, item).start()

    def units_out(item):
        fill_part(3, item, dot_rt(hidden[rows_of(item)], weight(W0, UNIT_COLS)))

    def send_units(_):
        for item in range(items):
            exchange(3, item).start()

    def norm_one_back(item):
        part = rows_of(item)
        value, gain_sum, shift_sum = norm_back(both(2, item), tokens[part].astype(F32), norm[0:1])
        input_grad[part] = grad_res[part] + value
        store(1, item).start()
        add_vector(0, 0, gain_sum)
        add_vector(1, 0, shift_sum)

    def finish_out(item):
        part = rows_of(item)
        out[part] = (residual[part] + both(3, item) + norm[5:6]).astype(BF16)
        store(0, item).start()

    def vec_copy(stage, owner_z=None, step=0):
        if stage < 2:
            peer = (place.across_x(), place.across_y())[stage]
            return remote(vectors, vec_got.at[stage], vs.at[stage], vr.at[stage], peer)
        block = vec_z.at[owner_z]
        return remote(block, block, vs.at[1 + step], vr.at[1 + step], place.along_z(step))

    def small_sums(stage):
        if stage in (1, 2):
            vec_copy(stage - 1).wait()
            vectors[...] = vectors[...] + vec_got[stage - 1]
        if stage < 2:
            vec_copy(stage).start()
        elif stage == 2:
            vec_z[place.z] = vectors[...]
            for step in range(1, NZ):
                vec_copy(2, place.z, step).start()
        else:
            for step in range(1, NZ):
                vec_copy(2, (place.z - step) % NZ, step).wait_recv()
                vec_copy(2, place.z, step).wait_send()
            vectors[...] = (vec_z[0] + vec_z[1]) + (vec_z[2] + vec_z[3])

    pieces = {
        "ln1": norm_one,
        "caps": masks,
        "tr": turned,
        "qkv": project,
        "att": attend,
        "op0": heads_out,
        "ln2": norm_two,
        "up": up,
        "gd": down_grad,
        "pre": pre_grad,
        "da2": units_back,
        "ln2b": norm_two_back,
        "gout": out_grad,
        "do": heads_back,
        "attb": attend_back,
        "gp": proj_grad,
        "da1": heads_in,
        "op2": units_out,
        "op2s": send_units,
        "ln1b": norm_one_back,
        "fout": finish_out,
        "vec": small_sums,
    }

    vectors[...] = jnp.zeros_like(vectors)
    place.greet()
    for load in loads:
        load.wait()
    for kind, *what in PLAN:
        if kind == "g":
            unit, stage = what
            if stage == 0:
                cols = pl.ds(*GATHER_UNITS[unit][:2])
                full[place.z, place.y, place.x, :, cols] = matrices[:, cols].astype(BF16)
            else:
                gather.settle(unit, stage - 1)
            gather.begin(unit, stage)
        elif kind == "gf":
            gather.settle(what[0], 4)
        elif kind == "s":
            unit, stage = what
            if stage > 0:
                scatter.add(unit, stage - 1)
            if stage < 5:
                scatter.begin(unit, stage)
        else:
            pieces[kind](*what)
    for which in range(2):
        for item in range(items):
            store(which, item).wait()
    gather.drain()
    scatter.drain()
    for turn in (2, 3):
        for item in range(items):
            exchange(turn, item).wait_send()


def run_block(inner, tokens, cotangent, task_mask, group_ids, slab, norm_bias, column_bias):
    rows = tokens.shape[0]
    items, length = group_ids.shape
    slab_rows, cols = slab.shape
    heads = HEAD_COLS // HD
    gather_units, scatter_units = len(GATHER_UNITS), len(SCATTER_UNITS)
    dma = pltpu.SemaphoreType.DMA
    vmem = pltpu.VMEM
    in_vmem = pl.BlockSpec(memory_space=pltpu.VMEM)
    anywhere = pl.BlockSpec(memory_space=pl.ANY)
    return pl.pallas_call(
        functools.partial(block_kernel, inner, items, length),
        out_shape=(
            jax.ShapeDtypeStruct((rows, D), BF16),
            jax.ShapeDtypeStruct((rows, D), F32),
            jax.ShapeDtypeStruct((slab_rows, cols), F32),
            jax.ShapeDtypeStruct((16, D), F32),
        ),
        in_specs=[anywhere, anywhere, in_vmem, in_vmem, anywhere, in_vmem, in_vmem],
        out_specs=(anywhere, anywhere, in_vmem, in_vmem),
        scratch_shapes=[
            vmem((NZ, NY, NX, slab_rows, cols), BF16),
            vmem((NZ, NY, NX, slab_rows, cols), BF16),
            vmem((NZ, 2, slab_rows, LATE_COLS), BF16),
            vmem((NZ, slab_rows, LATE_COLS), BF16),
            vmem((2, slab_rows, LATE_COLS), BF16),
            vmem((2, slab_rows, LATE_COLS), BF16),
            vmem((slab_rows, LATE_COLS), BF16),
            vmem((2, NY, NX, slab_rows, EARLY_COLS), BF16),
            vmem((2, NY, NX, slab_rows, EARLY_COLS), BF16),
            vmem((NY, NX, slab_rows, EARLY_COLS), BF16),
            vmem((2, slab_rows, EARLY_COLS), BF16),
            vmem((slab_rows, EARLY_COLS), BF16),
            vmem((rows, D), BF16),
            vmem((D, rows), BF16),
            vmem((rows, D), BF16),
            vmem((D, rows), BF16),
            vmem((D, rows), BF16),
            vmem((rows, 3 * HEAD_COLS), BF16),
            vmem((rows, 3 * HEAD_COLS), BF16),
            vmem((rows, HEAD_COLS), BF16),
            vmem((rows, HEAD_COLS), BF16),
            vmem((items, length, length), F32),
            vmem((items, heads, length, length), F32),
            vmem((rows, D), F32),
            vmem((rows, UNIT_COLS), F32),
            vmem((rows, UNIT_COLS), BF16),
            vmem((rows, UNIT_COLS), BF16),
            vmem((rows, D), F32),
            vmem((rows, D), BF16),
            vmem((2, rows, D), BF16),
            vmem((2, rows, D), BF16),
            vmem((2, 16, D), F32),
            vmem((NZ, 16, D), F32),
            dma((gather_units, 5)),
            dma((gather_units, 5)),
            dma((scatter_units, 5)),
            dma((scatter_units, 5)),
            dma((4, items)),
            dma((4, items)),
            dma((2 + NZ - 1,)),
            dma((2 + NZ - 1,)),
            vmem((rows, D), BF16),
            vmem((rows, D), BF16),
            vmem((slab_rows, cols), F32),
            vmem((rows, D), BF16),
            vmem((rows, D), F32),
            dma((3,)),
            dma((2, items)),
        ],
        compiler_params=pltpu.CompilerParams(
            collective_id=0, has_side_effects=True, vmem_limit_bytes=60 << 20
        ),
    )(tokens, cotangent, task_mask, group_ids, slab, norm_bias, column_bias)


def adam_update(weight_now, gradient, first_now, second_now, step_rate, weight_decay):
    first_new = BETA_FIRST * first_now + (1.0 - BETA_FIRST) * gradient
    second_new = BETA_SECOND * second_now + (1.0 - BETA_SECOND) * gradient * gradient
    first_fixed = first_new / (1.0 - BETA_FIRST**STEP)
    second_fixed = second_new / (1.0 - BETA_SECOND**STEP)
    weight_new = weight_now - step_rate * (
        first_fixed / (jnp.sqrt(second_fixed) + EPS_ADAM) + weight_decay * weight_now
    )
    return (weight_new, first_new, second_new)


FINISH_PARTS = 2
STATES = 4


def finish_kernel(*refs):
    out_in, dx_in, grad_in, vec_in = refs[:4]
    matrix_in, norm_in, column_in = refs[4:8], refs[8:12], refs[12:16]
    out_res, dx_res = refs[16:18]
    matrix_res, norm_res, column_res = refs[18:23], refs[23:28], refs[28:33]
    grad, mats, fresh, vectors, norms, norm_new = refs[33:39]
    cols, col_new = refs[39:43], refs[43:48]
    dx_held, out_held, pass_sem, in_sem, part_sem, out_sem, end_sem = refs[48:]
    width = grad.shape[1] // FINISH_PARTS
    copy = pltpu.make_async_copy

    def load(part):
        where = pl.ds(part * width, width)
        moves = [copy(grad_in.at[:, where], grad.at[:, where], part_sem.at[part, 0])]
        for spot, source in enumerate(matrix_in):
            moves.append(copy(source.at[:, where], mats.at[spot, :, where], part_sem.at[part, 1 + spot]))
        return moves

    def save(part):
        where = pl.ds(part * width, width)
        moves = [copy(grad.at[:, where], matrix_res[0].at[:, where], out_sem.at[part, 0])]
        for spot in range(STATES):
            moves.append(copy(fresh.at[spot, :, where], matrix_res[1 + spot].at[:, where], out_sem.at[part, 1 + spot]))
        return moves

    loads = [load(part) for part in range(FINISH_PARTS)]
    saves = [save(part) for part in range(FINISH_PARTS)]
    small = [copy(vec_in, vectors, in_sem.at[0])]
    for spot in range(STATES):
        small.append(copy(norm_in[spot], norms.at[spot], in_sem.at[1 + spot]))
        small.append(copy(column_in[spot], cols[spot], in_sem.at[1 + STATES + spot]))
    taken = [copy(dx_in, dx_held, pass_sem.at[0]), copy(out_in, out_held, pass_sem.at[1])]
    passed = [copy(dx_held, dx_res, end_sem.at[0]), copy(out_held, out_res, end_sem.at[1])]
    for move in loads[0] + taken + small:
        move.start()
    for moves in loads[1:]:
        for move in moves:
            move.start()

    def update(gradient, old, rate, decay):
        now, first, second, average = old
        new, first, second = adam_update(now, gradient, first, second, rate, decay)
        return new, first, second, AVERAGE_KEEP * average + (1.0 - AVERAGE_KEEP) * new

    for part in range(FINISH_PARTS):
        for move in loads[part]:
            move.wait()
        where = pl.ds(part * width, width)
        old = [mats[spot, :, where] for spot in range(STATES)]
        for spot, value in enumerate(update(grad[:, where], old, RATE_MATRIX, DECAY_MATRIX)):
            fresh[spot, :, where] = value
        for move in saves[part]:
            move.start()
        if part == 0:
            for move, onward in zip(taken, passed):
                move.wait()
                onward.start()
    for move in small:
        move.wait()
    gradient = vectors[0:6, :]
    norm_new[0] = gradient
    for spot, value in enumerate(update(gradient, [norms[spot] for spot in range(STATES)], RATE_VECTOR, 0.0)):
        norm_new[1 + spot] = value
    for row in range(3):
        where = pl.ds(row * D, D)
        gradient = vectors[6 + row : 7 + row, :]
        col_new[0][where] = gradient.reshape(D)
        old = [ref[where].reshape(1, D) for ref in cols]
        for spot, value in enumerate(update(gradient, old, RATE_VECTOR, 0.0)):
            col_new[1 + spot][where] = value.reshape(D)
    ends = []
    for spot in range(1 + STATES):
        ends.append(copy(norm_new.at[spot], norm_res[spot], end_sem.at[2 + spot]))
        ends.append(copy(col_new[spot], column_res[spot], end_sem.at[3 + STATES + spot]))
    for move in ends:
        move.start()
    for move in sum(saves, []) + passed + ends:
        move.wait()


def finish(output, input_grad, matrix_grad, vectors, matrix_set, norm_set, column_set):
    slab_rows, cols = matrix_grad.shape
    shape, vmem, dma = jax.ShapeDtypeStruct, pltpu.VMEM, pltpu.SemaphoreType.DMA
    norm_bias, column_bias = norm_set[0], column_set[0]
    anywhere = pl.BlockSpec(memory_space=pl.ANY)
    return pl.pallas_call(
        finish_kernel,
        out_shape=[shape(output.shape, output.dtype), shape(input_grad.shape, F32)]
        + [shape(matrix_grad.shape, F32)] * 5
        + [shape(norm_bias.shape, F32)] * 5
        + [shape(column_bias.shape, F32)] * 5,
        in_specs=[anywhere] * 16,
        out_specs=[anywhere] * 17,
        scratch_shapes=[
            vmem((slab_rows, cols), F32),
            vmem((STATES, slab_rows, cols), F32),
            vmem((STATES, slab_rows, cols), F32),
            vmem(vectors.shape, F32),
            vmem((STATES,) + norm_bias.shape, F32),
            vmem((1 + STATES,) + norm_bias.shape, F32),
        ]
        + [vmem(column_bias.shape, F32)] * (2 * STATES + 1)
        + [
            vmem(input_grad.shape, F32),
            vmem(output.shape, output.dtype),
            dma((2,)),
            dma((1 + 2 * STATES,)),
            dma((FINISH_PARTS, 1 + STATES)),
            dma((FINISH_PARTS, 1 + STATES)),
            dma((2 + 2 * (1 + STATES),)),
        ],
        compiler_params=pltpu.CompilerParams(vmem_limit_bytes=60 << 20),
    )(output, input_grad, matrix_grad, vectors, *matrix_set, *norm_set, *column_set)


def local(
    tokens,
    cotangent,
    task_mask,
    group_ids,
    matrices,
    matrix_first,
    matrix_second,
    matrix_average,
    norm_bias,
    norm_first,
    norm_second,
    norm_average,
    column_bias,
    column_first,
    column_second,
    column_average,
):
    inner = lax.axis_size("dp") // OUTER
    groups = [[outer * inner + i for i in range(inner)] for outer in range(OUTER)]
    slab = matrices
    if inner > 1:
        slab = lax.all_gather(
            matrices.astype(BF16), "dp", axis=0, tiled=True, axis_index_groups=groups
        ).astype(F32)
    output, input_grad, matrix_grad, vectors = run_block(
        inner, tokens, cotangent, task_mask, group_ids, slab, norm_bias, column_bias
    )
    if inner > 1:
        matrix_grad = lax.psum_scatter(
            matrix_grad, "dp", scatter_dimension=0, tiled=True, axis_index_groups=groups
        )
        vectors = jnp.sum(lax.all_gather(vectors, "dp", axis=0, axis_index_groups=groups), 0)
    return tuple(
        finish(
            output,
            input_grad,
            matrix_grad,
            vectors,
            (matrices, matrix_first, matrix_second, matrix_average),
            (norm_bias, norm_first, norm_second, norm_average),
            (column_bias, column_first, column_second, column_average),
        )
    )


def solution(mesh):
    placed = (
        P("dp", None),
        P("dp", None),
        P("dp", None),
        P("dp", None),
        P("dp", "mp"),
        P("dp", "mp"),
        P("dp", "mp"),
        P("dp", "mp"),
        P(),
        P(),
        P(),
        P(),
        P("mp"),
        P("mp"),
        P("mp"),
        P("mp"),
    )
    return jax.shard_map(
        local,
        mesh=mesh,
        in_specs=placed,
        out_specs=(
            P("dp", None),
            P("dp", None),
            P("dp", "mp"),
            P("dp", "mp"),
            P("dp", "mp"),
            P("dp", "mp"),
            P("dp", "mp"),
            P(),
            P(),
            P(),
            P(),
            P(),
            P("mp"),
            P("mp"),
            P("mp"),
            P("mp"),
            P("mp"),
        ),
        check_vma=False,
    )
```
